32 devices in a mesh: dp: 8 (over z, x), tensor: 4 (over y, core).
Axes of the slice: x: 2, y: 2, z: 4, core: 2. Of those that a mesh axis runs over, the one named last changes fastest.
Arguments:
- hidden_in: bfloat16 [2, 8, 64, 1600], P(None, 'dp'), may hold values from -6 to 6
- out_grad: bfloat16 [2, 8, 64, 1600], P(None, 'dp'), may hold values from -6 to 6
- lengths: int32 [2, 8], P(None, 'dp'), may hold values from 16 to 64, as said below
- norm_gains: float32 [2, 4, 1600], replicated, may hold values from 0.5 to 1.5
- q_weight: bfloat16 [2, 1600, 1600], P(None, 'dp'), may hold values from -0.15625 to 0.15625
- kv_weight: bfloat16 [2, 1600, 2, 320], P(None, 'dp'), may hold values from -0.15625 to 0.15625
- o_weight: bfloat16 [2, 1600, 1600], P(None, None, 'dp'), may hold values from -0.15625 to 0.15625
- in_weight: bfloat16 [2, 1600, 2, 3200], P(None, 'dp', None, 'tensor'), may hold values from -0.15625 to 0.15625
- conv_weight: float32 [2, 4, 3200], P(None, None, 'tensor'), may hold values from -3 to 3
- conv_bias: float32 [2, 3200], P(None, 'tensor'), may hold values from -3 to 3
- step_bias: float32 [2, 3200], P(None, 'tensor'), may hold values from -6 to -2
- decay_log: float32 [2, 3200, 16], P(None, 'tensor'), may hold values from 0 to 2.77
- skip_gain: float32 [2, 3200], P(None, 'tensor'), may hold values from 0.5 to 1.5
- scan_weight: bfloat16 [2, 3200, 132], P(None, 'tensor'), may hold values from -0.109375 to 0.109375
- step_weight: bfloat16 [2, 100, 3200], P(None, None, 'tensor'), may hold values from -0.625 to 0.625
- ssm_weight: bfloat16 [2, 3200, 1600], P(None, 'tensor', 'dp'), may hold values from -0.109375 to 0.109375
- gate_weight: bfloat16 [2, 1600, 2, 5504], P(None, 'dp', None, 'tensor'), may hold values from -0.15625 to 0.15625
- down_weight: bfloat16 [2, 5504, 1600], P(None, 'tensor', 'dp'), may hold values from -0.078125 to 0.078125
Outputs:
- output: bfloat16 [2, 8, 64, 1600], P(None, 'dp')
- input_grad: float32 [2, 8, 64, 1600], P(None, 'dp')
- grad_norm_gains: float32 [2, 4, 1600], replicated
- grad_q_weight: float32 [2, 1600, 1600], P(None, 'dp')
- grad_kv_weight: float32 [2, 1600, 2, 320], P(None, 'dp')
- grad_o_weight: float32 [2, 1600, 1600], P(None, None, 'dp')
- grad_in_weight: float32 [2, 1600, 2, 3200], P(None, 'dp', None, 'tensor')
- grad_conv_weight: float32 [2, 4, 3200], P(None, None, 'tensor')
- grad_conv_bias: float32 [2, 3200], P(None, 'tensor')
- grad_step_bias: float32 [2, 3200], P(None, 'tensor')
- grad_decay_log: float32 [2, 3200, 16], P(None, 'tensor')
- grad_skip_gain: float32 [2, 3200], P(None, 'tensor')
- grad_scan_weight: float32 [2, 3200, 132], P(None, 'tensor')
- grad_step_weight: float32 [2, 100, 3200], P(None, None, 'tensor')
- grad_ssm_weight: float32 [2, 3200, 1600], P(None, 'tensor', 'dp')
- grad_gate_weight: float32 [2, 1600, 2, 5504], P(None, 'dp', None, 'tensor')
- grad_down_weight: float32 [2, 5504, 1600], P(None, 'tensor', 'dp')
The draws below stay inside these ranges and needn't reach their ends.
Inputs may be any that keep to these rules, and one draw needn't show every extreme that they name: `lengths`: positions from a sequence's length to 64 are padding; in every draw some sequence has 16 tokens and some has 64.
All inputs are finite; a program needn't handle non-finite values.
Results may differ from the reference program's by a relative error of at most 0.035.
Values may be sent and summed in bfloat16 or wider, within the bound.
No kernel may reach another device: no remote copies, remote signals or barrier semaphores. Data moves between devices by JAX's collectives and lax.ppermute only.
A program may use at most 448 MiB of HBM per device.

```python
import jax
import jax.numpy as jnp
from jax import lax

D = 1600
KVH = 5
HEAD = 64
INNER = 3200
STATE = 16
RANK = 100
CONV = 4
FF = 5504
WINDOW = 1024
LAYERS = 2
MICRO = 2
SCAN_BLOCK = 64
SLOT = 64
SEQS = 8
GQ = 5
QD = 1600
KVD = 320


def draw_lengths(key, part):
    key = jax.random.fold_in(key, 11)
    total = MICRO * SEQS
    key_len, key_top, key_low = jax.random.split(key, 3)
    values = jax.random.randint(key_len, (total,), SLOT // 4, SLOT + 1)
    top_pos = jax.random.randint(key_top, (), 0, total)
    low_pos = (top_pos + 1 + jax.random.randint(key_low, (), 0, total - 1)) % total
    values = values.at[top_pos].set(SLOT).at[low_pos].set(SLOT // 4)
    return values.reshape(MICRO, SEQS).astype(jnp.int32)


def level_of(rng, dims, cuts, low, high):
    level = 1.0
    for axis_at, shards_of in cuts:
        heights = jax.random.uniform(jax.random.fold_in(jax.random.fold_in(rng, 6), axis_at), (shards_of,), jnp.float32, low / len(cuts), high / len(cuts))
        level = level * jnp.repeat(jnp.exp(heights), dims[axis_at] // shards_of).reshape((-1,) + (1,) * (len(dims) - 1 - axis_at))
    return level


def noise(rng, shape, width, bound, pieces=(), dtype=jnp.bfloat16):
    values = width * jax.random.normal(rng, shape, jnp.float32)
    if pieces:
        values = values * level_of(rng, shape, pieces, -0.22, 0.18)
    return jnp.clip(values, -bound, bound).astype(dtype)


def setup_inputs(seed: int = 0) -> dict:
    seeds = jax.random.split(jax.random.key(seed), 19)
    return {
        "hidden_in": noise(seeds[0], (MICRO, SEQS, SLOT, D), 1.0, 6.0, ((1, 8),)),
        "out_grad": noise(seeds[1], (MICRO, SEQS, SLOT, D), 1.0, 6.0, ((1, 8),)),
        "lengths": draw_lengths(jax.random.fold_in(seeds[18], 71), 0),
        "norm_gains": jnp.clip(1.0 + 0.1 * jax.random.normal(seeds[3], (LAYERS, 4, D), jnp.float32), 0.5, 1.5),
        "q_weight": noise(seeds[4], (LAYERS, D, QD), D ** -0.5, 0.15625, ((1, 8),)),
        "kv_weight": noise(seeds[5], (LAYERS, D, 2, KVD), D ** -0.5, 0.15625, ((1, 8),)),
        "o_weight": noise(seeds[6], (LAYERS, QD, D), QD ** -0.5, 0.15625, ((2, 8),)),
        "in_weight": noise(seeds[7], (LAYERS, D, 2, INNER), D ** -0.5, 0.15625, ((1, 8), (3, 4))),
        "conv_weight": noise(seeds[8], (LAYERS, CONV, INNER), CONV ** -0.5, 3.0, ((2, 4),), jnp.float32),
        "conv_bias": noise(seeds[9], (LAYERS, INNER), 0.5, 3.0, ((1, 4),), jnp.float32),
        "step_bias": jnp.clip(-6.0 + 4.0 * jax.random.uniform(seeds[10], (LAYERS, INNER), jnp.float32) ** level_of(seeds[10], (LAYERS, INNER), ((1, 4),), -0.2, 0.2), -6.0, -2.0),
        "decay_log": jnp.clip(2.77 * jax.random.uniform(seeds[11], (LAYERS, INNER, STATE), jnp.float32) ** level_of(seeds[11], (LAYERS, INNER, STATE), ((1, 4),), -0.2, 0.2), 0.0, 2.77),
        "skip_gain": jnp.clip(0.5 + 1.0 * jax.random.uniform(seeds[12], (LAYERS, INNER), jnp.float32) ** level_of(seeds[12], (LAYERS, INNER), ((1, 4),), -0.2, 0.2), 0.5, 1.5),
        "scan_weight": noise(seeds[13], (LAYERS, INNER, RANK + 2 * STATE), INNER ** -0.5, 0.109375, ((1, 4),)),
        "step_weight": noise(seeds[14], (LAYERS, RANK, INNER), RANK ** -0.5, 0.625, ((2, 4),)),
        "ssm_weight": noise(seeds[15], (LAYERS, INNER, D), INNER ** -0.5, 0.109375, ((1, 4), (2, 8))),
        "gate_weight": noise(seeds[16], (LAYERS, D, 2, FF), D ** -0.5, 0.15625, ((1, 8), (3, 4))),
        "down_weight": noise(seeds[17], (LAYERS, FF, D), FF ** -0.5, 0.078125, ((1, 4), (2, 8))),
    }


EPSILON = 1e-06
HIGHEST = lax.Precision.HIGHEST

@jax.custom_vjp
def low(v):
    return lax.optimization_barrier(v.astype(jnp.bfloat16)).astype(jnp.float32)

@jax.custom_vjp
def low_back(v):
    return v

def low_keep(v):
    return (low(v), None)

def low_pass(kept, grad):
    return (grad,)

def back_keep(v):
    return (v, None)

def back_low(kept, grad):
    return (low(grad),)
low.defvjp(low_keep, low_pass)
low_back.defvjp(back_keep, back_low)

def rms_scale(values, gain_vec):
    return values * lax.rsqrt(lax.optimization_barrier(jnp.mean(values * values, axis=-1, keepdims=True)) + EPSILON) * gain_vec

def conv_silu(inner_in, conv_taps, conv_shift):
    length = inner_in.shape[0]
    padded = jnp.pad(inner_in, ((CONV - 1, 0), (0, 0)))
    running = conv_shift
    for offset in range(CONV):
        running = running + padded[offset:offset + length] * conv_taps[offset]
    return jax.nn.silu(running)

def combine_steps(earlier, later):
    return (earlier[0] * later[0], later[0] * earlier[1] + later[1])

def ssm_tail(step_raw, conv_out, drive_in, read_out, gate_in, step_shift, log_rates, skip_scale):
    step_size = jax.nn.softplus(step_raw + step_shift)
    rate_mat = -jnp.exp(log_rates).T
    length = conv_out.shape[0]
    blocks = length // SCAN_BLOCK

    def advance(state_in, block_in):
        conv_blk, step_blk, drive_blk, read_blk = block_in
        decay_step = jnp.exp(step_blk[:, None, :] * rate_mat[None])
        source = (step_blk * conv_blk)[:, None, :] * drive_blk[:, :, None]
        acc_decay, acc_source = lax.associative_scan(combine_steps, (decay_step, source), axis=0)
        states = acc_decay * state_in[None] + acc_source
        return (states[-1], lax.optimization_barrier(jnp.sum(states * read_blk[:, :, None], axis=1)))

    def shaped(values):
        return values.reshape((blocks, SCAN_BLOCK) + values.shape[1:])
    initial = jnp.zeros(rate_mat.shape, jnp.float32)
    _, outputs = lax.scan(jax.checkpoint(advance), initial, (shaped(conv_out), shaped(step_size), shaped(drive_in), shaped(read_out)))
    scanned = outputs.reshape(length, -1) + skip_scale * conv_out
    return scanned * jax.nn.silu(gate_in)

def mix_branches(resid_in, attn_out, ssm_out, gain_attn, gain_ssm, gain_ffn):
    residual = resid_in + 0.5 * (rms_scale(attn_out, gain_attn) + rms_scale(ssm_out, gain_ssm))
    return (residual, rms_scale(residual, gain_ffn))

def gate_product(gate_out):
    return jax.nn.silu(gate_out[:, 0]) * gate_out[:, 1]

def product(left, right):
    return jnp.dot(left, right, precision=HIGHEST, preferred_element_type=jnp.float32)

def attend_all(queries, key_rows, value_rows):
    length = queries.shape[0]
    block_rows = min(length, 512)
    count_blk = length // block_rows
    query_blocks = queries.reshape(count_blk, block_rows, KVH, GQ, HEAD)
    key_pos = jnp.arange(length)

    def one_block(block_in):
        query_blk, first_row = block_in
        scores = low_back(jnp.einsum('qgrd,kgd->grqk', query_blk, key_rows, precision=HIGHEST)) * HEAD ** (-0.5)
        query_pos = first_row + jnp.arange(block_rows)
        allowed = (key_pos[None, :] <= query_pos[:, None]) & (key_pos[None, :] > query_pos[:, None] - WINDOW)
        scores = jnp.where(allowed[None, None], scores, -jnp.inf)
        row_max = lax.optimization_barrier(jnp.max(scores, axis=-1, keepdims=True))
        weights = jnp.exp(scores - row_max)
        probability = low(weights / lax.optimization_barrier(jnp.sum(weights, axis=-1, keepdims=True)))
        return jnp.einsum('grqk,kgd->qgrd', probability, value_rows, precision=HIGHEST)
    outputs = lax.map(jax.checkpoint(one_block), (query_blocks, jnp.arange(count_blk) * block_rows))
    return outputs.reshape(length, KVH * GQ * HEAD)

def hymba_layer(resid_in, params):
    gains, query_mat, keyval_mat, heads_mat, inner_mat, conv_taps, conv_shift, step_shift, log_rates, skip_scale, scan_mat, step_mat, ssm_mat, gate_mat, down_mat = params
    length = resid_in.shape[0]
    normed = low(rms_scale(resid_in, gains[0]))
    queries = low(low_back(product(normed, query_mat))).reshape(length, KVH, GQ, HEAD)
    keyval = low(low_back(jnp.einsum('sd,dkc->skc', normed, keyval_mat, precision=HIGHEST)))
    key_rows = keyval[:, 0].reshape(length, KVH, HEAD)
    value_rows = keyval[:, 1].reshape(length, KVH, HEAD)
    heads_out = low(low_back(attend_all(queries, key_rows, value_rows)))
    attn_out = low_back(product(heads_out, heads_mat))
    inner_out = low_back(jnp.einsum('sd,dkc->skc', normed, inner_mat, precision=HIGHEST))
    conv_out = low(conv_silu(inner_out[:, 0], conv_taps, conv_shift))
    scan_proj = low_back(product(conv_out, scan_mat))
    step_raw = low_back(product(low(scan_proj[:, :RANK]), step_mat))
    gated = low(ssm_tail(step_raw, conv_out, scan_proj[:, RANK:RANK + STATE], scan_proj[:, RANK + STATE:], inner_out[:, 1], step_shift, log_rates, skip_scale))
    ssm_out = low_back(product(gated, ssm_mat))
    residual, ffn_pre = mix_branches(resid_in, attn_out, ssm_out, gains[1], gains[2], gains[3])
    ffn_in = low(ffn_pre)
    gate_out = low_back(jnp.einsum('sd,dkf->skf', ffn_in, gate_mat, precision=HIGHEST))
    activ = low(gate_product(gate_out))
    return residual + low_back(product(activ, down_mat))

def reference(hidden_in, out_grad, lengths, norm_gains, q_weight, kv_weight, o_weight, in_weight, conv_weight, conv_bias, step_bias, decay_log, skip_gain, scan_weight, step_weight, ssm_weight, gate_weight, down_weight):
    params = tuple((entry.astype(jnp.float32) for entry in (norm_gains, q_weight, kv_weight, o_weight, in_weight, conv_weight, conv_bias, step_bias, decay_log, skip_gain, scan_weight, step_weight, ssm_weight, gate_weight, down_weight)))

    def network(inputs, weights):
        running = inputs
        for layer_idx in range(LAYERS):
            running = hymba_layer(running, tuple((entry[layer_idx] for entry in weights)))
        return running
    count_seq = MICRO * SEQS
    inputs_all = hidden_in.reshape(count_seq, SLOT, D).astype(jnp.float32)
    cot_all = out_grad.reshape(count_seq, SLOT, D).astype(jnp.float32)
    length_all = lengths.reshape(count_seq)

    def one_sequence(grad_sums, scan_item):
        inputs, cotangent, seq_len = scan_item
        pad_mask = (jnp.arange(SLOT) < seq_len).astype(jnp.float32)[:, None]
        result, pull_back = jax.vjp(network, inputs, params)
        grad_in, grad_params = pull_back(cotangent * pad_mask)
        grad_sums = jax.tree.map(jnp.add, grad_sums, grad_params)
        return (grad_sums, ((result * pad_mask).astype(jnp.bfloat16), grad_in))
    zero_grads = jax.tree.map(jnp.zeros_like, params)
    grad_sums, (outputs, grads_in) = lax.scan(one_sequence, zero_grads, (inputs_all, cot_all, length_all))
    return (outputs.reshape(MICRO, SEQS, SLOT, D), grads_in.reshape(MICRO, SEQS, SLOT, D), grad_sums[0], grad_sums[1], grad_sums[2], grad_sums[3], grad_sums[4], grad_sums[5], grad_sums[6], grad_sums[7], grad_sums[8], grad_sums[9], grad_sums[10], grad_sums[11], grad_sums[12], grad_sums[13], grad_sums[14])
```

```python
import functools

import jax
import jax.numpy as jnp
from jax import lax
from jax.experimental import pallas as pl
from jax.experimental.pallas import tpu as pltpu
from jax.sharding import PartitionSpec as P

KVH = 5
HEAD = 64
GQ = 5
CONV = 4
WINDOW = 1024
EPSILON = 1e-06
GROUP = 4
LANES = 128
F32 = jnp.float32
BF16 = jnp.bfloat16
NN = (((1,), (0,)), ((), ()))
NT = (((1,), (1,)), ((), ()))
TN = (((0,), (0,)), ((), ()))


def mm(left, right, dims=NN):
    return lax.dot_general(left, right, dims, preferred_element_type=F32)


def sigmoid(v):
    return 1.0 / (1.0 + jnp.exp(-v))


def softplus(v):
    return jnp.maximum(v, 0.0) + jnp.log(1.0 + jnp.exp(-jnp.abs(v)))


def params(megabytes=56):
    return pltpu.CompilerParams(vmem_limit_bytes=megabytes * 2**20)


def cost(flops, moved):
    return pl.CostEstimate(flops=int(flops), bytes_accessed=int(moved), transcendentals=0)


def call(kernel, outs, args, flops, scratch=()):
    moved = sum(a.size * a.dtype.itemsize for a in args)
    moved += sum(o.size * o.dtype.itemsize for o in outs)
    vmem = pl.BlockSpec(memory_space=pltpu.VMEM)
    return pl.pallas_call(
        kernel,
        out_shape=outs,
        in_specs=[vmem] * len(args),
        out_specs=[vmem] * len(outs),
        scratch_shapes=list(scratch),
        compiler_params=params(),
        cost_estimate=cost(flops, moved),
    )(*args)


def out(shape, dtype):
    return jax.ShapeDtypeStruct(shape, dtype)


def widen(values, width):
    rows, have = values.shape
    if have == width:
        return values
    return jnp.concatenate([values, jnp.zeros((rows, width - have), values.dtype)], axis=1)


def shift_rows(values, amount, length):
    if amount == 0:
        return values
    rows = values.shape[0]
    place = lax.broadcasted_iota(jnp.int32, values.shape, 0) % length
    moved = pltpu.roll(values, amount % rows, 0)
    inside = place >= amount if amount > 0 else place < length + amount
    return jnp.where(inside, moved, 0.0)


def conv_pre(inner_x, taps, bias, length):
    running = bias
    for k in range(CONV):
        running = running + shift_rows(inner_x, CONV - 1 - k, length) * taps[k : k + 1]
    return running


def scores_of(queries, keys, length):
    scores = lax.dot_general(
        queries, keys, (((2,), (2,)), ((0,), (0,))), preferred_element_type=F32
    ) * HEAD ** (-0.5)
    shape = scores.shape
    query_pos = lax.broadcasted_iota(jnp.int32, shape, 1)
    key_pos = lax.broadcasted_iota(jnp.int32, shape, 2)
    allowed = (key_pos <= query_pos) & (key_pos > query_pos - WINDOW)
    scores = jnp.where(allowed, scores, -1e30)
    weights = jnp.exp(scores - jnp.max(scores, axis=-1, keepdims=True))
    return weights / jnp.sum(weights, axis=-1, keepdims=True)


class Mix:
    def __init__(self, chan):
        self.q = 0
        self.kv = 2 * HEAD
        self.o = 4 * HEAD
        self.x = 6 * HEAD
        self.z = self.x + chan
        self.s = self.z + chan
        self.end = self.s + chan


def mix_forward_kernel(cols, chan, wide, length, n, w, taps, bias, scan_w, xi, z, conv, qkv, heads, proj, attn):
    normed = n[...]
    both = mm(normed, w[:, : cols.o]).astype(BF16)
    qkv[...] = both
    inner = mm(normed, w[:, cols.x : cols.s])
    inner_x = widen(inner[:, :chan], wide)
    xi[...] = inner_x
    z[...] = widen(inner[:, chan:], wide)
    running = conv_pre(inner_x, taps[...], bias[...], length)
    conv_low = (running * sigmoid(running)).astype(BF16)
    conv[...] = conv_low
    proj[...] = mm(scan_w[...], conv_low, NT).astype(BF16)
    seqs = normed.shape[0] // length
    keys = both[:, cols.kv : cols.kv + HEAD].reshape(seqs, length, HEAD)
    values = both[:, cols.kv + HEAD : cols.o].reshape(seqs, length, HEAD)
    outs = []
    for h in range(2):
        queries = both[:, h * HEAD : (h + 1) * HEAD].reshape(seqs, length, HEAD)
        probs = scores_of(queries, keys, length).astype(BF16)
        mixed = lax.dot_general(
            probs, values, (((2,), (1,)), ((0,), (0,))), preferred_element_type=F32
        )
        outs.append(mixed.reshape(seqs * length, HEAD))
    heads_out = jnp.concatenate(outs, axis=1).astype(BF16)
    heads[...] = heads_out
    attn[...] = mm(heads_out, w[:, cols.o : cols.x], NT).astype(BF16)


def spread(state, wide):
    row = lax.broadcasted_iota(jnp.int32, (state, wide), 0)
    col = lax.broadcasted_iota(jnp.int32, (state, wide), 1) // LANES
    return (row == col).astype(BF16)


def lane(n):
    return slice(n * LANES, (n + 1) * LANES)


def tiles_in(ref, values):
    for n in range(ref.shape[0]):
        ref[n] = values[:, lane(n)]


def tiles_out(ref):
    return jnp.concatenate([ref[n] for n in range(ref.shape[0])], axis=1)


def scan_setup(rank, state, seqs, proj, conv, step_w, step_b, dlog, dt_s, dtx_s, drive_s, read_s, rate_s):
    pre = mm(proj[:rank], step_w[...], TN) + step_b[...]
    dt = softplus(pre)
    tiles_in(dt_s, dt)
    tiles_in(dtx_s, dt * conv)
    table = spread(state, state * LANES)
    tiles_in(drive_s, mm(proj[rank : rank + state], table, TN))
    tiles_in(read_s, mm(proj[rank + state :], table, TN))
    rates = -jnp.exp(dlog[...])
    for n in range(state):
        rate_s[n] = jnp.broadcast_to(rates[n : n + 1], (seqs, rates.shape[1]))
    return pre


def scan_forward_loop(state, seqs, length, tile, dt_s, dtx_s, drive_s, read_s, rate_s, y_s, keep_s):
    def step(t, held):
        rows = pl.ds(t, seqs, stride=length)
        dt = dt_s[tile, rows]
        dtx = dtx_s[tile, rows]
        total = jnp.zeros_like(dt)
        fresh = []
        for n in range(state):
            now = jnp.exp(dt * rate_s[n, :, lane(tile)]) * held[n] + dtx * drive_s[n, rows]
            total = total + now * read_s[n, rows]
            if keep_s is not None:
                keep_s[t, n] = now
            fresh.append(now)
        y_s[tile, rows] = total
        return tuple(fresh)

    zero = jnp.zeros((seqs, LANES), F32)
    lax.fori_loop(0, length, step, (zero,) * state)


def scan_forward_kernel(cols, chan, wide, rank, state, seqs, length, proj, conv, z, step_w, step_b, dlog, skip, w, gated, ssm, dt_s, dtx_s, drive_s, read_s, rate_s, y_s):
    conv32 = conv[...].astype(F32)
    scan_setup(rank, state, seqs, proj, conv32, step_w, step_b, dlog, dt_s, dtx_s, drive_s, read_s, rate_s)
    for tile in range(wide // LANES):
        scan_forward_loop(state, seqs, length, tile, dt_s, dtx_s, drive_s, read_s, rate_s, y_s, None)
    gate = z[...]
    low = ((tiles_out(y_s) + skip[...] * conv32) * (gate * sigmoid(gate))).astype(BF16)
    gated[...] = low
    ssm[...] = mm(low[:, :chan], w[:, cols.s :], NT).astype(BF16)


def split_sum(table, values):
    high = values.astype(BF16)
    rest = (values - high.astype(F32)).astype(BF16)
    return mm(table, high, NT) + mm(table, rest, NT)


def scan_backward_kernel(cols, chan, wide, rank, state, seqs, length, grad, proj, conv, z, step_w, step_b, dlog, skip, w, d_proj, d_conv, d_z, small, d_step_w, dt_s, dtx_s, drive_s, read_s, rate_s, y_s, keep_s, ds_s, ddt_s, pd_s, pr_s, dr_s):
    conv32 = conv[...].astype(F32)
    pre = scan_setup(rank, state, seqs, proj, conv32, step_w, step_b, dlog, dt_s, dtx_s, drive_s, read_s, rate_s)
    d_gated = widen(mm(grad[...], w[:, cols.s :]), wide)
    gate = z[...]
    sig = sigmoid(gate)
    d_scanned = d_gated * (gate * sig)
    tiles_in(ds_s, d_scanned)
    d_rates = []
    for tile in range(wide // LANES):
        scan_forward_loop(state, seqs, length, tile, dt_s, dtx_s, drive_s, read_s, rate_s, y_s, keep_s)
        for n in range(state):
            dr_s[n] = jnp.zeros((seqs, LANES), F32)

        def step(back, carry):
            t = length - 1 - back
            rows = pl.ds(t, seqs, stride=length)
            dt = dt_s[tile, rows]
            dtx = dtx_s[tile, rows]
            ds = ds_s[tile, rows]
            earlier = jnp.maximum(t - 1, 0)
            alive = jnp.where(t > 0, 1.0, 0.0)
            d_src = jnp.zeros_like(dt)
            d_dt = jnp.zeros_like(dt)
            fresh = []
            for n in range(state):
                rate = rate_s[n, :, lane(tile)]
                lam = carry[n] + read_s[n, rows] * ds
                prod_read = keep_s[t, n] * ds
                prod_drive = lam * dtx
                if tile == 0:
                    pr_s[n, rows] = prod_read
                    pd_s[n, rows] = prod_drive
                else:
                    pr_s[n, rows] = pr_s[n, rows] + prod_read
                    pd_s[n, rows] = pd_s[n, rows] + prod_drive
                d_src = d_src + lam * drive_s[n, rows]
                passed = jnp.exp(dt * rate) * lam
                d_log = passed * (keep_s[earlier, n] * alive)
                d_dt = d_dt + d_log * rate
                dr_s[n] = dr_s[n] + d_log * dt
                fresh.append(passed)
            ddt_s[tile, rows] = d_dt
            dtx_s[tile, rows] = d_src
            return tuple(fresh)

        zero = jnp.zeros((seqs, LANES), F32)
        lax.fori_loop(0, length, step, (zero,) * state)
        d_rates.append(
            jnp.concatenate(
                [jnp.sum(dr_s[n], axis=0, keepdims=True) for n in range(state)], axis=0
            )
        )
    d_src = tiles_out(dtx_s)
    dt = tiles_out(dt_s)
    d_dt = tiles_out(ddt_s) + d_src * conv32
    d_conv[...] = skip[...] * d_scanned + d_src * dt
    scanned = tiles_out(y_s) + skip[...] * conv32
    d_z[...] = (d_gated * scanned * (sig * (1.0 + gate * (1.0 - sig)))).astype(BF16)
    d_pre = d_dt * sigmoid(pre)
    rates = -jnp.exp(dlog[...])
    d_log = jnp.concatenate(d_rates, axis=1) * rates
    small[0:1] = jnp.sum(d_pre, axis=0, keepdims=True)
    small[1:2] = jnp.sum(d_scanned * conv32, axis=0, keepdims=True)
    small[2:8] = jnp.zeros((6, wide), F32)
    small[8:] = d_log
    low = d_pre.astype(BF16)
    d_step_w[...] = mm(proj[:rank], low)
    table = spread(state, state * LANES)
    d_proj[:rank] = mm(step_w[...], low, NT).astype(BF16)
    d_proj[rank : rank + state] = split_sum(table, tiles_out(pd_s)).astype(BF16)
    d_proj[rank + state :] = split_sum(table, tiles_out(pr_s)).astype(BF16)


def attend_backward_kernel(cols, length, grad, w, qkv, d_qkv):
    d_heads = mm(grad[...], w[:, cols.o : cols.x]).astype(BF16)
    both = qkv[...]
    seqs = both.shape[0] // length
    keys = both[:, cols.kv : cols.kv + HEAD].reshape(seqs, length, HEAD)
    values = both[:, cols.kv + HEAD : cols.o].reshape(seqs, length, HEAD)
    parts = []
    d_keys = 0.0
    d_values = 0.0
    for h in range(2):
        queries = both[:, h * HEAD : (h + 1) * HEAD].reshape(seqs, length, HEAD)
        d_out = d_heads[:, h * HEAD : (h + 1) * HEAD].reshape(seqs, length, HEAD)
        probs = scores_of(queries, keys, length)
        d_probs = lax.dot_general(
            d_out, values, (((2,), (2,)), ((0,), (0,))), preferred_element_type=F32
        )
        d_scores = (
            probs
            * (d_probs - jnp.sum(d_probs * probs, axis=-1, keepdims=True))
            * HEAD ** (-0.5)
        ).astype(BF16)
        d_query = lax.dot_general(
            d_scores, keys, (((2,), (1,)), ((0,), (0,))), preferred_element_type=F32
        )
        parts.append(d_query.reshape(seqs * length, HEAD))
        d_keys = d_keys + lax.dot_general(
            d_scores, queries, (((1,), (1,)), ((0,), (0,))), preferred_element_type=F32
        )
        d_values = d_values + lax.dot_general(
            probs.astype(BF16), d_out, (((1,), (1,)), ((0,), (0,))), preferred_element_type=F32
        )
    parts.append(d_keys.reshape(seqs * length, HEAD))
    parts.append(d_values.reshape(seqs * length, HEAD))
    d_qkv[...] = jnp.concatenate(parts, axis=1).astype(BF16)


def mix_backward_kernel(cols, chan, length, proj, conv, xi, d_conv, d_z, d_qkv, w, taps, bias, scan_w, d_x, part, d_scan_w, small):
    d_out = d_conv[...] + mm(proj[...], scan_w[...], TN)
    inner_x = xi[...]
    running = conv_pre(inner_x, taps[...], bias[...], length)
    sig = sigmoid(running)
    d_run = d_out * (sig * (1.0 + running * (1.0 - sig)))
    d_in = 0.0
    for k in range(CONV):
        back = CONV - 1 - k
        d_in = d_in + shift_rows(d_run, -back, length) * taps[k : k + 1]
        small[k : k + 1] = jnp.sum(d_run * shift_rows(inner_x, back, length), axis=0, keepdims=True)
    small[CONV : CONV + 1] = jnp.sum(d_run, axis=0, keepdims=True)
    small[CONV + 1 :] = jnp.zeros((8 - CONV - 1, inner_x.shape[1]), F32)
    low = d_in.astype(BF16)
    d_x[...] = low
    inner = jnp.concatenate([low[:, :chan], d_z[:, :chan]], axis=1)
    part[...] = (
        mm(inner, w[:, cols.x : cols.s], NT) + mm(d_qkv[...], w[:, : cols.o], NT)
    ).astype(BF16)
    d_scan_w[...] = mm(proj[...], conv[...])


def mix_weights_kernel(cols, chan, n, d_attn, d_ssm, d_qkv, heads, d_x, d_z, gated, d_w):
    normed = n[...]
    d_w[:, : cols.o] = mm(normed, d_qkv[...], TN).astype(BF16)
    d_w[:, cols.o : cols.x] = mm(d_attn[...], heads[...], TN).astype(BF16)
    d_w[:, cols.x : cols.z] = mm(normed, d_x[:, :chan], TN).astype(BF16)
    d_w[:, cols.z : cols.s] = mm(normed, d_z[:, :chan], TN).astype(BF16)
    d_w[:, cols.s :] = mm(d_ssm[...], gated[:, :chan], TN).astype(BF16)


def ffn_forward_kernel(units, f, w, hidden, part):
    both = mm(f[...], w[:, : 2 * units])
    hidden[...] = both
    gate = both[:, :units]
    activ = (gate * sigmoid(gate) * both[:, units:]).astype(BF16)
    part[...] = mm(activ, w[:, 2 * units :], NT).astype(BF16)


def ffn_backward_kernel(units, d_out, hidden, w, d_hidden, activ, part):
    d_activ = mm(d_out[...], w[:, 2 * units :])
    gate = hidden[:, :units]
    up = hidden[:, units:]
    sig = sigmoid(gate)
    swish = gate * sig
    activ[...] = (swish * up).astype(BF16)
    low = jnp.concatenate(
        [d_activ * up * (sig * (1.0 + gate * (1.0 - sig))), d_activ * swish], axis=1
    ).astype(BF16)
    d_hidden[...] = low
    part[...] = mm(low, w[:, : 2 * units], NT).astype(BF16)


def ffn_weights_kernel(units, f, d_out, d_hidden, activ, d_w):
    d_w[:, : 2 * units] = mm(f[...], d_hidden[...], TN).astype(BF16)
    d_w[:, 2 * units :] = mm(d_out[...], activ[...], TN).astype(BF16)


def rms_scale(values, gain_vec):
    return (
        values * lax.rsqrt(jnp.mean(values * values, axis=-1, keepdims=True) + EPSILON) * gain_vec
    )


def mix_branches(resid_in, attn_out, ssm_out, gain_attn, gain_ssm, gain_ffn):
    residual = resid_in + 0.5 * (rms_scale(attn_out, gain_attn) + rms_scale(ssm_out, gain_ssm))
    return (residual, rms_scale(residual, gain_ffn))


def per_device(
    dp_size,
    tensor_size,
    hidden_in,
    out_grad,
    lengths,
    norm_gains,
    q_weight,
    kv_weight,
    o_weight,
    in_weight,
    conv_weight,
    conv_bias,
    step_bias,
    decay_log,
    skip_gain,
    scan_weight,
    step_weight,
    ssm_weight,
    gate_weight,
    down_weight,
):
    layers = q_weight.shape[0]
    batches, _, length, width = hidden_in.shape
    fast = dp_size // GROUP
    share = width // dp_size
    chan = in_weight.shape[3] // GROUP
    wide = -(-chan // LANES) * LANES
    units = gate_weight.shape[3] // GROUP
    rank_true = step_weight.shape[1]
    state = decay_log.shape[2]
    rank = -(-rank_true // 16) * 16
    proj_rows = rank + 2 * state
    cols = Mix(chan)
    ffn_cols = 3 * units
    dp_idx = lax.axis_index("dp")
    slow_idx = dp_idx // fast
    fast_idx = dp_idx % fast
    tensor_idx = lax.axis_index("tensor")
    rows_here = batches * length // tensor_size
    seqs = GROUP * batches
    tokens = seqs * length
    half = tensor_size // 2

    def slow_perm(by):
        return [
            (s * fast + f, ((s + by) % GROUP) * fast + f) for s in range(GROUP) for f in range(fast)
        ]

    def fast_perm(by):
        return [
            (s * fast + f, s * fast + (f + by) % fast) for s in range(GROUP) for f in range(fast)
        ]

    core_perm = [(t, t ^ 1) for t in range(tensor_size)]
    chip_perm = [(t, t ^ 2) for t in range(tensor_size)]
    core_idx = tensor_idx % 2
    chip_idx = tensor_idx // 2

    def slow(values, by):
        return lax.ppermute(values, "dp", slow_perm(by)) if by % GROUP else values

    def other_fast(values, by):
        return lax.ppermute(values, "dp", fast_perm(by)) if by % fast else values

    def add_low(*terms):
        total = terms[0].astype(F32)
        for term in terms[1:]:
            total = total + term.astype(F32)
        return total.astype(BF16)

    def gather_tokens(own):
        parts = jnp.stack([slow(own, by) for by in range(GROUP)])
        moved = lax.ppermute(parts, "tensor", chip_perm)
        parts = jnp.where(chip_idx == 0, jnp.stack([parts, moved], 1), jnp.stack([moved, parts], 1))
        moved = lax.ppermute(parts, "tensor", core_perm)
        parts = jnp.where(core_idx == 0, jnp.stack([parts, moved], 2), jnp.stack([moved, parts], 2))
        return parts.reshape(tokens, own.shape[1])

    def scatter_tokens(full):
        parts = full.reshape(GROUP, half, 2, rows_here, full.shape[1])
        mine = lax.dynamic_index_in_dim(parts, core_idx, 2, False)
        theirs = lax.dynamic_index_in_dim(parts, 1 - core_idx, 2, False)
        parts = add_low(mine, lax.ppermute(theirs, "tensor", core_perm))
        mine = lax.dynamic_index_in_dim(parts, chip_idx, 1, False)
        theirs = lax.dynamic_index_in_dim(parts, 1 - chip_idx, 1, False)
        parts = add_low(mine, lax.ppermute(theirs, "tensor", chip_perm))
        total = parts[0].astype(F32)
        for by in range(1, GROUP):
            total = total + slow(parts[by], GROUP - by).astype(F32)
        return total

    def sum_group(values):
        values = add_low(values, lax.ppermute(values, "tensor", core_perm))
        values = add_low(values, lax.ppermute(values, "tensor", chip_perm))
        chunk = tokens // GROUP
        parts = [values[:, k * chunk : (k + 1) * chunk] for k in range(GROUP)]
        total = add_low(parts[0], *[slow(parts[by], GROUP - by) for by in range(1, GROUP)])
        return jnp.concatenate([slow(total, by) for by in range(GROUP)], axis=1)

    def fetch(packed):
        columns = packed.shape[2]
        place = lax.dynamic_index_in_dim
        full = jnp.zeros((GROUP, fast, share, columns), BF16)
        for by in range(GROUP):
            got = slow(place(packed, (slow_idx + by) % GROUP, 0, False), by)
            source = (slow_idx - by) % GROUP
            for turn in range(fast):
                piece = other_fast(got, turn)
                full = lax.dynamic_update_slice(
                    full, piece[None, None], (source, (fast_idx - turn) % fast, 0, 0)
                )
        return full.reshape(width, columns)

    def settle(grad):
        columns = grad.shape[1]
        grad = grad.reshape(GROUP, fast, share, columns)
        pieces = []
        for by in range(GROUP):
            target = lax.dynamic_index_in_dim(grad, (slow_idx + by) % GROUP, 0, False)
            terms = [
                other_fast(
                    lax.dynamic_index_in_dim(target, (fast_idx + turn) % fast, 0, False), turn
                )
                for turn in range(fast)
            ]
            pieces.append(slow(add_low(*terms), by))
        stacked = jnp.stack(pieces)
        return [
            lax.dynamic_index_in_dim(stacked, (slow_idx - source) % GROUP, 0, False)
            for source in range(GROUP)
        ]

    def pack_mix(layer):
        padded_q = jnp.pad(q_weight[layer], ((0, 0), (0, 2 * HEAD)))
        padded_o = jnp.pad(o_weight[layer], ((0, 2 * HEAD), (0, 0)))
        ssm_t = ssm_weight[layer].T
        pieces = []
        for s in range(GROUP):
            unit = s * tensor_size + tensor_idx
            group = unit // 3
            sub = unit % 3
            start = group * GQ * HEAD + sub * 2 * HEAD
            valid = jnp.where(group >= KVH, 0, jnp.where(sub == 2, HEAD, 2 * HEAD))
            keep = jnp.arange(2 * HEAD) < valid
            query = lax.dynamic_slice_in_dim(padded_q, start, 2 * HEAD, 1)
            query = jnp.where(keep[None], query, 0)
            output = lax.dynamic_slice_in_dim(padded_o, start, 2 * HEAD, 0)
            output = jnp.where(keep[:, None], output, 0).T
            keyval = lax.dynamic_slice_in_dim(
                kv_weight[layer], jnp.minimum(group, KVH - 1) * HEAD, HEAD, 2
            )
            inner = in_weight[layer, :, :, s * chan : (s + 1) * chan]
            pieces.append(
                jnp.concatenate(
                    [
                        query,
                        keyval[:, 0],
                        keyval[:, 1],
                        output,
                        inner[:, 0],
                        inner[:, 1],
                        ssm_t[:, s * chan : (s + 1) * chan],
                    ],
                    axis=1,
                )
            )
        return jnp.stack(pieces)

    def pack_ffn(layer):
        down_t = down_weight[layer].T
        return jnp.stack(
            [
                jnp.concatenate(
                    [
                        gate_weight[layer, :, 0, s * units : (s + 1) * units],
                        gate_weight[layer, :, 1, s * units : (s + 1) * units],
                        down_t[:, s * units : (s + 1) * units],
                    ],
                    axis=1,
                )
                for s in range(GROUP)
            ]
        )

    def after(values, *earlier):
        return lax.optimization_barrier((values,) + earlier)[0]

    pad_chan = ((0, 0), (0, wide - chan))

    def channels(values, axis):
        return lax.dynamic_slice_in_dim(values, slow_idx * chan, chan, axis)

    small_weights = []
    for layer in range(layers):
        scan_t = channels(scan_weight[layer], 0).T
        scan_t = jnp.concatenate(
            [
                scan_t[:rank_true],
                jnp.zeros((rank - rank_true, chan), BF16),
                scan_t[rank_true:],
            ],
            axis=0,
        )
        step_mat = jnp.pad(channels(step_weight[layer], 1), ((0, rank - rank_true), (0, 0)))
        small_weights.append(
            (
                jnp.pad(channels(conv_weight[layer], 1), pad_chan),
                jnp.pad(channels(conv_bias[layer][None], 1), pad_chan),
                jnp.pad(scan_t, pad_chan),
                jnp.pad(step_mat, pad_chan),
                jnp.pad(channels(step_bias[layer][None], 1), pad_chan),
                jnp.pad(channels(decay_log[layer], 0).T, pad_chan),
                jnp.pad(channels(skip_gain[layer][None], 1), pad_chan),
            )
        )

    fetched = []
    for layer in range(layers):
        fetched.append((fetch(pack_mix(layer)), fetch(pack_ffn(layer))))

    bf_rows = lambda columns: out((tokens, columns), BF16)
    f_rows = lambda columns: out((tokens, columns), F32)
    tiled = pltpu.VMEM((wide // LANES, tokens, LANES), F32)
    state_tiled = pltpu.VMEM((state, tokens, LANES), F32)
    scan_scratch = [
        tiled,
        tiled,
        state_tiled,
        state_tiled,
        pltpu.VMEM((state, seqs, wide), F32),
        tiled,
    ]

    def own_rows(values):
        flat = values.reshape(batches * length, width)
        return lax.dynamic_slice_in_dim(flat, tensor_idx * rows_here, rows_here, 0)

    running = own_rows(hidden_in).astype(F32)
    kept = []
    for layer in range(layers):
        mix_w, ffn_w = fetched[layer]
        gains = norm_gains[layer]
        taps, bias, scan_w, step_w, step_b, dlog, skip = small_weights[layer]
        normed, pull_input = jax.vjp(rms_scale, running, gains[0])
        n = gather_tokens(normed.astype(BF16))
        xi, z, conv, qkv, heads, proj_part, attn_part = call(
            functools.partial(mix_forward_kernel, cols, chan, wide, length),
            [
                f_rows(wide),
                f_rows(wide),
                bf_rows(wide),
                bf_rows(cols.o),
                bf_rows(2 * HEAD),
                out((proj_rows, tokens), BF16),
                bf_rows(width),
            ],
            [n, mix_w, taps, bias, scan_w],
            2 * tokens * width * (cols.s),
        )
        proj = sum_group(proj_part)
        attn_out = scatter_tokens(attn_part)
        gated, ssm_part = call(
            functools.partial(
                scan_forward_kernel, cols, chan, wide, rank, state, seqs, length
            ),
            [bf_rows(wide), bf_rows(width)],
            [proj, conv, z, step_w, step_b, dlog, skip, mix_w],
            2 * tokens * width * chan + 100 * tokens * wide * state,
            scan_scratch,
        )
        ssm_out = scatter_tokens(ssm_part)
        (residual, ffn_in), pull_mix = jax.vjp(
            mix_branches, running, attn_out, ssm_out, gains[1], gains[2], gains[3]
        )
        f = gather_tokens(ffn_in.astype(BF16))
        hidden, ffn_part = call(
            functools.partial(ffn_forward_kernel, units),
            [f_rows(2 * units), bf_rows(width)],
            [f, ffn_w],
            2 * tokens * width * ffn_cols,
        )
        running = residual + scatter_tokens(ffn_part)
        kept.append((n, pull_input, xi, z, conv, qkv, heads, proj, gated, pull_mix, f, hidden))

    place = tensor_idx * rows_here + jnp.arange(rows_here)
    mask = (place % length < lengths[place // length, 0]).astype(F32)[:, None]
    output = (running * mask).astype(BF16)
    grad_run = own_rows(out_grad).astype(F32) * mask

    def all_rows(own):
        moved = lax.all_gather(own, "tensor", axis=0, tiled=True)
        return moved.reshape(batches, 1, length, width)

    output = all_rows(output)

    big_grads = [None] * layers
    small_grads = [None] * layers
    gain_grads = [None] * layers
    for layer in reversed(range(layers)):
        mix_w, ffn_w = fetched[layer]
        taps, bias, scan_w, step_w, step_b, dlog, skip = small_weights[layer]
        n, pull_input, xi, z, conv, qkv, heads, proj, gated, pull_mix, f, hidden = kept[layer]
        d_out = gather_tokens(grad_run.astype(BF16))
        d_hidden, activ, part = call(
            functools.partial(ffn_backward_kernel, units),
            [bf_rows(2 * units), bf_rows(units), bf_rows(width)],
            [d_out, hidden, ffn_w],
            2 * tokens * width * ffn_cols,
        )
        d_ffn_in = scatter_tokens(part)
        (d_ffn_w,) = call(
            functools.partial(ffn_weights_kernel, units),
            [out((width, ffn_cols), BF16)],
            [f, d_out, d_hidden, activ],
            2 * tokens * width * ffn_cols,
        )
        ffn_pieces = settle(d_ffn_w)
        grad_resid, d_attn, d_ssm, d_gain_attn, d_gain_ssm, d_gain_ffn = pull_mix(
            (grad_run, d_ffn_in)
        )
        d_attn = gather_tokens(d_attn.astype(BF16))
        d_ssm = gather_tokens(d_ssm.astype(BF16))
        d_proj, d_conv, d_z, small_scan, d_step_w = call(
            functools.partial(
                scan_backward_kernel, cols, chan, wide, rank, state, seqs, length
            ),
            [
                out((proj_rows, tokens), BF16),
                f_rows(wide),
                bf_rows(wide),
                out((8 + state, wide), F32),
                out((rank, wide), F32),
            ],
            [d_ssm, proj, conv, z, step_w, step_b, dlog, skip, mix_w],
            2 * tokens * width * chan + 400 * tokens * wide * state,
            scan_scratch
            + [
                pltpu.VMEM((length, state, seqs, LANES), F32),
                tiled,
                tiled,
                state_tiled,
                state_tiled,
                pltpu.VMEM((state, seqs, LANES), F32),
            ],
        )
        d_proj = sum_group(d_proj)
        (d_qkv,) = call(
            functools.partial(attend_backward_kernel, cols, length),
            [bf_rows(cols.o)],
            [d_attn, mix_w, qkv],
            2 * tokens * width * 2 * HEAD,
        )
        d_x, part, d_scan_w, small_conv = call(
            functools.partial(mix_backward_kernel, cols, chan, length),
            [
                bf_rows(wide),
                bf_rows(width),
                out((proj_rows, wide), F32),
                out((8, wide), F32),
            ],
            [d_proj, conv, xi, d_conv, d_z, d_qkv, mix_w, taps, bias, scan_w],
            2 * tokens * width * (cols.s),
        )
        d_normed = scatter_tokens(part)
        (d_mix_w,) = call(
            functools.partial(mix_weights_kernel, cols, chan),
            [out((width, cols.end), BF16)],
            [n, d_attn, d_ssm, d_qkv, heads, d_x, d_z, gated],
            2 * tokens * width * cols.end,
        )
        mix_pieces = settle(d_mix_w)
        grad_lower, d_gain_input = pull_input(d_normed)
        grad_run = grad_resid + grad_lower
        big_grads[layer] = (mix_pieces, ffn_pieces)
        small_grads[layer] = jnp.concatenate([small_scan, small_conv, d_step_w, d_scan_w], axis=0)
        gain_grads[layer] = jnp.stack([d_gain_input, d_gain_attn, d_gain_ssm, d_gain_ffn])

    input_grad = all_rows(grad_run.astype(BF16)).astype(F32)
    grad_gains = lax.psum(jnp.stack(gain_grads).astype(BF16), ("dp", "tensor")).astype(F32)

    small = jnp.stack(small_grads)[:, :, :chan].astype(BF16)
    small = add_low(*[other_fast(small, turn) for turn in range(fast)])
    turned = jnp.stack([slow(small, by) for by in range(GROUP)])
    small = jnp.concatenate(
        [
            lax.dynamic_index_in_dim(turned, (slow_idx - source) % GROUP, 0, False)
            for source in range(GROUP)
        ],
        axis=2,
    ).astype(F32)
    base = 8 + state
    grad_step_bias = small[:, 0]
    grad_skip = small[:, 1]
    grad_decay = small[:, 8:base].transpose(0, 2, 1)
    grad_conv_weight = small[:, base : base + CONV]
    grad_conv_bias = small[:, base + CONV]
    base = base + 8
    grad_step_weight = small[:, base : base + rank_true]
    base = base + rank
    scan_rows = jnp.concatenate(
        [small[:, base : base + rank_true], small[:, base + rank :]], axis=1
    )
    grad_scan = scan_rows.transpose(0, 2, 1)

    def joined(pieces, start, stop):
        return jnp.concatenate([p[:, start:stop] for p in pieces], axis=1).astype(F32)

    def by_unit(pieces, start, stop):
        mine = jnp.stack([p[:, start:stop] for p in pieces])
        every = lax.all_gather(mine, "tensor", axis=1)
        return every.reshape((GROUP * tensor_size,) + mine.shape[1:])

    grads = {name: [] for name in ("q", "kv", "o", "in", "ssm", "gate", "down")}
    for layer in range(layers):
        mix_pieces, ffn_pieces = big_grads[layer]
        every = by_unit(mix_pieces, 0, cols.x)

        def heads_of(start):
            parts = []
            for group in range(KVH):
                parts.append(every[3 * group, :, start : start + 2 * HEAD])
                parts.append(every[3 * group + 1, :, start : start + 2 * HEAD])
                parts.append(every[3 * group + 2, :, start : start + HEAD])
            return jnp.concatenate(parts, axis=1).astype(F32)

        def group_sum(start):
            parts = [
                sum(every[3 * group + i, :, start : start + HEAD].astype(F32) for i in range(3))
                for group in range(KVH)
            ]
            return jnp.concatenate(parts, axis=1)

        grads["q"].append(heads_of(cols.q))
        grads["kv"].append(jnp.stack([group_sum(cols.kv), group_sum(cols.kv + HEAD)], axis=1))
        grads["o"].append(heads_of(cols.o).T)
        grads["in"].append(
            jnp.stack(
                [joined(mix_pieces, cols.x, cols.z), joined(mix_pieces, cols.z, cols.s)], axis=1
            )
        )
        grads["ssm"].append(joined(mix_pieces, cols.s, cols.end).T)
        grads["gate"].append(
            jnp.stack(
                [joined(ffn_pieces, 0, units), joined(ffn_pieces, units, 2 * units)], axis=1
            )
        )
        grads["down"].append(joined(ffn_pieces, 2 * units, 3 * units).T)
    grads = {name: jnp.stack(parts) for name, parts in grads.items()}
    return (
        output,
        input_grad,
        grad_gains,
        grads["q"],
        grads["kv"],
        grads["o"],
        grads["in"],
        grad_conv_weight,
        grad_conv_bias,
        grad_step_bias,
        grad_decay,
        grad_skip,
        grad_scan,
        grad_step_weight,
        grads["ssm"],
        grads["gate"],
        grads["down"],
    )


def solution(mesh):
    return jax.shard_map(
        functools.partial(per_device, mesh.shape["dp"], mesh.shape["tensor"]),
        mesh=mesh,
        in_specs=(
            P(None, "dp", None, None),
            P(None, "dp", None, None),
            P(None, "dp"),
            P(),
            P(None, "dp", None),
            P(None, "dp", None, None),
            P(None, None, "dp"),
            P(None, "dp", None, "tensor"),
            P(None, None, "tensor"),
            P(None, "tensor"),
            P(None, "tensor"),
            P(None, "tensor", None),
            P(None, "tensor"),
            P(None, "tensor", None),
            P(None, None, "tensor"),
            P(None, "tensor", "dp"),
            P(None, "dp", None, "tensor"),
            P(None, "tensor", "dp"),
        ),
        out_specs=(
            P(None, "dp", None, None),
            P(None, "dp", None, None),
            P(),
            P(None, "dp", None),
            P(None, "dp", None, None),
            P(None, None, "dp"),
            P(None, "dp", None, "tensor"),
            P(None, None, "tensor"),
            P(None, "tensor"),
            P(None, "tensor"),
            P(None, "tensor", None),
            P(None, "tensor"),
            P(None, "tensor", None),
            P(None, None, "tensor"),
            P(None, "tensor", "dp"),
            P(None, "dp", None, "tensor"),
            P(None, "tensor", "dp"),
        ),
        check_vma=False,
    )
```

```python
import functools

import jax
import jax.numpy as jnp
from jax import lax
from jax.experimental import pallas as pl
from jax.experimental.pallas import tpu as pltpu
from jax.sharding import PartitionSpec as P

KVH = 5
HEAD = 64
GQ = 5
CONV = 4
WINDOW = 1024
EPSILON = 1e-06
GROUP = 4
LANES = 128
F32 = jnp.float32
BF16 = jnp.bfloat16
NN = (((1,), (0,)), ((), ()))
NT = (((1,), (1,)), ((), ()))
TN = (((0,), (0,)), ((), ()))


def mm(left, right, dims=NN):
    return lax.dot_general(left, right, dims, preferred_element_type=F32)


def sigmoid(v):
    return 1.0 / (1.0 + jnp.exp(-v))


def softplus(v):
    return jnp.maximum(v, 0.0) + jnp.log(1.0 + jnp.exp(-jnp.abs(v)))


def params(megabytes=56):
    return pltpu.CompilerParams(vmem_limit_bytes=megabytes * 2**20)


def cost(micros):
    return pl.CostEstimate(flops=int(micros * 10**9), bytes_accessed=1, transcendentals=0)


def call(kernel, outs, args, micros, scratch=(), place=None, layers=()):
    vmem = pl.BlockSpec(memory_space=pltpu.VMEM)
    specs = []
    for k, a in enumerate(args):
        layer = layers[k] if k < len(layers) else None
        if layer is None:
            specs.append(vmem)
        else:
            at = (layer,) + (0,) * (a.ndim - 1)
            specs.append(pl.BlockSpec((None,) + a.shape[1:], lambda step, at=at: at))
    if place is not None:
        specs.insert(0, pl.BlockSpec(memory_space=pltpu.SMEM))
        args = [place] + list(args)
    return pl.pallas_call(
        kernel,
        out_shape=outs,
        grid=(1,) if layers else (),
        in_specs=specs,
        out_specs=[vmem] * len(outs),
        scratch_shapes=list(scratch),
        compiler_params=params(),
        cost_estimate=cost(micros),
    )(*args)


def call_into(kernel, layer, outs, before, args, place):
    vmem = pl.BlockSpec(memory_space=pltpu.VMEM)
    specs = [pl.BlockSpec(memory_space=pltpu.SMEM)] + [vmem] * len(args)
    out_specs = []
    for o in outs:
        at = (layer,) + (0,) * (len(o.shape) - 1)
        out_specs.append(pl.BlockSpec((None,) + o.shape[1:], lambda step, at=at: at))
    operands = [place] + list(args)
    aliases = {}
    if before is not None:
        aliases = {len(operands) + k: k for k in range(len(outs))}
        specs += [pl.BlockSpec(memory_space=pl.ANY)] * len(outs)
        operands += list(before)
    skip = len(aliases)

    def body(*refs):
        count = 1 + len(args)
        kernel(*refs[:count], *refs[count + skip :])

    return pl.pallas_call(
        body,
        out_shape=outs,
        grid=(1,),
        in_specs=specs,
        out_specs=out_specs,
        input_output_aliases=aliases,
        compiler_params=params(),
        cost_estimate=cost(4),
    )(*operands)


def out(shape, dtype):
    return jax.ShapeDtypeStruct(shape, dtype)


def widen(values, width):
    rows, have = values.shape
    if have == width:
        return values
    return jnp.concatenate([values, jnp.zeros((rows, width - have), values.dtype)], axis=1)


def shift_rows(values, amount, length):
    if amount == 0:
        return values
    rows = values.shape[0]
    place = lax.broadcasted_iota(jnp.int32, values.shape, 0) % length
    moved = pltpu.roll(values, amount % rows, 0)
    inside = place >= amount if amount > 0 else place < length + amount
    return jnp.where(inside, moved, 0.0)


def conv_pre(inner_x, taps, bias, length):
    running = bias
    for k in range(CONV):
        running = running + shift_rows(inner_x, CONV - 1 - k, length) * taps[k : k + 1]
    return running


def scores_of(queries, keys, length):
    scores = lax.dot_general(
        queries, keys, (((2,), (2,)), ((0,), (0,))), preferred_element_type=F32
    ) * HEAD ** (-0.5)
    shape = scores.shape
    query_pos = lax.broadcasted_iota(jnp.int32, shape, 1)
    key_pos = lax.broadcasted_iota(jnp.int32, shape, 2)
    allowed = (key_pos <= query_pos) & (key_pos > query_pos - WINDOW)
    scores = jnp.where(allowed, scores, -1e30)
    weights = jnp.exp(scores - jnp.max(scores, axis=-1, keepdims=True))
    return weights / jnp.sum(weights, axis=-1, keepdims=True)


class Mix:
    def __init__(self, chan):
        self.q = 0
        self.kv = 2 * HEAD
        self.o = 4 * HEAD
        self.s = 6 * HEAD
        self.x = self.s + chan
        self.z = self.x + chan
        self.end = self.z + chan


def swap(flag, first, second):
    return jnp.where(flag, second, first), jnp.where(flag, first, second)


def to_sequences(place, values):
    rows, columns = values.shape
    blocks = values.reshape(4, GROUP, rows // (4 * GROUP), columns)
    chip, core = place[2] == 1, place[3] == 1
    low, high = [], []
    for own in (0, 1):
        first, second = swap(chip, blocks[2 * own], blocks[2 * own + 1])
        low.append(first)
        high.append(second)
    parts = []
    for pair in (low, high):
        parts.append(jnp.stack(swap(core, pair[0], pair[1]), axis=1))
    return jnp.stack(parts, axis=1).reshape(rows, columns)


def to_blocks(place, values):
    rows, columns = values.shape
    parts = values.reshape(GROUP, 2, 2, rows // (4 * GROUP), columns)
    chip, core = place[2] == 1, place[3] == 1
    own, other = swap(core, parts[:, :, 0], parts[:, :, 1])
    blocks = []
    for half in (own, other):
        blocks.extend(swap(chip, half[:, 0], half[:, 1]))
    return jnp.concatenate([b.reshape(rows // 4, columns) for b in blocks], axis=0)


def rows_of(blocks):
    return jnp.concatenate([b[...] for b in blocks], axis=0)


def to_parts(parts, values):
    count = values.shape[0] // 4
    for k in range(4):
        parts[k][...] = values[k * count : (k + 1) * count].astype(BF16)


def mix_forward_kernel(cols, chan, wide, length, place, n0, n1, n2, n3, w, vec, scan_w, xi, z, conv, qkv, heads, proj, p0, p1, p2, p3):
    normed = rows_of((n0, n1, n2, n3))
    both = to_sequences(place, mm(normed, w[:, : cols.o]).astype(BF16))
    qkv[...] = both
    inner = to_sequences(place, mm(normed, w[:, cols.x :]))
    inner_x = widen(inner[:, :chan], wide)
    xi[...] = inner_x
    z[...] = widen(inner[:, chan:], wide)
    running = conv_pre(inner_x, vec[:CONV], vec[CONV : CONV + 1], length)
    conv_low = (running * sigmoid(running)).astype(BF16)
    conv[...] = conv_low
    proj[...] = mm(scan_w[...], conv_low, NT).astype(BF16)
    seqs = normed.shape[0] // length
    keys = both[:, cols.kv : cols.kv + HEAD].reshape(seqs, length, HEAD)
    values = both[:, cols.kv + HEAD : cols.o].reshape(seqs, length, HEAD)
    outs = []
    for h in range(2):
        queries = both[:, h * HEAD : (h + 1) * HEAD].reshape(seqs, length, HEAD)
        probs = scores_of(queries, keys, length).astype(BF16)
        mixed = lax.dot_general(
            probs, values, (((2,), (1,)), ((0,), (0,))), preferred_element_type=F32
        )
        outs.append(mixed.reshape(seqs * length, HEAD))
    heads_out = to_blocks(place, jnp.concatenate(outs, axis=1).astype(BF16))
    heads[...] = heads_out
    to_parts((p0, p1, p2, p3), mm(heads_out, w[:, cols.o : cols.s], NT))


def spread(state, wide):
    row = lax.broadcasted_iota(jnp.int32, (state, wide), 0)
    col = lax.broadcasted_iota(jnp.int32, (state, wide), 1) // LANES
    return (row == col).astype(BF16)


def lane(n):
    return slice(n * LANES, (n + 1) * LANES)


def tiles_in(ref, values):
    for n in range(ref.shape[0]):
        ref[n] = values[:, lane(n)]


def tiles_out(ref):
    return jnp.concatenate([ref[n] for n in range(ref.shape[0])], axis=1)


LOG2E = 1.4426950408889634
STATES_AT_ONCE = 8


def time_major(rows, length):
    seqs = rows // length
    came = lax.broadcasted_iota(jnp.int32, (rows, rows), 0)
    goes = lax.broadcasted_iota(jnp.int32, (rows, rows), 1)
    return (came == (goes % seqs) * length + goes // seqs).astype(BF16)


def scan_setup(rank, state, seqs, length, proj, conv, step_w, step_b, dlog, dt_s, dtx_s, drive_s, read_s, rate_s):
    pre = mm(proj[:rank], step_w[...], TN) + step_b
    dt = softplus(pre)
    tiles_in(dt_s, dt)
    tiles_in(dtx_s, dt * conv)
    table = spread(state, state * LANES)
    order = time_major(seqs * length, length)
    maps = mm(proj[rank:], order).astype(BF16)
    drive = mm(maps[:state], table, TN)
    read = mm(maps[state:], table, TN)
    for n in range(state):
        drive_s[:, n] = drive[:, lane(n)].reshape(length, seqs, LANES)
        read_s[:, n] = read[:, lane(n)].reshape(length, seqs, LANES)
    rates = -LOG2E * jnp.exp(dlog[...])
    for n in range(state):
        rate_s[n] = jnp.broadcast_to(rates[n : n + 1], (seqs, rates.shape[1]))
    return pre


def scan_forward_loop(first, tiles, seqs, length, dt_s, dtx_s, drive_s, read_s, rate_s, y_s, keep_s):
    def step(t, held):
        rows = pl.ds(t, seqs, stride=length)
        dt = [dt_s[i, rows] for i in range(tiles)]
        dtx = [dtx_s[i, rows] for i in range(tiles)]
        total = [y_s[i, rows] if first else jnp.zeros_like(dt[i]) for i in range(tiles)]
        fresh = []
        for j in range(STATES_AT_ONCE):
            n = first + j
            drive = drive_s[t, n]
            read = read_s[t, n]
            for i in range(tiles):
                decay = jnp.exp2(dt[i] * rate_s[n, :, lane(i)])
                now = decay * held[j * tiles + i] + dtx[i] * drive
                total[i] = total[i] + now * read
                if keep_s is not None:
                    keep_s[t, j * tiles + i] = now
                fresh.append(now)
        for i in range(tiles):
            y_s[i, rows] = total[i]
        return tuple(fresh)

    zero = jnp.zeros((seqs, LANES), F32)
    lax.fori_loop(0, length, step, (zero,) * (STATES_AT_ONCE * tiles))


def scan_forward_kernel(cols, chan, wide, rank, state, seqs, length, place, proj, conv, z, step_w, vec, dlog, w, gated, p0, p1, p2, p3, dt_s, dtx_s, drive_s, read_s, rate_s, y_s):
    conv32 = conv[...].astype(F32)
    step_b, skip = vec[CONV + 1 : CONV + 2], vec[CONV + 2 : CONV + 3]
    scan_setup(rank, state, seqs, length, proj, conv32, step_w, step_b, dlog, dt_s, dtx_s, drive_s, read_s, rate_s)
    for first in range(0, state, STATES_AT_ONCE):
        scan_forward_loop(first, wide // LANES, seqs, length, dt_s, dtx_s, drive_s, read_s, rate_s, y_s, None)
    gate = z[...]
    low = ((tiles_out(y_s) + skip * conv32) * (gate * sigmoid(gate))).astype(BF16)
    low = to_blocks(place, low)
    gated[...] = low
    to_parts((p0, p1, p2, p3), mm(low[:, :chan], w[:, cols.s : cols.x], NT))


def split_sum(table, values):
    high = values.astype(BF16)
    rest = (values - high.astype(F32)).astype(BF16)
    return mm(table, high, NT) + mm(table, rest, NT)


def scan_backward_loop(first, tiles, seqs, length, dt_s, dtx_s, drive_s, read_s, rate_s, keep_s, ds_s, ddt_s, dsrc_s, pd_s, pr_s):
    count = STATES_AT_ONCE * tiles

    def step(back, carry):
        t = length - 1 - back
        rows = pl.ds(t, seqs, stride=length)
        dt = [dt_s[i, rows] for i in range(tiles)]
        dtx = [dtx_s[i, rows] for i in range(tiles)]
        ds = [ds_s[i, rows] for i in range(tiles)]
        zero = jnp.zeros_like(dt[0])
        d_src = [dsrc_s[i, rows] if first else zero for i in range(tiles)]
        d_dt = [ddt_s[i, rows] if first else zero for i in range(tiles)]
        lams = []
        sums = []
        for j in range(STATES_AT_ONCE):
            n = first + j
            drive = drive_s[t, n]
            read = read_s[t, n]
            of_read = zero
            of_drive = zero
            for i in range(tiles):
                k = j * tiles + i
                rate = rate_s[n, :, lane(i)]
                kept = keep_s[t, k]
                lam = carry[k] + read * ds[i]
                of_read = of_read + kept * ds[i]
                of_drive = of_drive + lam * dtx[i]
                d_src[i] = d_src[i] + lam * drive
                d_log = lam * (kept - dtx[i] * drive)
                d_dt[i] = d_dt[i] + d_log * rate
                sums.append(carry[count + k] + d_log * dt[i])
                lams.append(jnp.exp2(dt[i] * rate) * lam)
            pr_s[t, n] = of_read
            pd_s[t, n] = of_drive
        for i in range(tiles):
            dsrc_s[i, rows] = d_src[i]
            ddt_s[i, rows] = d_dt[i]
        return tuple(lams) + tuple(sums)

    zero = jnp.zeros((seqs, LANES), F32)
    return lax.fori_loop(0, length, step, (zero,) * (2 * count))[count:]


def scan_backward_kernel(cols, chan, wide, rank, state, seqs, length, place, g0, g1, g2, g3, proj, conv, z, step_w, vec, dlog, w, d_proj, d_conv, d_z, small, d_step_w, dt_s, dtx_s, drive_s, read_s, rate_s, y_s, keep_s, ds_s, ddt_s, dsrc_s, pd_s, pr_s):
    tiles = wide // LANES
    conv32 = conv[...].astype(F32)
    step_b, skip = vec[CONV + 1 : CONV + 2], vec[CONV + 2 : CONV + 3]
    pre = scan_setup(rank, state, seqs, length, proj, conv32, step_w, step_b, dlog, dt_s, dtx_s, drive_s, read_s, rate_s)
    d_gated = to_sequences(place, mm(rows_of((g0, g1, g2, g3)), w[:, cols.s : cols.x]))
    d_gated = widen(d_gated, wide)
    gate = z[...]
    sig = sigmoid(gate)
    d_scanned = d_gated * (gate * sig)
    tiles_in(ds_s, d_scanned)
    d_rates = []
    for first in range(0, state, STATES_AT_ONCE):
        scan_forward_loop(first, tiles, seqs, length, dt_s, dtx_s, drive_s, read_s, rate_s, y_s, keep_s)
        sums = scan_backward_loop(first, tiles, seqs, length, dt_s, dtx_s, drive_s, read_s, rate_s, keep_s, ds_s, ddt_s, dsrc_s, pd_s, pr_s)
        for j in range(STATES_AT_ONCE):
            d_rates.append(
                jnp.concatenate(
                    [jnp.sum(sums[j * tiles + i], axis=0, keepdims=True) for i in range(tiles)],
                    axis=1,
                )
            )
    d_src = tiles_out(dsrc_s)
    dt = tiles_out(dt_s)
    d_dt = tiles_out(ddt_s) * (1.0 / LOG2E) + d_src * conv32
    d_conv[...] = skip * d_scanned + d_src * dt
    scanned = tiles_out(y_s) + skip * conv32
    d_z[...] = (d_gated * scanned * (sig * (1.0 + gate * (1.0 - sig)))).astype(BF16)
    d_pre = d_dt * sigmoid(pre)
    rates = -jnp.exp(dlog[...])
    small[0:1] = jnp.sum(d_pre, axis=0, keepdims=True)
    small[1:2] = jnp.sum(d_scanned * conv32, axis=0, keepdims=True)
    small[2:8] = jnp.zeros((6, wide), F32)
    small[8:] = jnp.concatenate(d_rates, axis=0) * rates
    low = d_pre.astype(BF16)
    d_step_w[...] = mm(proj[:rank], low)
    table = spread(state, state * LANES)
    tokens = seqs * length
    by_time = [
        jnp.concatenate([ref[:, n].reshape(tokens, LANES) for n in range(state)], axis=1)
        for ref in (pd_s, pr_s)
    ]
    d_maps = jnp.concatenate([split_sum(table, values) for values in by_time], axis=0)
    order = time_major(tokens, length)
    d_proj[:rank] = mm(step_w[...], low, NT).astype(BF16)
    d_proj[rank:] = mm(d_maps.astype(BF16), order, NT).astype(BF16)


def attend_backward_kernel(cols, length, place, g0, g1, g2, g3, w, qkv, d_qkv):
    d_heads = mm(rows_of((g0, g1, g2, g3)), w[:, cols.o : cols.s]).astype(BF16)
    d_heads = to_sequences(place, d_heads)
    both = qkv[...]
    seqs = both.shape[0] // length
    keys = both[:, cols.kv : cols.kv + HEAD].reshape(seqs, length, HEAD)
    values = both[:, cols.kv + HEAD : cols.o].reshape(seqs, length, HEAD)
    parts = []
    d_keys = 0.0
    d_values = 0.0
    for h in range(2):
        queries = both[:, h * HEAD : (h + 1) * HEAD].reshape(seqs, length, HEAD)
        d_out = d_heads[:, h * HEAD : (h + 1) * HEAD].reshape(seqs, length, HEAD)
        probs = scores_of(queries, keys, length)
        d_probs = lax.dot_general(
            d_out, values, (((2,), (2,)), ((0,), (0,))), preferred_element_type=F32
        )
        d_scores = (
            probs
            * (d_probs - jnp.sum(d_probs * probs, axis=-1, keepdims=True))
            * HEAD ** (-0.5)
        ).astype(BF16)
        d_query = lax.dot_general(
            d_scores, keys, (((2,), (1,)), ((0,), (0,))), preferred_element_type=F32
        )
        parts.append(d_query.reshape(seqs * length, HEAD))
        d_keys = d_keys + lax.dot_general(
            d_scores, queries, (((1,), (1,)), ((0,), (0,))), preferred_element_type=F32
        )
        d_values = d_values + lax.dot_general(
            probs.astype(BF16), d_out, (((1,), (1,)), ((0,), (0,))), preferred_element_type=F32
        )
    parts.append(d_keys.reshape(seqs * length, HEAD))
    parts.append(d_values.reshape(seqs * length, HEAD))
    d_qkv[...] = jnp.concatenate(parts, axis=1).astype(BF16)


def mix_backward_kernel(cols, chan, length, place, proj, conv, xi, d_conv, d_z, d_qkv, w, vec, scan_w, d_x, p0, p1, p2, p3, d_scan_w, small):
    taps, bias = vec[:CONV], vec[CONV : CONV + 1]
    d_out = d_conv[...] + mm(proj[...], scan_w[...], TN)
    inner_x = xi[...]
    running = conv_pre(inner_x, taps, bias, length)
    sig = sigmoid(running)
    d_run = d_out * (sig * (1.0 + running * (1.0 - sig)))
    d_in = 0.0
    for k in range(CONV):
        back = CONV - 1 - k
        d_in = d_in + shift_rows(d_run, -back, length) * taps[k : k + 1]
        small[k : k + 1] = jnp.sum(d_run * shift_rows(inner_x, back, length), axis=0, keepdims=True)
    small[CONV : CONV + 1] = jnp.sum(d_run, axis=0, keepdims=True)
    small[CONV + 1 :] = jnp.zeros((8 - CONV - 1, inner_x.shape[1]), F32)
    low = d_in.astype(BF16)
    d_x[...] = low
    inner = to_blocks(place, jnp.concatenate([low[:, :chan], d_z[:, :chan]], axis=1))
    heads = to_blocks(place, d_qkv[...])
    to_parts((p0, p1, p2, p3), mm(inner, w[:, cols.x :], NT) + mm(heads, w[:, : cols.o], NT))
    d_scan_w[...] = mm(proj[...], conv[...])


def mix_weights_kernel(cols, chan, place, n0, n1, n2, n3, a0, a1, a2, a3, s0, s1, s2, s3, d_qkv, heads, gated, d_x, d_z, keep, rest):
    normed = rows_of((n0, n1, n2, n3))
    inner = jnp.concatenate([d_x[:, :chan], d_z[:, :chan]], axis=1)
    to_shares(place, keep, rest, 0, mm(normed, to_blocks(place, d_qkv[...]), TN))
    to_shares(place, keep, rest, cols.o, mm(rows_of((a0, a1, a2, a3)), heads[...], TN))
    to_shares(place, keep, rest, cols.s, mm(rows_of((s0, s1, s2, s3)), gated[:, :chan], TN))
    to_shares(place, keep, rest, cols.x, mm(normed, to_blocks(place, inner), TN))


def picker(rows, columns, start, valid):
    row = lax.broadcasted_iota(jnp.int32, (rows, columns), 0)
    col = lax.broadcasted_iota(jnp.int32, (rows, columns), 1)
    return ((row == start + col) & (col < valid)).astype(BF16)


def pack_mix_kernel(cols, chan, tensor_size, place, q, key, value, o, x, z, ssm, *packed):
    tensor_idx = place[1]
    for slow_idx in range(GROUP):

        @pl.when(place[0] == slow_idx)
        def _():
            for by in range(GROUP):
                s = (slow_idx + by) % GROUP
                unit = s * tensor_size + tensor_idx
                group = lax.div(unit, 3)
                sub = lax.rem(unit, 3)
                valid = jnp.where(group >= KVH, 0, jnp.where(sub == 2, HEAD, 2 * HEAD))
                heads = picker(q.shape[1], 2 * HEAD, group * GQ * HEAD + sub * 2 * HEAD, valid)
                both = picker(key.shape[1], HEAD, jnp.minimum(group, KVH - 1) * HEAD, HEAD)
                mine = slice(s * chan, (s + 1) * chan)
                packed[by][:, : cols.kv] = mm(q[...], heads).astype(BF16)
                packed[by][:, cols.kv : cols.o] = jnp.concatenate(
                    [mm(key[...], both), mm(value[...], both)], axis=1
                ).astype(BF16)
                packed[by][:, cols.o : cols.s] = mm(o[...], heads).astype(BF16)
                packed[by][:, cols.s : cols.x] = ssm[:, mine]
                packed[by][:, cols.x : cols.z] = x[:, mine]
                packed[by][:, cols.z :] = z[:, mine]


def pack_ffn_kernel(units, place, gate, up, down, *packed):
    for slow_idx in range(GROUP):

        @pl.when(place[0] == slow_idx)
        def _():
            for by in range(GROUP):
                s = (slow_idx + by) % GROUP
                mine = slice(s * units, (s + 1) * units)
                packed[by][:, :units] = gate[:, mine]
                packed[by][:, units : 2 * units] = up[:, mine]
                packed[by][:, 2 * units :] = down[:, mine]


def to_shares(place, keep, rest, start, values):
    share = keep.shape[1]
    fast = rest.shape[0] + 1
    values = values.astype(BF16)
    columns = slice(start, start + values.shape[1])
    for s in range(GROUP):
        by = lax.rem(s - place[0] + GROUP, GROUP)
        for f in range(fast):
            at = (s * fast + f) * share
            rows = values[at : at + share]
            turn = lax.rem(f - place[4] + fast, fast)

            @pl.when(turn == 0)
            def _():
                keep[by, :, columns] = rows

            @pl.when(turn > 0)
            def _():
                rest[turn - 1, by, :, columns] = rows


def unpack_mix_kernel(cols, chan, tensor_size, place, pieces, every, d_q, d_kv, d_o, d_ssm, d_in):
    slow_idx = place[0]

    def came(s):
        return lax.rem(slow_idx - s + GROUP, GROUP)

    for s in range(GROUP):
        mine = slice(s * chan, (s + 1) * chan)
        d_ssm[:, mine] = pieces[came(s), :, cols.s : cols.x].astype(F32)
        d_in[:, 0, mine] = pieces[came(s), :, cols.x : cols.z].astype(F32)
        d_in[:, 1, mine] = pieces[came(s), :, cols.z :].astype(F32)
    for group in range(KVH):
        total = 0.0
        for sub in range(3):
            unit = 3 * group + sub
            s, t = unit // tensor_size, unit % tensor_size
            piece = every[t, came(s)].astype(F32)
            start = group * GQ * HEAD + sub * 2 * HEAD
            width = HEAD if sub == 2 else 2 * HEAD
            d_q[:, start : start + width] = piece[:, :width]
            d_o[:, start : start + width] = piece[:, cols.o : cols.o + width]
            total = total + piece[:, cols.kv : cols.o]
        d_kv[:, 0, group * HEAD : (group + 1) * HEAD] = total[:, :HEAD]
        d_kv[:, 1, group * HEAD : (group + 1) * HEAD] = total[:, HEAD:]


def unpack_columns_kernel(width, place, pieces, pair, *single):
    slow_idx = place[0]
    for s in range(GROUP):
        came = lax.rem(slow_idx - s + GROUP, GROUP)
        mine = slice(s * width, (s + 1) * width)
        for k in range(2):
            pair[:, k, mine] = pieces[came, :, k * width : (k + 1) * width].astype(F32)
        for ref in single:
            ref[:, mine] = pieces[came, :, 2 * width :].astype(F32)


def small_weights_kernel(chan, wide, rank, place, conv_w, conv_b, step_b, dlog, skip, scan_w, step_w, vec, dlog_out, scan_out, step_out):
    layers = vec.shape[0]
    low = scan_w.shape[0] - 2 * dlog.shape[1]
    vec[...] = jnp.zeros(vec.shape, F32)
    dlog_out[...] = jnp.zeros(dlog_out.shape, F32)
    scan_out[...] = jnp.zeros(scan_out.shape, BF16)
    step_out[...] = jnp.zeros(step_out.shape, BF16)
    for s in range(GROUP):

        @pl.when(place[0] == s)
        def _():
            mine = slice(s * chan, (s + 1) * chan)
            for layer in range(layers):
                vec[layer, :CONV, :chan] = conv_w[layer, :, mine]
                vec[layer, CONV : CONV + 1, :chan] = conv_b[layer : layer + 1, mine]
                vec[layer, CONV + 1 : CONV + 2, :chan] = step_b[layer : layer + 1, mine]
                vec[layer, CONV + 2 : CONV + 3, :chan] = skip[layer : layer + 1, mine]
                dlog_out[layer, :, :chan] = dlog[layer, :, mine]
                scan_out[layer, :low, :chan] = scan_w[:low, layer, mine]
                scan_out[layer, rank:, :chan] = scan_w[low:, layer, mine]
                step_out[layer, :low, :chan] = step_w[:, layer, mine]


def ffn_forward_kernel(units, f0, f1, f2, f3, w, hidden, p0, p1, p2, p3):
    both = mm(rows_of((f0, f1, f2, f3)), w[:, : 2 * units])
    hidden[...] = both
    gate = both[:, :units]
    activ = (gate * sigmoid(gate) * both[:, units:]).astype(BF16)
    to_parts((p0, p1, p2, p3), mm(activ, w[:, 2 * units :], NT))


def ffn_backward_kernel(units, d0, d1, d2, d3, hidden, w, d_hidden, activ, p0, p1, p2, p3):
    d_activ = mm(rows_of((d0, d1, d2, d3)), w[:, 2 * units :])
    gate = hidden[:, :units]
    up = hidden[:, units:]
    sig = sigmoid(gate)
    swish = gate * sig
    activ[...] = (swish * up).astype(BF16)
    low = jnp.concatenate(
        [d_activ * up * (sig * (1.0 + gate * (1.0 - sig))), d_activ * swish], axis=1
    ).astype(BF16)
    d_hidden[...] = low
    to_parts((p0, p1, p2, p3), mm(low, w[:, : 2 * units], NT))


def ffn_weights_kernel(units, place, f0, f1, f2, f3, d0, d1, d2, d3, d_hidden, activ, keep, rest):
    to_shares(place, keep, rest, 0, mm(rows_of((f0, f1, f2, f3)), d_hidden[...], TN))
    to_shares(place, keep, rest, 2 * units, mm(rows_of((d0, d1, d2, d3)), activ[...], TN))


def rms_scale(values, gain_vec):
    return (
        values * lax.rsqrt(jnp.mean(values * values, axis=-1, keepdims=True) + EPSILON) * gain_vec
    )


def mix_branches(resid_in, attn_out, ssm_out, gain_attn, gain_ssm, gain_ffn):
    residual = resid_in + 0.5 * (rms_scale(attn_out, gain_attn) + rms_scale(ssm_out, gain_ssm))
    return (residual, rms_scale(residual, gain_ffn))


def per_device(
    dp_size,
    tensor_size,
    hidden_in,
    out_grad,
    lengths,
    norm_gains,
    q_weight,
    kv_weight,
    o_weight,
    in_weight,
    conv_weight,
    conv_bias,
    step_bias,
    decay_log,
    skip_gain,
    scan_weight,
    step_weight,
    ssm_weight,
    gate_weight,
    down_weight,
):
    layers = q_weight.shape[0]
    batches, _, length, width = hidden_in.shape
    fast = dp_size // GROUP
    share = width // dp_size
    chan = in_weight.shape[3] // GROUP
    wide = -(-chan // LANES) * LANES
    units = gate_weight.shape[3] // GROUP
    rank_true = step_weight.shape[1]
    state = decay_log.shape[2]
    rank = -(-rank_true // 16) * 16
    proj_rows = rank + 2 * state
    cols = Mix(chan)
    ffn_cols = 3 * units
    dp_idx = lax.axis_index("dp")
    slow_idx = dp_idx // fast
    fast_idx = dp_idx % fast
    tensor_idx = lax.axis_index("tensor")
    rows_here = batches * length // tensor_size
    seqs = GROUP * batches
    tokens = seqs * length
    half = tensor_size // 2

    def slow_perm(by):
        return [
            (s * fast + f, ((s + by) % GROUP) * fast + f) for s in range(GROUP) for f in range(fast)
        ]

    def fast_perm(by):
        return [
            (s * fast + f, s * fast + (f + by) % fast) for s in range(GROUP) for f in range(fast)
        ]

    core_perm = [(t, t ^ 1) for t in range(tensor_size)]
    chip_perm = [(t, t ^ 2) for t in range(tensor_size)]
    core_idx = tensor_idx % 2
    chip_idx = tensor_idx // 2

    def slow(values, by):
        return lax.ppermute(values, "dp", slow_perm(by)) if by % GROUP else values

    def other_fast(values, by):
        return lax.ppermute(values, "dp", fast_perm(by)) if by % fast else values

    def add_low(*terms):
        total = terms[0].astype(F32)
        for term in terms[1:]:
            total = total + term.astype(F32)
        return total.astype(BF16)

    def after(values, *earlier):
        return lax.optimization_barrier((values,) + earlier)[0] if earlier else values

    def gather_tokens(own):
        mine = jnp.concatenate([slow(own, by) for by in range(GROUP)], axis=0)
        chip = lax.ppermute(mine, "tensor", chip_perm)
        core = lax.ppermute(mine, "tensor", core_perm)
        return [mine, chip, core, lax.ppermute(chip, "tensor", core_perm)]

    def joined(values, done):
        values, done = tuple(values), tuple(done)
        return list(lax.optimization_barrier(values + done)[: len(values)]) if done else list(values)

    def scatter_near(parts):
        far = add_low(parts[1], lax.ppermute(parts[3], "tensor", core_perm))
        near = add_low(parts[0], lax.ppermute(parts[2], "tensor", core_perm))
        return add_low(near, lax.ppermute(far, "tensor", chip_perm))

    def scatter_far(total):
        total = total.reshape(GROUP, rows_here, width)
        result = total[0].astype(F32)
        for by in range(1, GROUP):
            result = result + slow(total[by], GROUP - by).astype(F32)
        return result

    def sum_group(values):
        values = add_low(values, lax.ppermute(values, "tensor", core_perm))
        values = add_low(values, lax.ppermute(values, "tensor", chip_perm))
        chunk = tokens // GROUP
        parts = [values[:, k * chunk : (k + 1) * chunk] for k in range(GROUP)]
        total = add_low(parts[0], *[slow(parts[by], GROUP - by) for by in range(1, GROUP)])
        return jnp.concatenate([slow(total, by) for by in range(GROUP)], axis=1)

    place = jnp.stack([slow_idx, tensor_idx, chip_idx, core_idx, fast_idx]).astype(jnp.int32)

    middle = share // 16 * 8
    one, three, two = (1, 0, share), (3, 0, share), (2, 0, share)
    two_a, two_b = (2, 0, middle), (2, middle, share)

    def send(pieces, unit, *ties):
        by, low, high = unit
        return slow(after(pieces[by][low:high], *ties), by)

    class Fetched:
        def __init__(self, own):
            self.full = jnp.zeros((GROUP, fast, share, own.shape[1]), BF16)
            self.add((0, 0, share), own)

        def add(self, unit, piece):
            by, low, _ = unit
            for turn in range(fast):
                self.full = lax.dynamic_update_slice(
                    self.full,
                    other_fast(piece, turn)[None, None],
                    ((slow_idx - by) % GROUP, (fast_idx - turn) % fast, low, 0),
                )

        def whole(self):
            return self.full.reshape(width, self.full.shape[3])

    def rows_round(own, units_in, tie):
        columns = own.shape[1]
        half = jnp.zeros((GROUP, share, columns), BF16)
        for (by, low, _), piece in [((0, 0, share), own)] + list(units_in.items()):
            half = lax.dynamic_update_slice(half, piece[None], ((slow_idx - by) % GROUP, low, 0))
        moved = [half] + [other_fast(half, turn) for turn in range(1, fast)]
        moved = joined(moved, [tie])
        if fast == 2:
            first, second = moved
            full = jnp.where(
                fast_idx == 0, jnp.stack([first, second], 1), jnp.stack([second, first], 1)
            )
        else:
            full = jnp.zeros((GROUP, fast, share, columns), BF16)
            for turn, rows in enumerate(moved):
                full = lax.dynamic_update_slice(
                    full, rows[:, None], (0, (fast_idx - turn) % fast, 0, 0)
                )
        return full.reshape(width, columns)

    def shares_out(columns):
        return [
            out((GROUP, share, columns), BF16),
            out((fast - 1, GROUP, share, columns), BF16),
        ]

    def settle_fast(keep, rest):
        return add_low(keep, *[other_fast(rest[turn - 1], turn) for turn in range(1, fast)])

    def stacked(rows, units_in, tie):
        two_rows = units_in[two] if two in units_in else None
        if two_rows is None:
            two_rows = jnp.concatenate([units_in[two_a], units_in[two_b]], axis=0)
        pieces = [rows[0], units_in[one], two_rows, units_in[three]]
        return jnp.stack(joined(pieces, [] if tie is None else [tie]))

    o_turned = o_weight.swapaxes(1, 2)
    ssm_turned = ssm_weight.swapaxes(1, 2)
    down_turned = down_weight.swapaxes(1, 2)

    def pack_mix(layer, place):
        inner = in_weight[layer]
        both = kv_weight[layer]
        packed = call(
            functools.partial(pack_mix_kernel, cols, chan, tensor_size),
            [out((share, cols.end), BF16)] * GROUP,
            [q_weight, both[:, 0], both[:, 1], o_turned, inner[:, 0], inner[:, 1], ssm_turned],
            5,
            place=place,
            layers=(layer, None, None, layer, None, None, layer),
        )
        return packed

    def pack_ffn(layer, place):
        gate = gate_weight[layer]
        packed = call(
            functools.partial(pack_ffn_kernel, units),
            [out((share, ffn_cols), BF16)] * GROUP,
            [gate[:, 0], gate[:, 1], down_turned],
            3,
            place=place,
            layers=(None, None, layer),
        )
        return packed

    vecs, dlogs, scan_mats, step_mats = call(
        functools.partial(small_weights_kernel, chan, wide, rank),
        [
            out((layers, 8, wide), F32),
            out((layers, state, wide), F32),
            out((layers, proj_rows, wide), BF16),
            out((layers, rank, wide), BF16),
        ],
        [
            conv_weight,
            conv_bias,
            step_bias,
            decay_log.swapaxes(1, 2),
            skip_gain,
            scan_weight.transpose(2, 0, 1),
            step_weight.swapaxes(0, 1),
        ],
        2,
        place=place,
    )

    bf_rows = lambda columns: out((tokens, columns), BF16)
    f_rows = lambda columns: out((tokens, columns), F32)
    tiled = pltpu.VMEM((wide // LANES, tokens, LANES), F32)
    state_tiled = pltpu.VMEM((length, state, seqs, LANES), F32)
    scan_scratch = [
        tiled,
        tiled,
        state_tiled,
        state_tiled,
        pltpu.VMEM((state, seqs, wide), F32),
        tiled,
    ]

    def own_rows(values):
        flat = values.reshape(batches * length, width)
        return lax.dynamic_slice_in_dim(flat, tensor_idx * rows_here, rows_here, 0)

    part_outs = [out((tokens // 4, width), BF16)] * 4
    token = tensor_idx * rows_here + jnp.arange(rows_here)
    mask = (token % length < lengths[token // length, 0]).astype(F32)[:, None]
    grad_run = own_rows(out_grad).astype(F32) * mask
    part_outs = [out((tokens // 4, width), BF16)] * 4
    running = own_rows(hidden_in).astype(F32)
    kept = []
    fetched = []
    own = pack_mix(0, place)
    first = {unit: send(own, unit) for unit in (one, three)}
    first[two] = send(own, two, first[one])
    mix_packed = [own]
    ffn_packed = [pack_ffn(0, after(place, first[one]))]
    for layer in range(layers):
        final = layer + 1 == layers
        gains = norm_gains[layer]
        normed, pull_input = jax.vjp(rms_scale, running, gains[0])
        normed = normed.astype(BF16)
        ffn_own, ffn_in_units = ffn_packed[layer], {}
        if layer == 0:
            mix_got = Fetched(own[0])
            for unit, piece in first.items():
                mix_got.add(unit, piece)
            n = gather_tokens(after(normed, own[0]))
            mix_w = after(mix_got.whole(), ffn_own[0])
            with_first, with_scan = (one, three), (two,)
        else:
            n = gather_tokens(normed)
            ffn_in_units[one] = send(ffn_own, one, n[0])
            mix_w = after(mix_got.whole(), ffn_in_units[one])
            with_first, with_scan = (three,), (two,)
        ready = joined(n, [mix_w])
        for unit in with_first:
            ffn_in_units[unit] = send(ffn_own, unit, first[two] if layer == 0 else ready[0])
        xi, z, conv, qkv, heads, proj_part, *attn_parts = call(
            functools.partial(mix_forward_kernel, cols, chan, wide, length),
            [
                f_rows(wide),
                f_rows(wide),
                bf_rows(wide),
                bf_rows(cols.o),
                bf_rows(2 * HEAD),
                out((proj_rows, tokens), BF16),
            ]
            + part_outs,
            ready + [mix_w, vecs, scan_mats],
            7,
            place=place,
            layers=(None,) * 5 + (layer, layer),
        )
        proj_part = after(proj_part, *[ffn_in_units[unit] for unit in with_first])
        proj = sum_group(proj_part)
        if not final:
            mix_packed.append(pack_mix(layer + 1, after(place, proj_part)))
            ffn_packed.append(pack_ffn(layer + 1, after(place, proj_part)))
            proj = after(proj, mix_packed[-1][0], ffn_packed[-1][0])
        for unit in with_scan:
            ffn_in_units[unit] = send(ffn_own, unit, proj)
        attn_total = scatter_near(joined(attn_parts, [proj]))
        gated, *ssm_parts = call(
            functools.partial(
                scan_forward_kernel, cols, chan, wide, rank, state, seqs, length
            ),
            [bf_rows(wide)] + part_outs,
            [proj, conv, z, step_mats, vecs, dlogs, mix_w],
            11,
            scan_scratch,
            place=place,
            layers=(None,) * 3 + (layer,) * 3,
        )
        done = [ffn_in_units[unit] for unit in with_scan]
        ssm_parts = joined(ssm_parts, [attn_total] + done)
        attn_out = scatter_far(after(attn_total, ssm_parts[0]))
        ssm_out = scatter_far(scatter_near(ssm_parts))
        (residual, ffn_in), pull_mix = jax.vjp(
            mix_branches, running, attn_out, ssm_out, gains[1], gains[2], gains[3]
        )
        ffn_in = ffn_in.astype(BF16)
        f = gather_tokens(ffn_in)
        ffn_w = rows_round(ffn_own[0], ffn_in_units, ffn_in)
        fetched.append((mix_w, ffn_w))
        if final:
            d_out = gather_tokens(after(grad_run.astype(BF16), f[0]))
            ffn_w = after(ffn_w, d_out[0])
        else:
            own = mix_packed[layer + 1]
            mix_got = Fetched(own[0])
            unit_two = send(own, two, f[0])
            ffn_w = after(ffn_w, unit_two)
            mix_got.add(two, unit_two)
        ready = joined(f, [ffn_w])
        if not final:
            unit_one = send(own, one, ready[0])
        hidden, *ffn_parts = call(
            functools.partial(ffn_forward_kernel, units),
            [f_rows(2 * units)] + part_outs,
            ready + [ffn_w],
            7,
        )
        if not final:
            ffn_parts = joined(ffn_parts, [unit_one])
            mix_got.add(one, unit_one)
            unit_three = send(own, three, ffn_parts[0])
            total = after(scatter_near(ffn_parts), unit_three)
            mix_got.add(three, unit_three)
            running = residual + scatter_far(total)
        kept.append((n, pull_input, xi, z, conv, qkv, heads, proj, gated, pull_mix, f, hidden))

    def every_tensor(values):
        moved = lax.ppermute(values, "tensor", chip_perm)
        values = jnp.where(chip_idx == 0, jnp.stack([values, moved]), jnp.stack([moved, values]))
        moved = lax.ppermute(values, "tensor", core_perm)
        values = jnp.where(
            core_idx == 0, jnp.stack([values, moved], 1), jnp.stack([moved, values], 1)
        )
        return values.reshape((tensor_size,) + values.shape[2:])

    def every_fast(values):
        turned = jnp.stack([other_fast(values, turn) for turn in range(fast)])
        return [
            lax.dynamic_index_in_dim(turned, (fast_idx - source) % fast, 0, False)
            for source in range(fast)
        ]

    def every_slow(values):
        turned = jnp.stack([slow(values, by) for by in range(GROUP)])
        return [
            lax.dynamic_index_in_dim(turned, (slow_idx - source) % GROUP, 0, False)
            for source in range(GROUP)
        ]

    def rounded(values):
        return lax.optimization_barrier(values.astype(BF16))

    def all_rows(own, *ties):
        return every_tensor(after(rounded(own), *ties)).reshape(batches, 1, length, width)

    big = {"mix": None, "ffn": None}
    small_rows = []
    gain_grads = [None] * layers
    early_rows = late_rows = None

    def finish_mix(layer, rows, units_in, tie):
        pieces = stacked(rows, units_in, tie)
        every = every_tensor(pieces[:, :, : cols.s])
        big["mix"] = call_into(
            functools.partial(unpack_mix_kernel, cols, chan, tensor_size),
            layer,
            [
                out((layers, share, KVH * GQ * HEAD), F32),
                out((layers, share, 2, KVH * HEAD), F32),
                out((layers, share, KVH * GQ * HEAD), F32),
                out((layers, share, GROUP * chan), F32),
                out((layers, share, 2, GROUP * chan), F32),
            ],
            big["mix"],
            [pieces, every],
            place,
        )

    def finish_ffn(layer, rows, units_in, tie):
        big["ffn"] = call_into(
            functools.partial(unpack_columns_kernel, units),
            layer,
            [
                out((layers, share, 2, GROUP * units), F32),
                out((layers, share, GROUP * units), F32),
            ],
            big["ffn"],
            [stacked(rows, units_in, tie)],
            place,
        )

    def finish_small(rows):
        small = rounded(sum(p.astype(F32) for p in every_fast(rounded(rows))))
        return jnp.concatenate(every_slow(small), axis=2).astype(F32)

    above = None
    for layer in reversed(range(layers)):
        mix_w, ffn_w = fetched[layer]
        n, pull_input, xi, z, conv, qkv, heads, proj, gated, pull_mix, f, hidden = kept[layer]
        if above is not None:
            d_out = gather_tokens(grad_run.astype(BF16))
            mix_rows, ffn_above, ffn_above_units = above
            mix_units = {one: send(mix_rows, one, d_out[0])}
            ffn_w = after(ffn_w, mix_units[one])
        ready = joined(d_out, [ffn_w])
        if above is not None:
            mix_units[three] = send(mix_rows, three, ready[0])
        d_hidden, activ, *parts = call(
            functools.partial(ffn_backward_kernel, units),
            [bf_rows(2 * units), bf_rows(units)] + part_outs,
            ready + [hidden, ffn_w],
            7,
        )
        done = []
        if above is not None:
            parts = joined(parts, [mix_units[three]])
            mix_units[two] = send(mix_rows, two, parts[0])
            done = [mix_units[two]]
        d_ffn_w = call(
            functools.partial(ffn_weights_kernel, units),
            shares_out(ffn_cols),
            f + joined(d_out, [parts[0]]) + [d_hidden, activ],
            6,
            place=place,
        )
        total = after(scatter_near(parts), d_ffn_w[0], *done)
        d_ffn_in = scatter_far(total)
        ffn_rows = settle_fast(*d_ffn_w)
        if above is None:
            out_total = scatter_near(joined(ffn_parts, [total]))
            d_ffn_in = after(d_ffn_in, out_total)
        grad_resid, d_attn, d_ssm, d_gain_attn, d_gain_ssm, d_gain_ffn = pull_mix(
            (grad_run, d_ffn_in)
        )
        d_ssm = gather_tokens(d_ssm.astype(BF16))
        d_attn = gather_tokens(after(d_attn.astype(BF16), d_ssm[0]))
        if above is not None:
            finish_ffn(layer + 1, ffn_above, ffn_above_units, d_ssm[0])
        ready = joined(d_ssm, [d_attn[0], ffn_rows])
        ffn_units = {unit: send(ffn_rows, unit, ready[0]) for unit in (one, three, two_a)}
        d_proj, d_conv, d_z, small_scan, d_step_w = call(
            functools.partial(
                scan_backward_kernel, cols, chan, wide, rank, state, seqs, length
            ),
            [
                out((proj_rows, tokens), BF16),
                f_rows(wide),
                bf_rows(wide),
                out((8 + state, wide), F32),
                out((rank, wide), F32),
            ],
            ready + [proj, conv, z, step_mats, vecs, dlogs, mix_w],
            26,
            scan_scratch
            + [
                pltpu.VMEM((length, STATES_AT_ONCE * (wide // LANES), seqs, LANES), F32),
                tiled,
                tiled,
                tiled,
                state_tiled,
                state_tiled,
            ],
            place=place,
            layers=(None,) * 7 + (layer,) * 3,
        )
        d_proj = after(d_proj, *ffn_units.values(), *d_attn[1:3])
        (d_qkv,) = call(
            functools.partial(attend_backward_kernel, cols, length),
            [bf_rows(cols.o)],
            joined(d_attn, [d_proj]) + [mix_w, qkv],
            5,
            place=place,
        )
        d_proj = after(sum_group(d_proj), d_qkv)
        ffn_units[two_b] = send(ffn_rows, two_b, d_proj)
        d_x, *parts, d_scan_w, small_conv = call(
            functools.partial(mix_backward_kernel, cols, chan, length),
            [bf_rows(wide)] + part_outs + [out((proj_rows, wide), F32), out((8, wide), F32)],
            [d_proj, conv, xi, d_conv, d_z, d_qkv, mix_w, vecs, scan_mats],
            6,
            place=place,
            layers=(None,) * 7 + (layer, layer),
        )
        parts = joined(parts, [ffn_units[two_b]])
        d_mix_w = call(
            functools.partial(mix_weights_kernel, cols, chan),
            shares_out(cols.end),
            n + d_attn + d_ssm + [d_qkv, heads, gated, after(d_x, parts[0]), d_z],
            7,
            place=place,
        )
        done = [d_mix_w[0]]
        if above is None:
            running = residual + scatter_far(after(out_total, parts[0]))
            output = (running * mask).astype(BF16)
            done.append(output)
        total = after(scatter_near(parts), *done)
        d_normed = scatter_far(total)
        mix_rows = settle_fast(*d_mix_w)
        if above is not None:
            finish_mix(layer + 1, above[0], mix_units, total)
        grad_lower, d_gain_input = pull_input(d_normed)
        grad_run = grad_resid + grad_lower
        gain_grads[layer] = jnp.stack([d_gain_input, d_gain_attn, d_gain_ssm, d_gain_ffn])
        small = jnp.concatenate([small_scan, small_conv, d_step_w, d_scan_w], axis=0)[:, :chan]
        small_rows.append(small)
        above = (mix_rows, ffn_rows, ffn_units)

    output = all_rows(output, d_normed)
    mix_units = {unit: send(mix_rows, unit, d_normed) for unit in (one, two, three)}
    finish_ffn(0, ffn_rows, ffn_units, d_normed)
    small = finish_small(after(jnp.stack(small_rows[::-1]), grad_run))
    input_grad = all_rows(grad_run).astype(F32)
    finish_mix(0, mix_rows, mix_units, None)

    gains = jnp.sum(every_tensor(rounded(jnp.stack(gain_grads))).astype(F32), axis=0)
    gains = sum(p.astype(F32) for p in every_fast(rounded(gains)))
    grad_gains = sum(p.astype(F32) for p in every_slow(rounded(gains)))

    base = 8 + state
    grad_step_bias = small[:, 0]
    grad_skip = small[:, 1]
    grad_decay = small[:, 8:base].transpose(0, 2, 1)
    grad_conv_weight = small[:, base : base + CONV]
    grad_conv_bias = small[:, base + CONV]
    base = base + 8
    grad_step_weight = small[:, base : base + rank_true]
    base = base + rank
    scan_rows = jnp.concatenate(
        [small[:, base : base + rank_true], small[:, base + rank :]], axis=1
    )
    grad_scan = scan_rows.transpose(0, 2, 1)
    d_q, d_kv, d_o, d_ssm_w, d_in = big["mix"]
    d_gate, d_down = big["ffn"]
    return (
        output,
        input_grad,
        grad_gains,
        d_q,
        d_kv,
        d_o.swapaxes(1, 2),
        d_in,
        grad_conv_weight,
        grad_conv_bias,
        grad_step_bias,
        grad_decay,
        grad_skip,
        grad_scan,
        grad_step_weight,
        d_ssm_w.swapaxes(1, 2),
        d_gate,
        d_down.swapaxes(1, 2),
    )


def solution(mesh):
    return jax.shard_map(
        functools.partial(per_device, mesh.shape["dp"], mesh.shape["tensor"]),
        mesh=mesh,
        in_specs=(
            P(None, "dp", None, None),
            P(None, "dp", None, None),
            P(None, "dp"),
            P(),
            P(None, "dp", None),
            P(None, "dp", None, None),
            P(None, None, "dp"),
            P(None, "dp", None, "tensor"),
            P(None, None, "tensor"),
            P(None, "tensor"),
            P(None, "tensor"),
            P(None, "tensor", None),
            P(None, "tensor"),
            P(None, "tensor", None),
            P(None, None, "tensor"),
            P(None, "tensor", "dp"),
            P(None, "dp", None, "tensor"),
            P(None, "tensor", "dp"),
        ),
        out_specs=(
            P(None, "dp", None, None),
            P(None, "dp", None, None),
            P(),
            P(None, "dp", None),
            P(None, "dp", None, None),
            P(None, None, "dp"),
            P(None, "dp", None, "tensor"),
            P(None, None, "tensor"),
            P(None, "tensor"),
            P(None, "tensor"),
            P(None, "tensor", None),
            P(None, "tensor"),
            P(None, "tensor", None),
            P(None, None, "tensor"),
            P(None, "tensor", "dp"),
            P(None, "dp", None, "tensor"),
            P(None, "tensor", "dp"),
        ),
        check_vma=False,
    )
```

```python
import functools

import jax
import jax.numpy as jnp
from jax import lax
from jax.experimental import pallas as pl
from jax.experimental.pallas import tpu as pltpu
from jax.sharding import PartitionSpec as P

KVH = 5
HEAD = 64
GQ = 5
CONV = 4
WINDOW = 1024
EPSILON = 1e-06
GROUP = 4
LANES = 128
F32 = jnp.float32
BF16 = jnp.bfloat16
NN = (((1,), (0,)), ((), ()))
NT = (((1,), (1,)), ((), ()))
TN = (((0,), (0,)), ((), ()))


def mm(left, right, dims=NN):
    return lax.dot_general(left, right, dims, preferred_element_type=F32)


def sigmoid(v):
    return 1.0 / (1.0 + jnp.exp(-v))


def softplus(v):
    return jnp.maximum(v, 0.0) + jnp.log(1.0 + jnp.exp(-jnp.abs(v)))


def params(megabytes=56):
    return pltpu.CompilerParams(vmem_limit_bytes=megabytes * 2**20)


def cost(micros):
    return pl.CostEstimate(flops=int(micros * 10**9), bytes_accessed=1, transcendentals=0)


def call(kernel, outs, args, micros, scratch=(), place=None, layers=()):
    vmem = pl.BlockSpec(memory_space=pltpu.VMEM)
    specs = []
    for k, a in enumerate(args):
        layer = layers[k] if k < len(layers) else None
        if layer is None:
            specs.append(vmem)
        else:
            at = (layer,) + (0,) * (a.ndim - 1)
            specs.append(pl.BlockSpec((None,) + a.shape[1:], lambda step, at=at: at))
    if place is not None:
        specs.insert(0, pl.BlockSpec(memory_space=pltpu.SMEM))
        args = [place] + list(args)
    return pl.pallas_call(
        kernel,
        out_shape=outs,
        grid=(1,) if layers else (),
        in_specs=specs,
        out_specs=[vmem] * len(outs),
        scratch_shapes=list(scratch),
        compiler_params=params(),
        cost_estimate=cost(micros),
    )(*args)


def call_into(kernel, layer, outs, before, args, place):
    vmem = pl.BlockSpec(memory_space=pltpu.VMEM)
    specs = [pl.BlockSpec(memory_space=pltpu.SMEM)] + [vmem] * len(args)
    out_specs = []
    for o in outs:
        at = (layer,) + (0,) * (len(o.shape) - 1)
        out_specs.append(pl.BlockSpec((None,) + o.shape[1:], lambda step, at=at: at))
    operands = [place] + list(args)
    aliases = {}
    if before is not None:
        aliases = {len(operands) + k: k for k in range(len(outs))}
        specs += [pl.BlockSpec(memory_space=pl.ANY)] * len(outs)
        operands += list(before)
    skip = len(aliases)

    def body(*refs):
        count = 1 + len(args)
        kernel(*refs[:count], *refs[count + skip :])

    return pl.pallas_call(
        body,
        out_shape=outs,
        grid=(1,),
        in_specs=specs,
        out_specs=out_specs,
        input_output_aliases=aliases,
        compiler_params=params(),
        cost_estimate=cost(4),
    )(*operands)


def out(shape, dtype):
    return jax.ShapeDtypeStruct(shape, dtype)


def widen(values, width):
    rows, have = values.shape
    if have == width:
        return values
    return jnp.concatenate([values, jnp.zeros((rows, width - have), values.dtype)], axis=1)


def shift_rows(values, amount, length):
    if amount == 0:
        return values
    rows = values.shape[0]
    place = lax.broadcasted_iota(jnp.int32, values.shape, 0) % length
    moved = pltpu.roll(values, amount % rows, 0)
    inside = place >= amount if amount > 0 else place < length + amount
    return jnp.where(inside, moved, 0.0)


def conv_pre(inner_x, taps, bias, length):
    running = bias
    for k in range(CONV):
        running = running + shift_rows(inner_x, CONV - 1 - k, length) * taps[k : k + 1]
    return running


def scores_of(queries, keys, length):
    scores = lax.dot_general(
        queries, keys, (((2,), (2,)), ((0,), (0,))), preferred_element_type=F32
    ) * HEAD ** (-0.5)
    shape = scores.shape
    query_pos = lax.broadcasted_iota(jnp.int32, shape, 1)
    key_pos = lax.broadcasted_iota(jnp.int32, shape, 2)
    allowed = (key_pos <= query_pos) & (key_pos > query_pos - WINDOW)
    scores = jnp.where(allowed, scores, -1e30)
    weights = jnp.exp(scores - jnp.max(scores, axis=-1, keepdims=True))
    return weights / jnp.sum(weights, axis=-1, keepdims=True)


class Mix:
    def __init__(self, chan):
        self.q = 0
        self.kv = 2 * HEAD
        self.o = 4 * HEAD
        self.s = 6 * HEAD
        self.x = self.s + chan
        self.z = self.x + chan
        self.end = self.z + chan


def swap(flag, first, second):
    return jnp.where(flag, second, first), jnp.where(flag, first, second)


def to_sequences(place, values):
    rows, columns = values.shape
    blocks = values.reshape(4, GROUP, rows // (4 * GROUP), columns)
    chip, core = place[2] == 1, place[3] == 1
    low, high = [], []
    for own in (0, 1):
        first, second = swap(chip, blocks[2 * own], blocks[2 * own + 1])
        low.append(first)
        high.append(second)
    parts = []
    for pair in (low, high):
        parts.append(jnp.stack(swap(core, pair[0], pair[1]), axis=1))
    return jnp.stack(parts, axis=1).reshape(rows, columns)


def to_blocks(place, values):
    rows, columns = values.shape
    parts = values.reshape(GROUP, 2, 2, rows // (4 * GROUP), columns)
    chip, core = place[2] == 1, place[3] == 1
    own, other = swap(core, parts[:, :, 0], parts[:, :, 1])
    blocks = []
    for half in (own, other):
        blocks.extend(swap(chip, half[:, 0], half[:, 1]))
    return jnp.concatenate([b.reshape(rows // 4, columns) for b in blocks], axis=0)


def rows_of(blocks):
    return jnp.concatenate([b[...] for b in blocks], axis=0)


def to_parts(parts, values):
    count = values.shape[0] // 4
    for k in range(4):
        parts[k][...] = values[k * count : (k + 1) * count].astype(BF16)


def mix_forward_kernel(cols, chan, wide, length, place, n0, n1, n2, n3, w, vec, scan_w, xi, z, conv, qkv, heads, proj, p0, p1, p2, p3):
    normed = rows_of((n0, n1, n2, n3))
    both = to_sequences(place, mm(normed, w[:, : cols.o]).astype(BF16))
    qkv[...] = both
    inner = to_sequences(place, mm(normed, w[:, cols.x :]))
    inner_x = widen(inner[:, :chan], wide)
    xi[...] = inner_x
    z[...] = widen(inner[:, chan:], wide)
    running = conv_pre(inner_x, vec[:CONV], vec[CONV : CONV + 1], length)
    conv_low = (running * sigmoid(running)).astype(BF16)
    conv[...] = conv_low
    proj[...] = mm(scan_w[...], conv_low, NT).astype(BF16)
    seqs = normed.shape[0] // length
    keys = both[:, cols.kv : cols.kv + HEAD].reshape(seqs, length, HEAD)
    values = both[:, cols.kv + HEAD : cols.o].reshape(seqs, length, HEAD)
    outs = []
    for h in range(2):
        queries = both[:, h * HEAD : (h + 1) * HEAD].reshape(seqs, length, HEAD)
        probs = scores_of(queries, keys, length).astype(BF16)
        mixed = lax.dot_general(
            probs, values, (((2,), (1,)), ((0,), (0,))), preferred_element_type=F32
        )
        outs.append(mixed.reshape(seqs * length, HEAD))
    heads_out = to_blocks(place, jnp.concatenate(outs, axis=1).astype(BF16))
    heads[...] = heads_out
    to_parts((p0, p1, p2, p3), mm(heads_out, w[:, cols.o : cols.s], NT))


def spread(state, wide):
    row = lax.broadcasted_iota(jnp.int32, (state, wide), 0)
    col = lax.broadcasted_iota(jnp.int32, (state, wide), 1) // LANES
    return (row == col).astype(BF16)


def lane(n):
    return slice(n * LANES, (n + 1) * LANES)


def tiles_in(ref, values):
    for n in range(ref.shape[0]):
        ref[n] = values[:, lane(n)]


def tiles_out(ref):
    return jnp.concatenate([ref[n] for n in range(ref.shape[0])], axis=1)


LOG2E = 1.4426950408889634
STATES_AT_ONCE = 8


def time_major(rows, length):
    seqs = rows // length
    came = lax.broadcasted_iota(jnp.int32, (rows, rows), 0)
    goes = lax.broadcasted_iota(jnp.int32, (rows, rows), 1)
    return (came == (goes % seqs) * length + goes // seqs).astype(BF16)


def scan_setup(rank, state, seqs, length, proj, conv, step_w, step_b, dlog, dt_s, dtx_s, drive_s, read_s, rate_s):
    pre = mm(proj[:rank], step_w[...], TN) + step_b
    dt = softplus(pre)
    tiles_in(dt_s, dt)
    tiles_in(dtx_s, dt * conv)
    table = spread(state, state * LANES)
    order = time_major(seqs * length, length)
    maps = mm(proj[rank:], order).astype(BF16)
    drive = mm(maps[:state], table, TN)
    read = mm(maps[state:], table, TN)
    for n in range(state):
        drive_s[:, n] = drive[:, lane(n)].reshape(length, seqs, LANES)
        read_s[:, n] = read[:, lane(n)].reshape(length, seqs, LANES)
    rates = -LOG2E * jnp.exp(dlog[...])
    for n in range(state):
        rate_s[n] = jnp.broadcast_to(rates[n : n + 1], (seqs, rates.shape[1]))
    return pre


def scan_forward_loop(first, tiles, seqs, length, dt_s, dtx_s, drive_s, read_s, rate_s, y_s, keep_s):
    def step(t, held):
        rows = pl.ds(t, seqs, stride=length)
        dt = [dt_s[i, rows] for i in range(tiles)]
        dtx = [dtx_s[i, rows] for i in range(tiles)]
        total = [y_s[i, rows] if first else jnp.zeros_like(dt[i]) for i in range(tiles)]
        fresh = []
        for j in range(STATES_AT_ONCE):
            n = first + j
            drive = drive_s[t, n]
            read = read_s[t, n]
            for i in range(tiles):
                decay = jnp.exp2(dt[i] * rate_s[n, :, lane(i)])
                now = decay * held[j * tiles + i] + dtx[i] * drive
                total[i] = total[i] + now * read
                if keep_s is not None:
                    keep_s[t, j * tiles + i] = now
                fresh.append(now)
        for i in range(tiles):
            y_s[i, rows] = total[i]
        return tuple(fresh)

    zero = jnp.zeros((seqs, LANES), F32)
    lax.fori_loop(0, length, step, (zero,) * (STATES_AT_ONCE * tiles), unroll=4)


def scan_forward_kernel(cols, chan, wide, rank, state, seqs, length, place, proj, conv, z, step_w, vec, dlog, w, gated, p0, p1, p2, p3, dt_s, dtx_s, drive_s, read_s, rate_s, y_s):
    conv32 = conv[...].astype(F32)
    step_b, skip = vec[CONV + 1 : CONV + 2], vec[CONV + 2 : CONV + 3]
    scan_setup(rank, state, seqs, length, proj, conv32, step_w, step_b, dlog, dt_s, dtx_s, drive_s, read_s, rate_s)
    for first in range(0, state, STATES_AT_ONCE):
        scan_forward_loop(first, wide // LANES, seqs, length, dt_s, dtx_s, drive_s, read_s, rate_s, y_s, None)
    gate = z[...]
    low = ((tiles_out(y_s) + skip * conv32) * (gate * sigmoid(gate))).astype(BF16)
    low = to_blocks(place, low)
    gated[...] = low
    to_parts((p0, p1, p2, p3), mm(low[:, :chan], w[:, cols.s : cols.x], NT))


def split_sum(table, values):
    high = values.astype(BF16)
    rest = (values - high.astype(F32)).astype(BF16)
    return mm(table, high, NT) + mm(table, rest, NT)


def scan_backward_loop(first, tiles, seqs, length, dt_s, dtx_s, drive_s, read_s, rate_s, keep_s, ds_s, ddt_s, dsrc_s, pd_s, pr_s):
    count = STATES_AT_ONCE * tiles

    def step(back, carry):
        t = length - 1 - back
        rows = pl.ds(t, seqs, stride=length)
        dt = [dt_s[i, rows] for i in range(tiles)]
        dtx = [dtx_s[i, rows] for i in range(tiles)]
        ds = [ds_s[i, rows] for i in range(tiles)]
        zero = jnp.zeros_like(dt[0])
        d_src = [dsrc_s[i, rows] if first else zero for i in range(tiles)]
        d_dt = [ddt_s[i, rows] if first else zero for i in range(tiles)]
        lams = []
        sums = []
        for j in range(STATES_AT_ONCE):
            n = first + j
            drive = drive_s[t, n]
            read = read_s[t, n]
            of_read = zero
            of_drive = zero
            for i in range(tiles):
                k = j * tiles + i
                rate = rate_s[n, :, lane(i)]
                kept = keep_s[t, k]
                lam = carry[k] + read * ds[i]
                of_read = of_read + kept * ds[i]
                of_drive = of_drive + lam * dtx[i]
                d_src[i] = d_src[i] + lam * drive
                d_log = lam * (kept - dtx[i] * drive)
                d_dt[i] = d_dt[i] + d_log * rate
                sums.append(carry[count + k] + d_log * dt[i])
                lams.append(jnp.exp2(dt[i] * rate) * lam)
            pr_s[t, n] = of_read
            pd_s[t, n] = of_drive
        for i in range(tiles):
            dsrc_s[i, rows] = d_src[i]
            ddt_s[i, rows] = d_dt[i]
        return tuple(lams) + tuple(sums)

    zero = jnp.zeros((seqs, LANES), F32)
    return lax.fori_loop(0, length, step, (zero,) * (2 * count), unroll=4)[count:]


def scan_backward_kernel(cols, chan, wide, rank, state, seqs, length, place, g0, g1, g2, g3, proj, conv, z, step_w, vec, dlog, w, d_proj, d_conv, d_z, small, d_step_w, dt_s, dtx_s, drive_s, read_s, rate_s, y_s, keep_s, ds_s, ddt_s, dsrc_s, pd_s, pr_s):
    tiles = wide // LANES
    conv32 = conv[...].astype(F32)
    step_b, skip = vec[CONV + 1 : CONV + 2], vec[CONV + 2 : CONV + 3]
    pre = scan_setup(rank, state, seqs, length, proj, conv32, step_w, step_b, dlog, dt_s, dtx_s, drive_s, read_s, rate_s)
    d_gated = to_sequences(place, mm(rows_of((g0, g1, g2, g3)), w[:, cols.s : cols.x]))
    d_gated = widen(d_gated, wide)
    gate = z[...]
    sig = sigmoid(gate)
    d_scanned = d_gated * (gate * sig)
    tiles_in(ds_s, d_scanned)
    d_rates = []
    for first in range(0, state, STATES_AT_ONCE):
        scan_forward_loop(first, tiles, seqs, length, dt_s, dtx_s, drive_s, read_s, rate_s, y_s, keep_s)
        sums = scan_backward_loop(first, tiles, seqs, length, dt_s, dtx_s, drive_s, read_s, rate_s, keep_s, ds_s, ddt_s, dsrc_s, pd_s, pr_s)
        for j in range(STATES_AT_ONCE):
            d_rates.append(
                jnp.concatenate(
                    [jnp.sum(sums[j * tiles + i], axis=0, keepdims=True) for i in range(tiles)],
                    axis=1,
                )
            )
    d_src = tiles_out(dsrc_s)
    dt = tiles_out(dt_s)
    d_dt = tiles_out(ddt_s) * (1.0 / LOG2E) + d_src * conv32
    d_conv[...] = skip * d_scanned + d_src * dt
    scanned = tiles_out(y_s) + skip * conv32
    d_z[...] = (d_gated * scanned * (sig * (1.0 + gate * (1.0 - sig)))).astype(BF16)
    d_pre = d_dt * sigmoid(pre)
    rates = -jnp.exp(dlog[...])
    sums = [
        jnp.sum(d_pre, axis=0, keepdims=True),
        jnp.sum(d_scanned * conv32, axis=0, keepdims=True),
        jnp.zeros((14, wide), F32),
        jnp.concatenate(d_rates, axis=0) * rates,
    ]
    small[...] = jnp.concatenate(sums, axis=0).astype(BF16)
    low = d_pre.astype(BF16)
    d_step_w[...] = mm(proj[:rank], low).astype(BF16)
    table = spread(state, state * LANES)
    tokens = seqs * length
    by_time = [
        jnp.concatenate([ref[:, n].reshape(tokens, LANES) for n in range(state)], axis=1)
        for ref in (pd_s, pr_s)
    ]
    d_maps = jnp.concatenate([split_sum(table, values) for values in by_time], axis=0)
    order = time_major(tokens, length)
    d_proj[:rank] = mm(step_w[...], low, NT).astype(BF16)
    d_proj[rank:] = mm(d_maps.astype(BF16), order, NT).astype(BF16)


def attend_backward_kernel(cols, length, place, g0, g1, g2, g3, w, qkv, d_qkv):
    d_heads = mm(rows_of((g0, g1, g2, g3)), w[:, cols.o : cols.s]).astype(BF16)
    d_heads = to_sequences(place, d_heads)
    both = qkv[...]
    seqs = both.shape[0] // length
    keys = both[:, cols.kv : cols.kv + HEAD].reshape(seqs, length, HEAD)
    values = both[:, cols.kv + HEAD : cols.o].reshape(seqs, length, HEAD)
    parts = []
    d_keys = 0.0
    d_values = 0.0
    for h in range(2):
        queries = both[:, h * HEAD : (h + 1) * HEAD].reshape(seqs, length, HEAD)
        d_out = d_heads[:, h * HEAD : (h + 1) * HEAD].reshape(seqs, length, HEAD)
        probs = scores_of(queries, keys, length)
        d_probs = lax.dot_general(
            d_out, values, (((2,), (2,)), ((0,), (0,))), preferred_element_type=F32
        )
        d_scores = (
            probs
            * (d_probs - jnp.sum(d_probs * probs, axis=-1, keepdims=True))
            * HEAD ** (-0.5)
        ).astype(BF16)
        d_query = lax.dot_general(
            d_scores, keys, (((2,), (1,)), ((0,), (0,))), preferred_element_type=F32
        )
        parts.append(d_query.reshape(seqs * length, HEAD))
        d_keys = d_keys + lax.dot_general(
            d_scores, queries, (((1,), (1,)), ((0,), (0,))), preferred_element_type=F32
        )
        d_values = d_values + lax.dot_general(
            probs.astype(BF16), d_out, (((1,), (1,)), ((0,), (0,))), preferred_element_type=F32
        )
    parts.append(d_keys.reshape(seqs * length, HEAD))
    parts.append(d_values.reshape(seqs * length, HEAD))
    d_qkv[...] = jnp.concatenate(parts, axis=1).astype(BF16)


def mix_backward_kernel(cols, chan, length, place, proj, conv, xi, d_conv, d_z, d_qkv, w, vec, scan_w, d_x, p0, p1, p2, p3, d_scan_w, small):
    taps, bias = vec[:CONV], vec[CONV : CONV + 1]
    d_out = d_conv[...] + mm(proj[...], scan_w[...], TN)
    inner_x = xi[...]
    running = conv_pre(inner_x, taps, bias, length)
    sig = sigmoid(running)
    d_run = d_out * (sig * (1.0 + running * (1.0 - sig)))
    d_in = 0.0
    sums = []
    for k in range(CONV):
        back = CONV - 1 - k
        d_in = d_in + shift_rows(d_run, -back, length) * taps[k : k + 1]
        sums.append(jnp.sum(d_run * shift_rows(inner_x, back, length), axis=0, keepdims=True))
    sums.append(jnp.sum(d_run, axis=0, keepdims=True))
    sums.append(jnp.zeros((16 - CONV - 1, inner_x.shape[1]), F32))
    small[...] = jnp.concatenate(sums, axis=0).astype(BF16)
    low = d_in.astype(BF16)
    d_x[...] = low
    inner = to_blocks(place, jnp.concatenate([low[:, :chan], d_z[:, :chan]], axis=1))
    heads = to_blocks(place, d_qkv[...])
    to_parts((p0, p1, p2, p3), mm(inner, w[:, cols.x :], NT) + mm(heads, w[:, : cols.o], NT))
    d_scan_w[...] = mm(proj[...], conv[...]).astype(BF16)


def mix_weights_kernel(cols, chan, place, n0, n1, n2, n3, a0, a1, a2, a3, s0, s1, s2, s3, d_qkv, heads, gated, d_x, d_z, *outs):
    normed = rows_of((n0, n1, n2, n3))
    inner = jnp.concatenate([d_x[:, :chan], d_z[:, :chan]], axis=1)
    to_shares(place, outs, 0, mm(normed, to_blocks(place, d_qkv[...]), TN))
    to_shares(place, outs, cols.o, mm(rows_of((a0, a1, a2, a3)), heads[...], TN))
    to_shares(place, outs, cols.s, mm(rows_of((s0, s1, s2, s3)), gated[:, :chan], TN))
    to_shares(place, outs, cols.x, mm(normed, to_blocks(place, inner), TN))


def picker(rows, columns, start, valid):
    row = lax.broadcasted_iota(jnp.int32, (rows, columns), 0)
    col = lax.broadcasted_iota(jnp.int32, (rows, columns), 1)
    return ((row == start + col) & (col < valid)).astype(BF16)


def pack_mix_kernel(cols, chan, tensor_size, place, q, key, value, o, x, z, ssm, *packed):
    tensor_idx = place[1]
    for slow_idx in range(GROUP):

        @pl.when(place[0] == slow_idx)
        def _():
            for by in range(GROUP):
                s = (slow_idx + by) % GROUP
                unit = s * tensor_size + tensor_idx
                group = lax.div(unit, 3)
                sub = lax.rem(unit, 3)
                valid = jnp.where(group >= KVH, 0, jnp.where(sub == 2, HEAD, 2 * HEAD))
                heads = picker(q.shape[1], 2 * HEAD, group * GQ * HEAD + sub * 2 * HEAD, valid)
                both = picker(key.shape[1], HEAD, jnp.minimum(group, KVH - 1) * HEAD, HEAD)
                mine = slice(s * chan, (s + 1) * chan)
                packed[by][:, : cols.kv] = mm(q[...], heads).astype(BF16)
                packed[by][:, cols.kv : cols.o] = jnp.concatenate(
                    [mm(key[...], both), mm(value[...], both)], axis=1
                ).astype(BF16)
                packed[by][:, cols.o : cols.s] = mm(o[...], heads).astype(BF16)
                packed[by][:, cols.s : cols.x] = ssm[:, mine]
                packed[by][:, cols.x : cols.z] = x[:, mine]
                packed[by][:, cols.z :] = z[:, mine]


def pack_ffn_kernel(units, place, gate, up, down, *packed):
    for slow_idx in range(GROUP):

        @pl.when(place[0] == slow_idx)
        def _():
            for by in range(GROUP):
                s = (slow_idx + by) % GROUP
                mine = slice(s * units, (s + 1) * units)
                packed[by][:, :units] = gate[:, mine]
                packed[by][:, units : 2 * units] = up[:, mine]
                packed[by][:, 2 * units :] = down[:, mine]


def to_shares(place, outs, start, values):
    keep, odd, even = outs
    share = keep.shape[1]
    fast = odd.shape[0] + 1
    values = values.astype(BF16)
    columns = slice(start, start + values.shape[1])
    for s in range(GROUP):
        by = lax.rem(s - place[0] + GROUP, GROUP)
        for f in range(fast):
            at = (s * fast + f) * share
            rows = values[at : at + share]
            turn = lax.rem(f - place[4] + fast, fast)

            @pl.when(turn == 0)
            def _():
                keep[by, :, columns] = rows

            @pl.when((turn > 0) & (lax.rem(by, 2) == 1))
            def _():
                odd[turn - 1, lax.div(by, 2), :, columns] = rows

            @pl.when((turn > 0) & (lax.rem(by, 2) == 0))
            def _():
                even[turn - 1, 1 - lax.div(by, 2), :, columns] = rows


def unpack_heads_kernel(cols, tensor_size, place, *refs):
    blocks, (d_q, d_kv, d_o) = (refs[:4], refs[4:8]), refs[8:]
    slow_idx = place[0]
    for tensor_idx in range(tensor_size):

        @pl.when(place[1] == tensor_idx)
        def _():
            for group in range(KVH):
                total = 0.0
                for sub in range(3):
                    unit = 3 * group + sub
                    s, t = unit // tensor_size, unit % tensor_size
                    by = lax.rem(slow_idx - s + GROUP, GROUP)
                    at = lax.div(by, 2)
                    apart = t ^ tensor_idx
                    block = apart // 2 + 2 * (apart % 2)
                    piece = jnp.where(
                        lax.rem(by, 2) == 0, blocks[0][block][at], blocks[1][block][at]
                    ).astype(F32)
                    start = group * GQ * HEAD + sub * 2 * HEAD
                    width = HEAD if sub == 2 else 2 * HEAD
                    d_q[:, start : start + width] = piece[:, :width]
                    d_o[:, start : start + width] = piece[:, cols.o : cols.o + width]
                    total = total + piece[:, cols.kv : cols.o]
                d_kv[:, 0, group * HEAD : (group + 1) * HEAD] = total[:, :HEAD]
                d_kv[:, 1, group * HEAD : (group + 1) * HEAD] = total[:, HEAD:]


def unpack_channels_kernel(cols, chan, place, pieces, d_ssm, d_in):
    slow_idx = place[0]
    for s in range(GROUP):
        came = lax.rem(slow_idx - s + GROUP, GROUP)
        mine = slice(s * chan, (s + 1) * chan)
        d_ssm[:, mine] = pieces[came, :, cols.s : cols.x].astype(F32)
        d_in[:, 0, mine] = pieces[came, :, cols.x : cols.z].astype(F32)
        d_in[:, 1, mine] = pieces[came, :, cols.z :].astype(F32)


def unpack_columns_kernel(width, place, pieces, pair, *single):
    slow_idx = place[0]
    for s in range(GROUP):
        came = lax.rem(slow_idx - s + GROUP, GROUP)
        mine = slice(s * width, (s + 1) * width)
        for k in range(2):
            pair[:, k, mine] = pieces[came, :, k * width : (k + 1) * width].astype(F32)
        for ref in single:
            ref[:, mine] = pieces[came, :, 2 * width :].astype(F32)


def small_grads_kernel(chan, rank, state, place, shared, conv_w, conv_b, step_b, dlog, skip, scan_w, step_w):
    low = step_w.shape[0]
    layers = conv_w.shape[0]
    per = 2 * 16 + state + 2 * rank + 2 * state
    for layer in range(layers):
        for s in range(GROUP):
            mine = slice(s * chan, (s + 1) * chan)

            def rows(start, count):
                at = layer * per + start
                return shared[s, at : at + count].astype(F32)

            step_b[layer : layer + 1, mine] = rows(0, 1)
            skip[layer : layer + 1, mine] = rows(1, 1)
            dlog[layer, :, mine] = rows(16, state)
            base = 16 + state
            conv_w[layer, :, mine] = rows(base, CONV)
            conv_b[layer : layer + 1, mine] = rows(base + CONV, 1)
            base = base + 16
            step_w[:, layer, mine] = rows(base, low)
            base = base + rank
            scan_w[:low, layer, mine] = rows(base, low)
            scan_w[low:, layer, mine] = rows(base + rank, 2 * state)


def small_weights_kernel(chan, wide, rank, place, conv_w, conv_b, step_b, dlog, skip, scan_w, step_w, vec, dlog_out, scan_out, step_out):
    layers = vec.shape[0]
    low = scan_w.shape[0] - 2 * dlog.shape[1]
    vec[...] = jnp.zeros(vec.shape, F32)
    dlog_out[...] = jnp.zeros(dlog_out.shape, F32)
    scan_out[...] = jnp.zeros(scan_out.shape, BF16)
    step_out[...] = jnp.zeros(step_out.shape, BF16)
    for s in range(GROUP):

        @pl.when(place[0] == s)
        def _():
            mine = slice(s * chan, (s + 1) * chan)
            for layer in range(layers):
                vec[layer, :CONV, :chan] = conv_w[layer, :, mine]
                vec[layer, CONV : CONV + 1, :chan] = conv_b[layer : layer + 1, mine]
                vec[layer, CONV + 1 : CONV + 2, :chan] = step_b[layer : layer + 1, mine]
                vec[layer, CONV + 2 : CONV + 3, :chan] = skip[layer : layer + 1, mine]
                dlog_out[layer, :, :chan] = dlog[layer, :, mine]
                scan_out[layer, :low, :chan] = scan_w[:low, layer, mine]
                scan_out[layer, rank:, :chan] = scan_w[low:, layer, mine]
                step_out[layer, :low, :chan] = step_w[:, layer, mine]


def ffn_forward_kernel(units, f0, f1, f2, f3, w, hidden, p0, p1, p2, p3):
    both = mm(rows_of((f0, f1, f2, f3)), w[:, : 2 * units])
    hidden[...] = both
    gate = both[:, :units]
    activ = (gate * sigmoid(gate) * both[:, units:]).astype(BF16)
    to_parts((p0, p1, p2, p3), mm(activ, w[:, 2 * units :], NT))


def ffn_backward_kernel(units, d0, d1, d2, d3, hidden, w, d_hidden, activ, p0, p1, p2, p3):
    d_activ = mm(rows_of((d0, d1, d2, d3)), w[:, 2 * units :])
    gate = hidden[:, :units]
    up = hidden[:, units:]
    sig = sigmoid(gate)
    swish = gate * sig
    activ[...] = (swish * up).astype(BF16)
    low = jnp.concatenate(
        [d_activ * up * (sig * (1.0 + gate * (1.0 - sig))), d_activ * swish], axis=1
    ).astype(BF16)
    d_hidden[...] = low
    to_parts((p0, p1, p2, p3), mm(low, w[:, : 2 * units], NT))


def ffn_weights_kernel(units, place, f0, f1, f2, f3, d0, d1, d2, d3, d_hidden, activ, *outs):
    to_shares(place, outs, 0, mm(rows_of((f0, f1, f2, f3)), d_hidden[...], TN))
    to_shares(place, outs, 2 * units, mm(rows_of((d0, d1, d2, d3)), activ[...], TN))


def rms_scale(values, gain_vec):
    return (
        values * lax.rsqrt(jnp.mean(values * values, axis=-1, keepdims=True) + EPSILON) * gain_vec
    )


def mix_branches(resid_in, attn_out, ssm_out, gain_attn, gain_ssm, gain_ffn):
    residual = resid_in + 0.5 * (rms_scale(attn_out, gain_attn) + rms_scale(ssm_out, gain_ssm))
    return (residual, rms_scale(residual, gain_ffn))


def per_device(
    dp_size,
    tensor_size,
    hidden_in,
    out_grad,
    lengths,
    norm_gains,
    q_weight,
    kv_weight,
    o_weight,
    in_weight,
    conv_weight,
    conv_bias,
    step_bias,
    decay_log,
    skip_gain,
    scan_weight,
    step_weight,
    ssm_weight,
    gate_weight,
    down_weight,
):
    layers = q_weight.shape[0]
    batches, _, length, width = hidden_in.shape
    fast = dp_size // GROUP
    share = width // dp_size
    chan = in_weight.shape[3] // GROUP
    wide = -(-chan // LANES) * LANES
    units = gate_weight.shape[3] // GROUP
    rank_true = step_weight.shape[1]
    state = decay_log.shape[2]
    rank = -(-rank_true // 16) * 16
    proj_rows = rank + 2 * state
    cols = Mix(chan)
    ffn_cols = 3 * units
    dp_idx = lax.axis_index("dp")
    slow_idx = dp_idx // fast
    fast_idx = dp_idx % fast
    tensor_idx = lax.axis_index("tensor")
    rows_here = batches * length // tensor_size
    seqs = GROUP * batches
    tokens = seqs * length
    half = tensor_size // 2

    def slow_perm(by):
        return [
            (s * fast + f, ((s + by) % GROUP) * fast + f) for s in range(GROUP) for f in range(fast)
        ]

    def fast_perm(by):
        return [
            (s * fast + f, s * fast + (f + by) % fast) for s in range(GROUP) for f in range(fast)
        ]

    core_perm = [(t, t ^ 1) for t in range(tensor_size)]
    chip_perm = [(t, t ^ 2) for t in range(tensor_size)]
    core_idx = tensor_idx % 2
    chip_idx = tensor_idx // 2

    def slow(values, by):
        return lax.ppermute(values, "dp", slow_perm(by)) if by % GROUP else values

    def other_fast(values, by):
        return lax.ppermute(values, "dp", fast_perm(by)) if by % fast else values

    def add_low(*terms):
        total = terms[0].astype(F32)
        for term in terms[1:]:
            total = total + term.astype(F32)
        return total.astype(BF16)

    def after(values, *earlier):
        return lax.optimization_barrier((values,) + earlier)[0] if earlier else values

    def gather_far(own):
        return jnp.concatenate([slow(own, by) for by in range(GROUP)], axis=0)

    def joined(values, done):
        values, done = tuple(values), tuple(done)
        return list(lax.optimization_barrier(values + done)[: len(values)]) if done else list(values)

    def gather_near(mine, work=()):
        chip = after(lax.ppermute(mine, "tensor", chip_perm), *work)
        core = lax.ppermute(mine, "tensor", core_perm)
        return [mine, chip, core, lax.ppermute(chip, "tensor", core_perm)]

    def gather_tokens(own):
        return gather_near(gather_far(own))

    def scatter_core(parts):
        return add_low(parts[1], lax.ppermute(parts[3], "tensor", core_perm))

    def scatter_near(parts, far=None):
        far = scatter_core(parts) if far is None else far
        near = add_low(parts[0], lax.ppermute(parts[2], "tensor", core_perm))
        return add_low(near, lax.ppermute(far, "tensor", chip_perm))

    def scatter_far(total):
        total = total.reshape(GROUP, rows_here, width)
        result = total[0].astype(F32)
        for by in range(1, GROUP):
            result = result + slow(total[by], GROUP - by).astype(F32)
        return result

    def sum_near(values):
        halves = values.reshape(2, values.shape[0] // 2, tokens)
        mine = lax.dynamic_index_in_dim(halves, core_idx, 0, False)
        theirs = lax.dynamic_index_in_dim(halves, 1 - core_idx, 0, False)
        mine = add_low(mine, lax.ppermute(theirs, "tensor", core_perm))
        return add_low(mine, lax.ppermute(mine, "tensor", chip_perm))

    def sum_far(mine):
        chunk = tokens // GROUP
        terms = [mine] + [slow(mine, by) for by in range(1, GROUP)]
        mine = add_low(*[jnp.roll(term, by * chunk, axis=1) for by, term in enumerate(terms)])
        theirs = lax.ppermute(mine, "tensor", core_perm)
        return jnp.where(
            core_idx == 0,
            jnp.concatenate([mine, theirs], axis=0),
            jnp.concatenate([theirs, mine], axis=0),
        )

    place = jnp.stack([slow_idx, tensor_idx, chip_idx, core_idx, fast_idx]).astype(jnp.int32)

    middle = share // 16 * 8
    one, three, two = (1, 0, share), (3, 0, share), (2, 0, share)
    two_a, two_b = (2, 0, middle), (2, middle, share)

    def send(pieces, unit, *ties):
        by, low, high = unit
        return slow(after(pieces[by][low:high], *ties), by)

    class Fetched:
        def __init__(self, own):
            self.full = jnp.zeros((GROUP, fast, share, own.shape[1]), BF16)
            self.add((0, 0, share), own)

        def add(self, unit, piece):
            by, low, _ = unit
            for turn in range(fast):
                self.full = lax.dynamic_update_slice(
                    self.full,
                    other_fast(piece, turn)[None, None],
                    ((slow_idx - by) % GROUP, (fast_idx - turn) % fast, low, 0),
                )

        def whole(self):
            return self.full.reshape(width, self.full.shape[3])

    def rows_round(own, units_in, tie):
        columns = own.shape[1]
        half = jnp.zeros((GROUP, share, columns), BF16)
        for (by, low, _), piece in [((0, 0, share), own)] + list(units_in.items()):
            half = lax.dynamic_update_slice(half, piece[None], ((slow_idx - by) % GROUP, low, 0))
        moved = [half] + [other_fast(half, turn) for turn in range(1, fast)]
        moved = joined(moved, [tie])
        if fast == 2:
            first, second = moved
            full = jnp.where(
                fast_idx == 0, jnp.stack([first, second], 1), jnp.stack([second, first], 1)
            )
        else:
            full = jnp.zeros((GROUP, fast, share, columns), BF16)
            for turn, rows in enumerate(moved):
                full = lax.dynamic_update_slice(
                    full, rows[:, None], (0, (fast_idx - turn) % fast, 0, 0)
                )
        return full.reshape(width, columns)

    def shares_out(columns):
        some = out((fast - 1, 2, share, columns), BF16)
        return [out((GROUP, share, columns), BF16), some, some]

    def go_round(some, *ties):
        some = after(some, *ties)
        return [other_fast(some[turn - 1], turn) for turn in range(1, fast)]

    def add_round(keep, moved, pieces):
        return {by: add_low(keep[by], *[m[k] for m in moved]) for k, by in enumerate(pieces)}

    def all_pieces(rows, units_in, tie):
        names = (one, three) + ((two,) if two in units_in else (two_a, two_b))
        own, first, third, *second = joined([rows[0]] + [units_in[unit] for unit in names], [tie])
        second = second[0] if len(second) == 1 else jnp.concatenate(second, axis=0)
        return own, first, second, third

    def stacked(rows, units_in, tie):
        return jnp.stack(all_pieces(rows, units_in, tie))

    o_turned = o_weight.swapaxes(1, 2)
    ssm_turned = ssm_weight.swapaxes(1, 2)
    down_turned = down_weight.swapaxes(1, 2)

    def pack_mix(layer, place):
        inner = in_weight[layer]
        both = kv_weight[layer]
        packed = call(
            functools.partial(pack_mix_kernel, cols, chan, tensor_size),
            [out((share, cols.end), BF16)] * GROUP,
            [q_weight, both[:, 0], both[:, 1], o_turned, inner[:, 0], inner[:, 1], ssm_turned],
            5,
            place=place,
            layers=(layer, None, None, layer, None, None, layer),
        )
        return packed

    def pack_ffn(layer, place):
        gate = gate_weight[layer]
        packed = call(
            functools.partial(pack_ffn_kernel, units),
            [out((share, ffn_cols), BF16)] * GROUP,
            [gate[:, 0], gate[:, 1], down_turned],
            3,
            place=place,
            layers=(None, None, layer),
        )
        return packed

    vecs, dlogs, scan_mats, step_mats = call(
        functools.partial(small_weights_kernel, chan, wide, rank),
        [
            out((layers, 8, wide), F32),
            out((layers, state, wide), F32),
            out((layers, proj_rows, wide), BF16),
            out((layers, rank, wide), BF16),
        ],
        [
            conv_weight,
            conv_bias,
            step_bias,
            decay_log.swapaxes(1, 2),
            skip_gain,
            scan_weight.transpose(2, 0, 1),
            step_weight.swapaxes(0, 1),
        ],
        2,
        place=place,
    )

    bf_rows = lambda columns: out((tokens, columns), BF16)
    f_rows = lambda columns: out((tokens, columns), F32)
    tiled = pltpu.VMEM((wide // LANES, tokens, LANES), F32)
    state_tiled = pltpu.VMEM((length, state, seqs, LANES), F32)
    scan_scratch = [
        tiled,
        tiled,
        state_tiled,
        state_tiled,
        pltpu.VMEM((state, seqs, wide), F32),
        tiled,
    ]

    def own_rows(values):
        flat = values.reshape(batches * length, width)
        return lax.dynamic_slice_in_dim(flat, tensor_idx * rows_here, rows_here, 0)

    part_outs = [out((tokens // 4, width), BF16)] * 4
    token = tensor_idx * rows_here + jnp.arange(rows_here)
    mask = (token % length < lengths[token // length, 0]).astype(F32)[:, None]
    grad_run = own_rows(out_grad).astype(F32) * mask
    part_outs = [out((tokens // 4, width), BF16)] * 4
    running = own_rows(hidden_in).astype(F32)
    kept = []
    fetched = []
    own = pack_mix(0, place)
    first = {unit: send(own, unit) for unit in (one, three)}
    first[two] = send(own, two, first[one], first[three])
    mix_packed = [own]
    ffn_packed = [pack_ffn(0, after(place, first[one]))]
    place_later = after(place, first[one], first[three])
    for layer in range(1, layers):
        mix_packed.append(pack_mix(layer, place_later))
        ffn_packed.append(pack_ffn(layer, place_later))
    for layer in range(layers):
        final = layer + 1 == layers
        gains = norm_gains[layer]
        normed, pull_input = jax.vjp(rms_scale, running, gains[0])
        normed = normed.astype(BF16)
        ffn_own, ffn_in_units = ffn_packed[layer], {}
        if layer == 0:
            mix_got = Fetched(own[0])
            for unit, piece in first.items():
                mix_got.add(unit, piece)
            n = gather_tokens(normed)
            mix_w = after(mix_got.whole(), *[p[0] for p in mix_packed[1:] + ffn_packed])
        else:
            n = gather_tokens(normed)
            for unit in (one, three):
                ffn_in_units[unit] = send(ffn_own, unit, n[0])
            mix_w = after(mix_got.whole(), ffn_in_units[one])
        ready = joined(n, [mix_w])
        if layer == 0:
            for unit in (one, three):
                ffn_in_units[unit] = send(ffn_own, unit, first[two])
        xi, z, conv, qkv, heads, proj_part, *attn_parts = call(
            functools.partial(mix_forward_kernel, cols, chan, wide, length),
            [
                f_rows(wide),
                f_rows(wide),
                bf_rows(wide),
                bf_rows(cols.o),
                bf_rows(2 * HEAD),
                out((proj_rows, tokens), BF16),
            ]
            + part_outs,
            ready + [mix_w, vecs, scan_mats],
            7,
            place=place,
            layers=(None,) * 5 + (layer, layer),
        )
        proj_part = after(proj_part, ffn_in_units[one], ffn_in_units[three])
        ffn_in_units[two_a] = send(ffn_own, two_a, proj_part)
        proj = sum_far(after(sum_near(proj_part), ffn_in_units[two_a]))
        ffn_in_units[two_b] = send(ffn_own, two_b, proj)
        attn_total = scatter_near(joined(attn_parts, [proj]))
        gated, *ssm_parts = call(
            functools.partial(
                scan_forward_kernel, cols, chan, wide, rank, state, seqs, length
            ),
            [bf_rows(wide)] + part_outs,
            [proj, conv, z, step_mats, vecs, dlogs, mix_w],
            11,
            scan_scratch,
            place=place,
            layers=(None,) * 3 + (layer,) * 3,
        )
        ssm_parts = joined(ssm_parts, [attn_total, ffn_in_units[two_b]])
        attn_out = scatter_far(after(attn_total, ssm_parts[0]))
        ssm_out = scatter_far(scatter_near(ssm_parts))
        (residual, ffn_in), pull_mix = jax.vjp(
            mix_branches, running, attn_out, ssm_out, gains[1], gains[2], gains[3]
        )
        ffn_in = ffn_in.astype(BF16)
        f = gather_tokens(ffn_in)
        ffn_w = rows_round(ffn_own[0], ffn_in_units, ffn_in)
        fetched.append((mix_w, ffn_w))
        if final:
            d_out = gather_tokens(after(grad_run.astype(BF16), f[2]))
            ffn_w = after(ffn_w, d_out[0])
        else:
            own = mix_packed[layer + 1]
            mix_got = Fetched(own[0])
            unit_two = send(own, two, f[0])
            ffn_w = after(ffn_w, unit_two)
            mix_got.add(two, unit_two)
        ready = joined(f, [ffn_w])
        if not final:
            unit_one = send(own, one, ready[0])
        hidden, *ffn_parts = call(
            functools.partial(ffn_forward_kernel, units),
            [f_rows(2 * units)] + part_outs,
            ready + [ffn_w],
            7,
        )
        if not final:
            ffn_parts = joined(ffn_parts, [unit_one])
            mix_got.add(one, unit_one)
            unit_three = send(own, three, ffn_parts[0])
            total = after(scatter_near(ffn_parts), unit_three)
            mix_got.add(three, unit_three)
            running = residual + scatter_far(total)
        kept.append((n, pull_input, xi, z, conv, qkv, heads, proj, gated, pull_mix, f, hidden))

    def every_tensor(values):
        moved = lax.ppermute(values, "tensor", chip_perm)
        values = jnp.where(chip_idx == 0, jnp.stack([values, moved]), jnp.stack([moved, values]))
        moved = lax.ppermute(values, "tensor", core_perm)
        values = jnp.where(
            core_idx == 0, jnp.stack([values, moved], 1), jnp.stack([moved, values], 1)
        )
        return values.reshape((tensor_size,) + values.shape[2:])

    def tensor_blocks(mine):
        chip = lax.ppermute(mine, "tensor", chip_perm)
        core = lax.ppermute(mine, "tensor", core_perm)
        return [mine, chip, core, lax.ppermute(chip, "tensor", core_perm)]

    def every_fast(values):
        turned = jnp.stack([other_fast(values, turn) for turn in range(fast)])
        return [
            lax.dynamic_index_in_dim(turned, (fast_idx - source) % fast, 0, False)
            for source in range(fast)
        ]

    def every_slow(values):
        turned = jnp.stack([slow(values, by) for by in range(GROUP)])
        return [
            lax.dynamic_index_in_dim(turned, (slow_idx - source) % GROUP, 0, False)
            for source in range(GROUP)
        ]

    def rounded(values):
        return lax.optimization_barrier(values.astype(BF16))

    def all_rows(own, *ties):
        return every_tensor(after(rounded(own), *ties)).reshape(batches, 1, length, width)

    big = {"heads": None, "mix": None, "ffn": None}
    small_rows = []
    gain_grads = [None] * layers
    early_rows = late_rows = None

    def finish_mix(layer, rows, units_in, tie):
        own, first, second, third = all_pieces(rows, units_in, tie)
        blocks = []
        for pair in ((own, second), (first, third)):
            blocks += tensor_blocks(jnp.stack([p[:, : cols.s] for p in pair]))
        big["heads"] = call_into(
            functools.partial(unpack_heads_kernel, cols, tensor_size),
            layer,
            [
                out((layers, share, KVH * GQ * HEAD), F32),
                out((layers, share, 2, KVH * HEAD), F32),
                out((layers, share, KVH * GQ * HEAD), F32),
            ],
            big["heads"],
            blocks,
            place,
        )
        big["mix"] = call_into(
            functools.partial(unpack_channels_kernel, cols, chan),
            layer,
            [
                out((layers, share, GROUP * chan), F32),
                out((layers, share, 2, GROUP * chan), F32),
            ],
            big["mix"],
            [stacked(rows, units_in, tie)],
            place,
        )

    def finish_ffn(layer, rows, units_in, tie):
        big["ffn"] = call_into(
            functools.partial(unpack_columns_kernel, units),
            layer,
            [
                out((layers, share, 2, GROUP * units), F32),
                out((layers, share, GROUP * units), F32),
            ],
            big["ffn"],
            [stacked(rows, units_in, tie)],
            place,
        )

    def small_near(rows):
        parts = rows.reshape(fast, rows.shape[0] // fast, chan)
        terms = []
        for turn in range(fast):
            part = lax.dynamic_index_in_dim(parts, (fast_idx + turn) % fast, 0, False)
            terms.append(other_fast(part, turn).astype(F32))
        return rounded(sum(terms))

    above = None
    for layer in reversed(range(layers)):
        mix_w, ffn_w = fetched[layer]
        n, pull_input, xi, z, conv, qkv, heads, proj, gated, pull_mix, f, hidden = kept[layer]
        if above is not None:
            d_out = gather_tokens(grad_run.astype(BF16))
            mix_rows, ffn_above, ffn_above_units = above
            running = residual + scatter_far(after(out_total, d_out[0]))
            output = (running * mask).astype(BF16)
            ffn_w = after(ffn_w, output)
        ready = joined(d_out, [ffn_w])
        if above is not None:
            mix_units = {one: send(mix_rows, one, ready[0])}
        d_hidden, activ, *parts = call(
            functools.partial(ffn_backward_kernel, units),
            [bf_rows(2 * units), bf_rows(units)] + part_outs,
            ready + [hidden, ffn_w],
            7,
        )
        done = []
        if above is not None:
            parts = joined(parts, [mix_units[one]])
            mix_units[three] = send(mix_rows, three, parts[0])
            done = [mix_units[three]]
        far = scatter_core(parts)
        d_ffn_w = call(
            functools.partial(ffn_weights_kernel, units),
            shares_out(ffn_cols),
            f + joined(d_out, [far]) + [d_hidden, activ],
            6,
            place=place,
        )
        total = after(scatter_near(parts, far), d_ffn_w[0], *done)
        d_ffn_in = scatter_far(total)
        if above is None:
            out_total = scatter_near(joined(ffn_parts, [total]))
            d_ffn_in = after(d_ffn_in, out_total)
        grad_resid, d_attn, d_ssm, d_gain_attn, d_gain_ssm, d_gain_ffn = pull_mix(
            (grad_run, d_ffn_in)
        )
        moved = go_round(d_ffn_w[1])
        d_ssm = gather_far(d_ssm.astype(BF16))
        work = ()
        if above is not None:
            finish_ffn(layer + 1, ffn_above, ffn_above_units, d_ssm)
            work = (big["ffn"][1],)
        d_ssm = gather_near(d_ssm, work)
        d_attn = gather_far(after(d_attn.astype(BF16), d_ssm[0]))
        done = [d_attn]
        ffn_rows = add_round(after(d_ffn_w[0], d_ssm[0]), moved, (1, 3))
        ffn_even = go_round(d_ffn_w[2], ffn_rows[1])
        ready = joined(d_ssm, done + list(ffn_rows.values()))
        d_attn = gather_near(after(d_attn, ready[0]))
        ffn_units = {one: send(ffn_rows, one, ready[0])}
        done = []
        if above is None:
            ffn_units[three] = send(ffn_rows, three, ready[0])
        else:
            mix_units[two] = send(mix_rows, two, ready[0])
            done = [mix_units[two]]
        d_proj, d_conv, d_z, small_scan, d_step_w = call(
            functools.partial(
                scan_backward_kernel, cols, chan, wide, rank, state, seqs, length
            ),
            [
                out((proj_rows, tokens), BF16),
                f_rows(wide),
                bf_rows(wide),
                out((16 + state, wide), BF16),
                out((rank, wide), BF16),
            ],
            ready + [proj, conv, z, step_mats, vecs, dlogs, mix_w],
            26,
            scan_scratch
            + [
                pltpu.VMEM((length, STATES_AT_ONCE * (wide // LANES), seqs, LANES), F32),
                tiled,
                tiled,
                tiled,
                state_tiled,
                state_tiled,
            ],
            place=place,
            layers=(None,) * 7 + (layer,) * 3,
        )
        d_proj = after(d_proj, *ffn_units.values(), *done, *ffn_even, *d_attn[1:3])
        ffn_rows.update(add_round(after(d_ffn_w[0], d_proj), ffn_even, (2, 0)))
        (d_qkv,) = call(
            functools.partial(attend_backward_kernel, cols, length),
            [bf_rows(cols.o)],
            joined(d_attn, [d_proj]) + [mix_w, qkv],
            5,
            place=place,
        )
        d_proj = sum_far(after(sum_near(d_proj), d_qkv))
        beside = two_a if above is None else three
        ffn_units[beside] = send(ffn_rows, beside, d_proj)
        d_x, *parts, d_scan_w, small_conv = call(
            functools.partial(mix_backward_kernel, cols, chan, length),
            [bf_rows(wide)] + part_outs + [out((proj_rows, wide), BF16), out((16, wide), BF16)],
            [d_proj, conv, xi, d_conv, d_z, d_qkv, mix_w, vecs, scan_mats],
            6,
            place=place,
            layers=(None,) * 7 + (layer, layer),
        )
        parts = joined(parts, [ffn_units[beside]])
        beside = two_b if above is None else two_a
        ffn_units[beside] = send(ffn_rows, beside, parts[0])
        done = [ffn_units[beside]]
        far = scatter_core(parts)
        d_mix_w = call(
            functools.partial(mix_weights_kernel, cols, chan),
            shares_out(cols.end),
            n + d_attn + d_ssm + [d_qkv, heads, gated, after(d_x, far), d_z],
            7,
            place=place,
        )
        done.append(d_mix_w[0])
        total = after(scatter_near(parts, far), *done)
        d_normed = scatter_far(total)
        keep, odd, even = d_mix_w
        mix_rows = add_round(keep, go_round(odd), (1, 3))
        d_normed = after(d_normed, mix_rows[1], mix_rows[3])
        moved = go_round(even, mix_rows[1])
        mix_rows.update(add_round(after(keep, d_normed), moved, (2, 0)))
        if above is not None:
            above_mix = above[0], mix_units
        grad_lower, d_gain_input = pull_input(d_normed)
        grad_run = grad_resid + grad_lower
        gain_grads[layer] = jnp.stack([d_gain_input, d_gain_attn, d_gain_ssm, d_gain_ffn])
        small = jnp.concatenate([small_scan, small_conv, d_step_w, d_scan_w], axis=0)[:, :chan]
        small_rows.append(small)
        above = (mix_rows, ffn_rows, ffn_units)

    mix_units = {unit: send(mix_rows, unit) for unit in (one, three)}
    gains = jnp.sum(every_tensor(rounded(jnp.stack(gain_grads))).astype(F32), axis=0)
    gains = after(gains, *mix_units.values(), mix_rows[2], mix_rows[0])
    small_count = layers * small_rows[0].shape[0]
    small = jnp.concatenate(small_rows[::-1] + [rounded(gains).reshape(-1, chan)], axis=0)
    extra = -small.shape[0] % (8 * fast)
    mix_units[two] = send(mix_rows, two, gains)
    small = small_near(jnp.pad(small, ((0, extra), (0, 0))))
    small = after(small, mix_units[two])
    for unit in (one, three, two_a, two_b):
        if unit not in ffn_units:
            ffn_units[unit] = send(ffn_rows, unit, small)
    if layers > 1:
        finish_mix(1, *above_mix, small)
    output = all_rows(output, small)
    input_grad = all_rows(grad_run, small).astype(F32)
    finish_mix(0, mix_rows, mix_units, small)
    small = jnp.stack(every_slow(small))
    finish_ffn(0, ffn_rows, ffn_units, small)
    shared = jnp.concatenate(every_fast(small), axis=1)
    grad_gains = jnp.sum(
        shared[:, small_count : shared.shape[1] - extra].astype(F32), axis=0
    ).reshape(norm_gains.shape)
    (
        grad_conv_weight,
        grad_conv_bias,
        grad_step_bias,
        grad_decay,
        grad_skip,
        grad_scan,
        grad_step_weight,
    ) = call(
        functools.partial(small_grads_kernel, chan, rank, state),
        [
            out(conv_weight.shape, F32),
            out(conv_bias.shape, F32),
            out(step_bias.shape, F32),
            out((layers, state, GROUP * chan), F32),
            out(skip_gain.shape, F32),
            out((rank_true + 2 * state, layers, GROUP * chan), F32),
            out((rank_true, layers, GROUP * chan), F32),
        ],
        [shared],
        4,
        place=place,
    )
    grad_decay = grad_decay.swapaxes(1, 2)
    grad_scan = grad_scan.transpose(1, 2, 0)
    grad_step_weight = grad_step_weight.swapaxes(0, 1)
    d_q, d_kv, d_o = big["heads"]
    d_ssm_w, d_in = big["mix"]
    d_gate, d_down = big["ffn"]
    return (
        output,
        input_grad,
        grad_gains,
        d_q,
        d_kv,
        d_o.swapaxes(1, 2),
        d_in,
        grad_conv_weight,
        grad_conv_bias,
        grad_step_bias,
        grad_decay,
        grad_skip,
        grad_scan,
        grad_step_weight,
        d_ssm_w.swapaxes(1, 2),
        d_gate,
        d_down.swapaxes(1, 2),
    )


def solution(mesh):
    return jax.shard_map(
        functools.partial(per_device, mesh.shape["dp"], mesh.shape["tensor"]),
        mesh=mesh,
        in_specs=(
            P(None, "dp", None, None),
            P(None, "dp", None, None),
            P(None, "dp"),
            P(),
            P(None, "dp", None),
            P(None, "dp", None, None),
            P(None, None, "dp"),
            P(None, "dp", None, "tensor"),
            P(None, None, "tensor"),
            P(None, "tensor"),
            P(None, "tensor"),
            P(None, "tensor", None),
            P(None, "tensor"),
            P(None, "tensor", None),
            P(None, None, "tensor"),
            P(None, "tensor", "dp"),
            P(None, "dp", None, "tensor"),
            P(None, "tensor", "dp"),
        ),
        out_specs=(
            P(None, "dp", None, None),
            P(None, "dp", None, None),
            P(),
            P(None, "dp", None),
            P(None, "dp", None, None),
            P(None, None, "dp"),
            P(None, "dp", None, "tensor"),
            P(None, None, "tensor"),
            P(None, "tensor"),
            P(None, "tensor"),
            P(None, "tensor", None),
            P(None, "tensor"),
            P(None, "tensor", None),
            P(None, None, "tensor"),
            P(None, "tensor", "dp"),
            P(None, "dp", None, "tensor"),
            P(None, "tensor", "dp"),
        ),
        check_vma=False,
    )
```

```python
import functools

import jax
import jax.numpy as jnp
from jax import lax
from jax.experimental import pallas as pl
from jax.experimental.pallas import tpu as pltpu
from jax.sharding import PartitionSpec as P

KVH = 5
HEAD = 64
GQ = 5
CONV = 4
WINDOW = 1024
EPSILON = 1e-06
GROUP = 4
LANES = 128
F32 = jnp.float32
BF16 = jnp.bfloat16
NN = (((1,), (0,)), ((), ()))
NT = (((1,), (1,)), ((), ()))
TN = (((0,), (0,)), ((), ()))


def mm(left, right, dims=NN):
    return lax.dot_general(left, right, dims, preferred_element_type=F32)


def sigmoid(v):
    return 1.0 / (1.0 + jnp.exp(-v))


def softplus(v):
    return jnp.maximum(v, 0.0) + jnp.log(1.0 + jnp.exp(-jnp.abs(v)))


def params(megabytes=56):
    return pltpu.CompilerParams(vmem_limit_bytes=megabytes * 2**20)


def cost(micros):
    return pl.CostEstimate(flops=int(micros * 10**9), bytes_accessed=1, transcendentals=0)


def call(kernel, outs, args, micros, scratch=(), place=None, layers=()):
    vmem = pl.BlockSpec(memory_space=pltpu.VMEM)
    specs = []
    for k, a in enumerate(args):
        layer = layers[k] if k < len(layers) else None
        if layer is None:
            specs.append(vmem)
        else:
            at = (layer,) + (0,) * (a.ndim - 1)
            specs.append(pl.BlockSpec((None,) + a.shape[1:], lambda step, at=at: at))
    if place is not None:
        specs.insert(0, pl.BlockSpec(memory_space=pltpu.SMEM))
        args = [place] + list(args)
    return pl.pallas_call(
        kernel,
        out_shape=outs,
        grid=(1,) if layers else (),
        in_specs=specs,
        out_specs=[vmem] * len(outs),
        scratch_shapes=list(scratch),
        compiler_params=params(),
        cost_estimate=cost(micros),
    )(*args)


def call_into(kernel, layer, outs, before, args, place):
    vmem = pl.BlockSpec(memory_space=pltpu.VMEM)
    specs = [pl.BlockSpec(memory_space=pltpu.SMEM)] + [vmem] * len(args)
    out_specs = []
    for o in outs:
        at = (layer,) + (0,) * (len(o.shape) - 1)
        out_specs.append(pl.BlockSpec((None,) + o.shape[1:], lambda step, at=at: at))
    operands = [place] + list(args)
    aliases = {}
    if before is not None:
        aliases = {len(operands) + k: k for k in range(len(outs))}
        specs += [pl.BlockSpec(memory_space=pl.ANY)] * len(outs)
        operands += list(before)
    skip = len(aliases)

    def body(*refs):
        count = 1 + len(args)
        kernel(*refs[:count], *refs[count + skip :])

    return pl.pallas_call(
        body,
        out_shape=outs,
        grid=(1,),
        in_specs=specs,
        out_specs=out_specs,
        input_output_aliases=aliases,
        compiler_params=params(),
        cost_estimate=cost(4),
    )(*operands)


def out(shape, dtype):
    return jax.ShapeDtypeStruct(shape, dtype)


def widen(values, width):
    rows, have = values.shape
    if have == width:
        return values
    return jnp.concatenate([values, jnp.zeros((rows, width - have), values.dtype)], axis=1)


def shift_rows(values, amount, length):
    if amount == 0:
        return values
    rows = values.shape[0]
    place = lax.broadcasted_iota(jnp.int32, values.shape, 0) % length
    moved = pltpu.roll(values, amount % rows, 0)
    inside = place >= amount if amount > 0 else place < length + amount
    return jnp.where(inside, moved, 0.0)


def conv_pre(inner_x, taps, bias, length):
    running = bias
    for k in range(CONV):
        running = running + shift_rows(inner_x, CONV - 1 - k, length) * taps[k : k + 1]
    return running


def scores_of(queries, keys, length):
    scores = lax.dot_general(
        queries, keys, (((2,), (2,)), ((0,), (0,))), preferred_element_type=F32
    ) * HEAD ** (-0.5)
    shape = scores.shape
    query_pos = lax.broadcasted_iota(jnp.int32, shape, 1)
    key_pos = lax.broadcasted_iota(jnp.int32, shape, 2)
    allowed = (key_pos <= query_pos) & (key_pos > query_pos - WINDOW)
    scores = jnp.where(allowed, scores, -1e30)
    weights = jnp.exp(scores - jnp.max(scores, axis=-1, keepdims=True))
    return weights / jnp.sum(weights, axis=-1, keepdims=True)


class Mix:
    def __init__(self, chan):
        self.q = 0
        self.kv = 2 * HEAD
        self.o = 4 * HEAD
        self.s = 6 * HEAD
        self.x = self.s + chan
        self.z = self.x + chan
        self.end = self.z + chan


def swap(flag, first, second):
    return jnp.where(flag, second, first), jnp.where(flag, first, second)


def to_sequences(place, values):
    rows, columns = values.shape
    blocks = values.reshape(4, GROUP, rows // (4 * GROUP), columns)
    chip, core = place[2] == 1, place[3] == 1
    low, high = [], []
    for own in (0, 1):
        first, second = swap(chip, blocks[2 * own], blocks[2 * own + 1])
        low.append(first)
        high.append(second)
    parts = []
    for pair in (low, high):
        parts.append(jnp.stack(swap(core, pair[0], pair[1]), axis=1))
    return jnp.stack(parts, axis=1).reshape(rows, columns)


def to_blocks(place, values):
    rows, columns = values.shape
    parts = values.reshape(GROUP, 2, 2, rows // (4 * GROUP), columns)
    chip, core = place[2] == 1, place[3] == 1
    own, other = swap(core, parts[:, :, 0], parts[:, :, 1])
    blocks = []
    for half in (own, other):
        blocks.extend(swap(chip, half[:, 0], half[:, 1]))
    return jnp.concatenate([b.reshape(rows // 4, columns) for b in blocks], axis=0)


def rows_of(blocks):
    return jnp.concatenate([b[...] for b in blocks], axis=0)


def to_parts(parts, values):
    count = values.shape[0] // 4
    for k in range(4):
        parts[k][...] = values[k * count : (k + 1) * count].astype(BF16)


def mix_forward_kernel(cols, chan, wide, length, place, n0, n1, n2, n3, w, vec, scan_w, xi, z, conv, qkv, heads, proj, p0, p1, p2, p3, *rest):
    if rest:
        rest[0][...] = w[:, cols.end :]
    normed = rows_of((n0, n1, n2, n3))
    both = to_sequences(place, mm(normed, w[:, : cols.o]).astype(BF16))
    qkv[...] = both
    inner = to_sequences(place, mm(normed, w[:, cols.x : cols.end]))
    inner_x = widen(inner[:, :chan], wide)
    xi[...] = inner_x
    z[...] = widen(inner[:, chan:], wide)
    running = conv_pre(inner_x, vec[:CONV], vec[CONV : CONV + 1], length)
    conv_low = (running * sigmoid(running)).astype(BF16)
    conv[...] = conv_low
    proj[...] = mm(scan_w[...], conv_low, NT).astype(BF16)
    seqs = normed.shape[0] // length
    keys = both[:, cols.kv : cols.kv + HEAD].reshape(seqs, length, HEAD)
    values = both[:, cols.kv + HEAD : cols.o].reshape(seqs, length, HEAD)
    outs = []
    for h in range(2):
        queries = both[:, h * HEAD : (h + 1) * HEAD].reshape(seqs, length, HEAD)
        probs = scores_of(queries, keys, length).astype(BF16)
        mixed = lax.dot_general(
            probs, values, (((2,), (1,)), ((0,), (0,))), preferred_element_type=F32
        )
        outs.append(mixed.reshape(seqs * length, HEAD))
    heads_out = to_blocks(place, jnp.concatenate(outs, axis=1).astype(BF16))
    heads[...] = heads_out
    to_parts((p0, p1, p2, p3), mm(heads_out, w[:, cols.o : cols.s], NT))


def spread(state, wide):
    row = lax.broadcasted_iota(jnp.int32, (state, wide), 0)
    col = lax.broadcasted_iota(jnp.int32, (state, wide), 1) // LANES
    return (row == col).astype(BF16)


def lane(n):
    return slice(n * LANES, (n + 1) * LANES)


def tiles_in(ref, values):
    for n in range(ref.shape[0]):
        ref[n] = values[:, lane(n)]


def tiles_out(ref):
    return jnp.concatenate([ref[n] for n in range(ref.shape[0])], axis=1)


LOG2E = 1.4426950408889634
STATES_AT_ONCE = 8


def time_major(rows, length):
    seqs = rows // length
    came = lax.broadcasted_iota(jnp.int32, (rows, rows), 0)
    goes = lax.broadcasted_iota(jnp.int32, (rows, rows), 1)
    return (came == (goes % seqs) * length + goes // seqs).astype(BF16)


def scan_setup(rank, state, seqs, length, proj, conv, step_w, step_b, dlog, dt_s, dtx_s, drive_s, read_s, rate_s):
    pre = mm(proj[:rank], step_w[...], TN) + step_b
    dt = softplus(pre)
    tiles_in(dt_s, dt)
    tiles_in(dtx_s, dt * conv)
    table = spread(state, state * LANES)
    order = time_major(seqs * length, length)
    maps = mm(proj[rank:], order).astype(BF16)
    drive = mm(maps[:state], table, TN)
    read = mm(maps[state:], table, TN)
    for n in range(state):
        drive_s[:, n] = drive[:, lane(n)].reshape(length, seqs, LANES)
        read_s[:, n] = read[:, lane(n)].reshape(length, seqs, LANES)
    rates = -LOG2E * jnp.exp(dlog[...])
    for n in range(state):
        rate_s[n] = jnp.broadcast_to(rates[n : n + 1], (seqs, rates.shape[1]))
    return pre


def scan_forward_loop(first, tiles, seqs, length, dt_s, dtx_s, drive_s, read_s, rate_s, y_s, keep_s):
    def step(t, held):
        rows = pl.ds(t, seqs, stride=length)
        dt = [dt_s[i, rows] for i in range(tiles)]
        dtx = [dtx_s[i, rows] for i in range(tiles)]
        total = [y_s[i, rows] if first else jnp.zeros_like(dt[i]) for i in range(tiles)]
        fresh = []
        for j in range(STATES_AT_ONCE):
            n = first + j
            drive = drive_s[t, n]
            read = read_s[t, n]
            for i in range(tiles):
                decay = jnp.exp2(dt[i] * rate_s[n, :, lane(i)])
                now = decay * held[j * tiles + i] + dtx[i] * drive
                total[i] = total[i] + now * read
                if keep_s is not None:
                    keep_s[t, j * tiles + i] = now
                fresh.append(now)
        for i in range(tiles):
            y_s[i, rows] = total[i]
        return tuple(fresh)

    zero = jnp.zeros((seqs, LANES), F32)
    lax.fori_loop(0, length, step, (zero,) * (STATES_AT_ONCE * tiles), unroll=4)


def scan_forward_kernel(cols, chan, wide, rank, state, seqs, length, place, proj, conv, z, step_w, vec, dlog, w, gated, p0, p1, p2, p3, dt_s, dtx_s, drive_s, read_s, rate_s, y_s):
    conv32 = conv[...].astype(F32)
    step_b, skip = vec[CONV + 1 : CONV + 2], vec[CONV + 2 : CONV + 3]
    scan_setup(rank, state, seqs, length, proj, conv32, step_w, step_b, dlog, dt_s, dtx_s, drive_s, read_s, rate_s)
    for first in range(0, state, STATES_AT_ONCE):
        scan_forward_loop(first, wide // LANES, seqs, length, dt_s, dtx_s, drive_s, read_s, rate_s, y_s, None)
    gate = z[...]
    low = ((tiles_out(y_s) + skip * conv32) * (gate * sigmoid(gate))).astype(BF16)
    low = to_blocks(place, low)
    gated[...] = low
    to_parts((p0, p1, p2, p3), mm(low[:, :chan], w[:, cols.s : cols.x], NT))


def split_sum(table, values):
    high = values.astype(BF16)
    rest = (values - high.astype(F32)).astype(BF16)
    return mm(table, high, NT) + mm(table, rest, NT)


def scan_backward_loop(first, tiles, seqs, length, dt_s, dtx_s, drive_s, read_s, rate_s, keep_s, ds_s, ddt_s, dsrc_s, pd_s, pr_s):
    count = STATES_AT_ONCE * tiles

    def step(back, carry):
        t = length - 1 - back
        rows = pl.ds(t, seqs, stride=length)
        dt = [dt_s[i, rows] for i in range(tiles)]
        dtx = [dtx_s[i, rows] for i in range(tiles)]
        ds = [ds_s[i, rows] for i in range(tiles)]
        zero = jnp.zeros_like(dt[0])
        d_src = [dsrc_s[i, rows] if first else zero for i in range(tiles)]
        d_dt = [ddt_s[i, rows] if first else zero for i in range(tiles)]
        lams = []
        sums = []
        for j in range(STATES_AT_ONCE):
            n = first + j
            drive = drive_s[t, n]
            read = read_s[t, n]
            of_read = zero
            of_drive = zero
            for i in range(tiles):
                k = j * tiles + i
                rate = rate_s[n, :, lane(i)]
                kept = keep_s[t, k]
                lam = carry[k] + read * ds[i]
                of_read = of_read + kept * ds[i]
                of_drive = of_drive + lam * dtx[i]
                d_src[i] = d_src[i] + lam * drive
                d_log = lam * (kept - dtx[i] * drive)
                d_dt[i] = d_dt[i] + d_log * rate
                sums.append(carry[count + k] + d_log * dt[i])
                lams.append(jnp.exp2(dt[i] * rate) * lam)
            pr_s[t, n] = of_read
            pd_s[t, n] = of_drive
        for i in range(tiles):
            dsrc_s[i, rows] = d_src[i]
            ddt_s[i, rows] = d_dt[i]
        return tuple(lams) + tuple(sums)

    zero = jnp.zeros((seqs, LANES), F32)
    return lax.fori_loop(0, length, step, (zero,) * (2 * count), unroll=4)[count:]


def scan_backward_kernel(cols, chan, wide, rank, state, seqs, length, place, g0, g1, g2, g3, proj, conv, z, step_w, vec, dlog, w, d_proj, d_conv, d_z, small, d_step_w, dt_s, dtx_s, drive_s, read_s, rate_s, y_s, keep_s, ds_s, ddt_s, dsrc_s, pd_s, pr_s):
    tiles = wide // LANES
    conv32 = conv[...].astype(F32)
    step_b, skip = vec[CONV + 1 : CONV + 2], vec[CONV + 2 : CONV + 3]
    pre = scan_setup(rank, state, seqs, length, proj, conv32, step_w, step_b, dlog, dt_s, dtx_s, drive_s, read_s, rate_s)
    d_gated = to_sequences(place, mm(rows_of((g0, g1, g2, g3)), w[:, cols.s : cols.x]))
    d_gated = widen(d_gated, wide)
    gate = z[...]
    sig = sigmoid(gate)
    d_scanned = d_gated * (gate * sig)
    tiles_in(ds_s, d_scanned)
    d_rates = []
    for first in range(0, state, STATES_AT_ONCE):
        scan_forward_loop(first, tiles, seqs, length, dt_s, dtx_s, drive_s, read_s, rate_s, y_s, keep_s)
        sums = scan_backward_loop(first, tiles, seqs, length, dt_s, dtx_s, drive_s, read_s, rate_s, keep_s, ds_s, ddt_s, dsrc_s, pd_s, pr_s)
        for j in range(STATES_AT_ONCE):
            d_rates.append(
                jnp.concatenate(
                    [jnp.sum(sums[j * tiles + i], axis=0, keepdims=True) for i in range(tiles)],
                    axis=1,
                )
            )
    d_src = tiles_out(dsrc_s)
    dt = tiles_out(dt_s)
    d_dt = tiles_out(ddt_s) * (1.0 / LOG2E) + d_src * conv32
    d_conv[...] = skip * d_scanned + d_src * dt
    scanned = tiles_out(y_s) + skip * conv32
    d_z[...] = (d_gated * scanned * (sig * (1.0 + gate * (1.0 - sig)))).astype(BF16)
    d_pre = d_dt * sigmoid(pre)
    rates = -jnp.exp(dlog[...])
    sums = [
        jnp.sum(d_pre, axis=0, keepdims=True),
        jnp.sum(d_scanned * conv32, axis=0, keepdims=True),
        jnp.zeros((14, wide), F32),
        jnp.concatenate(d_rates, axis=0) * rates,
    ]
    small[...] = jnp.concatenate(sums, axis=0).astype(BF16)
    low = d_pre.astype(BF16)
    d_step_w[...] = mm(proj[:rank], low).astype(BF16)
    table = spread(state, state * LANES)
    tokens = seqs * length
    by_time = [
        jnp.concatenate([ref[:, n].reshape(tokens, LANES) for n in range(state)], axis=1)
        for ref in (pd_s, pr_s)
    ]
    d_maps = jnp.concatenate([split_sum(table, values) for values in by_time], axis=0)
    order = time_major(tokens, length)
    d_proj[:rank] = mm(step_w[...], low, NT).astype(BF16)
    d_proj[rank:] = mm(d_maps.astype(BF16), order, NT).astype(BF16)


def attend_backward_kernel(cols, length, place, g0, g1, g2, g3, w, qkv, d_qkv):
    d_heads = mm(rows_of((g0, g1, g2, g3)), w[:, cols.o : cols.s]).astype(BF16)
    d_heads = to_sequences(place, d_heads)
    both = qkv[...]
    seqs = both.shape[0] // length
    keys = both[:, cols.kv : cols.kv + HEAD].reshape(seqs, length, HEAD)
    values = both[:, cols.kv + HEAD : cols.o].reshape(seqs, length, HEAD)
    parts = []
    d_keys = 0.0
    d_values = 0.0
    for h in range(2):
        queries = both[:, h * HEAD : (h + 1) * HEAD].reshape(seqs, length, HEAD)
        d_out = d_heads[:, h * HEAD : (h + 1) * HEAD].reshape(seqs, length, HEAD)
        probs = scores_of(queries, keys, length)
        d_probs = lax.dot_general(
            d_out, values, (((2,), (2,)), ((0,), (0,))), preferred_element_type=F32
        )
        d_scores = (
            probs
            * (d_probs - jnp.sum(d_probs * probs, axis=-1, keepdims=True))
            * HEAD ** (-0.5)
        ).astype(BF16)
        d_query = lax.dot_general(
            d_scores, keys, (((2,), (1,)), ((0,), (0,))), preferred_element_type=F32
        )
        parts.append(d_query.reshape(seqs * length, HEAD))
        d_keys = d_keys + lax.dot_general(
            d_scores, queries, (((1,), (1,)), ((0,), (0,))), preferred_element_type=F32
        )
        d_values = d_values + lax.dot_general(
            probs.astype(BF16), d_out, (((1,), (1,)), ((0,), (0,))), preferred_element_type=F32
        )
    parts.append(d_keys.reshape(seqs * length, HEAD))
    parts.append(d_values.reshape(seqs * length, HEAD))
    d_qkv[...] = jnp.concatenate(parts, axis=1).astype(BF16)


def mix_backward_kernel(cols, chan, length, place, proj, conv, xi, d_conv, d_z, d_qkv, w, vec, scan_w, d_x, p0, p1, p2, p3, d_scan_w, small):
    taps, bias = vec[:CONV], vec[CONV : CONV + 1]
    d_out = d_conv[...] + mm(proj[...], scan_w[...], TN)
    inner_x = xi[...]
    running = conv_pre(inner_x, taps, bias, length)
    sig = sigmoid(running)
    d_run = d_out * (sig * (1.0 + running * (1.0 - sig)))
    d_in = 0.0
    sums = []
    for k in range(CONV):
        back = CONV - 1 - k
        d_in = d_in + shift_rows(d_run, -back, length) * taps[k : k + 1]
        sums.append(jnp.sum(d_run * shift_rows(inner_x, back, length), axis=0, keepdims=True))
    sums.append(jnp.sum(d_run, axis=0, keepdims=True))
    sums.append(jnp.zeros((16 - CONV - 1, inner_x.shape[1]), F32))
    small[...] = jnp.concatenate(sums, axis=0).astype(BF16)
    low = d_in.astype(BF16)
    d_x[...] = low
    inner = to_blocks(place, jnp.concatenate([low[:, :chan], d_z[:, :chan]], axis=1))
    heads = to_blocks(place, d_qkv[...])
    to_parts((p0, p1, p2, p3), mm(inner, w[:, cols.x : cols.end], NT) + mm(heads, w[:, : cols.o], NT))
    d_scan_w[...] = mm(proj[...], conv[...]).astype(BF16)


def mix_weights_kernel(cols, chan, extra, place, n0, n1, n2, n3, a0, a1, a2, a3, s0, s1, s2, s3, d_qkv, heads, gated, d_x, d_z, *refs):
    outs = refs[-3:]
    normed = rows_of((n0, n1, n2, n3))
    inner = jnp.concatenate([d_x[:, :chan], d_z[:, :chan]], axis=1)
    to_shares(place, outs, 0, mm(normed, to_blocks(place, d_qkv[...]), TN))
    to_shares(place, outs, cols.o, mm(rows_of((a0, a1, a2, a3)), heads[...], TN))
    to_shares(place, outs, cols.s, mm(rows_of((s0, s1, s2, s3)), gated[:, :chan], TN))
    to_shares(place, outs, cols.x, mm(normed, to_blocks(place, inner), TN))
    if extra:
        to_shares(place, outs, cols.end, refs[0][...])


def picker(rows, columns, start, valid):
    row = lax.broadcasted_iota(jnp.int32, (rows, columns), 0)
    col = lax.broadcasted_iota(jnp.int32, (rows, columns), 1)
    return ((row == start + col) & (col < valid)).astype(BF16)


def pack_mix_kernel(cols, chan, units, extra, tensor_size, place, q, key, value, o, x, z, ssm, down, *packed):
    tensor_idx = place[1]
    for slow_idx in range(GROUP):

        @pl.when(place[0] == slow_idx)
        def _():
            for by in range(GROUP):
                s = (slow_idx + by) % GROUP
                unit = s * tensor_size + tensor_idx
                group = lax.div(unit, 3)
                sub = lax.rem(unit, 3)
                valid = jnp.where(group >= KVH, 0, jnp.where(sub == 2, HEAD, 2 * HEAD))
                heads = picker(q.shape[1], 2 * HEAD, group * GQ * HEAD + sub * 2 * HEAD, valid)
                both = picker(key.shape[1], HEAD, jnp.minimum(group, KVH - 1) * HEAD, HEAD)
                mine = slice(s * chan, (s + 1) * chan)
                packed[by][:, : cols.kv] = mm(q[...], heads).astype(BF16)
                packed[by][:, cols.kv : cols.o] = jnp.concatenate(
                    [mm(key[...], both), mm(value[...], both)], axis=1
                ).astype(BF16)
                packed[by][:, cols.o : cols.s] = mm(o[...], heads).astype(BF16)
                packed[by][:, cols.s : cols.x] = ssm[:, mine]
                packed[by][:, cols.x : cols.z] = x[:, mine]
                packed[by][:, cols.z : cols.end] = z[:, mine]
                if extra:
                    packed[by][:, cols.end :] = down[:, (s + 1) * units - extra : (s + 1) * units]


def pack_ffn_kernel(units, extra, place, gate, up, down, *packed):
    for slow_idx in range(GROUP):

        @pl.when(place[0] == slow_idx)
        def _():
            for by in range(GROUP):
                s = (slow_idx + by) % GROUP
                mine = slice(s * units, (s + 1) * units)
                packed[by][:, :units] = gate[:, mine]
                packed[by][:, units : 2 * units] = up[:, mine]
                packed[by][:, 2 * units :] = down[:, s * units : (s + 1) * units - extra]


def to_shares(place, outs, start, values):
    keep, odd, even = outs
    share = keep.shape[1]
    fast = odd.shape[0] + 1
    values = values.astype(BF16)
    columns = slice(start, start + values.shape[1])
    for s in range(GROUP):
        by = lax.rem(s - place[0] + GROUP, GROUP)
        for f in range(fast):
            at = (s * fast + f) * share
            rows = values[at : at + share]
            turn = lax.rem(f - place[4] + fast, fast)

            @pl.when(turn == 0)
            def _():
                keep[by, :, columns] = rows

            @pl.when((turn > 0) & (lax.rem(by, 2) == 1))
            def _():
                odd[turn - 1, lax.div(by, 2), :, columns] = rows

            @pl.when((turn > 0) & (lax.rem(by, 2) == 0))
            def _():
                even[turn - 1, 1 - lax.div(by, 2), :, columns] = rows


def unpack_heads_kernel(cols, tensor_size, place, *refs):
    blocks, (d_q, d_kv, d_o) = (refs[:4], refs[4:8]), refs[8:]
    slow_idx = place[0]
    for tensor_idx in range(tensor_size):

        @pl.when(place[1] == tensor_idx)
        def _():
            for group in range(KVH):
                total = 0.0
                for sub in range(3):
                    unit = 3 * group + sub
                    s, t = unit // tensor_size, unit % tensor_size
                    by = lax.rem(slow_idx - s + GROUP, GROUP)
                    at = lax.div(by, 2)
                    apart = t ^ tensor_idx
                    block = apart // 2 + 2 * (apart % 2)
                    piece = jnp.where(
                        lax.rem(by, 2) == 0, blocks[0][block][at], blocks[1][block][at]
                    ).astype(F32)
                    start = group * GQ * HEAD + sub * 2 * HEAD
                    width = HEAD if sub == 2 else 2 * HEAD
                    d_q[:, start : start + width] = piece[:, :width]
                    d_o[:, start : start + width] = piece[:, cols.o : cols.o + width]
                    total = total + piece[:, cols.kv : cols.o]
                d_kv[:, 0, group * HEAD : (group + 1) * HEAD] = total[:, :HEAD]
                d_kv[:, 1, group * HEAD : (group + 1) * HEAD] = total[:, HEAD:]


def unpack_channels_kernel(cols, chan, place, pieces, d_ssm, d_in):
    slow_idx = place[0]
    for s in range(GROUP):
        came = lax.rem(slow_idx - s + GROUP, GROUP)
        mine = slice(s * chan, (s + 1) * chan)
        d_ssm[:, mine] = pieces[came, :, cols.s : cols.x].astype(F32)
        d_in[:, 0, mine] = pieces[came, :, cols.x : cols.z].astype(F32)
        d_in[:, 1, mine] = pieces[came, :, cols.z : cols.end].astype(F32)


def unpack_ffn_kernel(units, extra, place, pieces, mix_pieces, gate_up, down):
    slow_idx = place[0]
    for s in range(GROUP):
        came = lax.rem(slow_idx - s + GROUP, GROUP)
        mine = slice(s * units, (s + 1) * units)
        last = (s + 1) * units - extra
        for k in range(2):
            gate_up[:, k, mine] = pieces[came, :, k * units : (k + 1) * units].astype(F32)
        down[:, s * units : last] = pieces[came, :, 2 * units :].astype(F32)
        if extra:
            columns = mix_pieces.shape[2]
            down[:, last : last + extra] = mix_pieces[came, :, columns - extra :].astype(F32)


def small_grads_kernel(chan, rank, state, place, shared, conv_w, conv_b, step_b, dlog, skip, scan_w, step_w):
    low = step_w.shape[0]
    layers = conv_w.shape[0]
    per = 2 * 16 + state + 2 * rank + 2 * state
    for layer in range(layers):
        for s in range(GROUP):
            mine = slice(s * chan, (s + 1) * chan)

            def rows(start, count):
                at = layer * per + start
                return shared[s, at : at + count].astype(F32)

            step_b[layer : layer + 1, mine] = rows(0, 1)
            skip[layer : layer + 1, mine] = rows(1, 1)
            dlog[layer, :, mine] = rows(16, state)
            base = 16 + state
            conv_w[layer, :, mine] = rows(base, CONV)
            conv_b[layer : layer + 1, mine] = rows(base + CONV, 1)
            base = base + 16
            step_w[:, layer, mine] = rows(base, low)
            base = base + rank
            scan_w[:low, layer, mine] = rows(base, low)
            scan_w[low:, layer, mine] = rows(base + rank, 2 * state)


def small_weights_kernel(chan, wide, rank, place, conv_w, conv_b, step_b, dlog, skip, scan_w, step_w, vec, dlog_out, scan_out, step_out):
    layers = vec.shape[0]
    low = scan_w.shape[0] - 2 * dlog.shape[1]
    vec[...] = jnp.zeros(vec.shape, F32)
    dlog_out[...] = jnp.zeros(dlog_out.shape, F32)
    scan_out[...] = jnp.zeros(scan_out.shape, BF16)
    step_out[...] = jnp.zeros(step_out.shape, BF16)
    for s in range(GROUP):

        @pl.when(place[0] == s)
        def _():
            mine = slice(s * chan, (s + 1) * chan)
            for layer in range(layers):
                vec[layer, :CONV, :chan] = conv_w[layer, :, mine]
                vec[layer, CONV : CONV + 1, :chan] = conv_b[layer : layer + 1, mine]
                vec[layer, CONV + 1 : CONV + 2, :chan] = step_b[layer : layer + 1, mine]
                vec[layer, CONV + 2 : CONV + 3, :chan] = skip[layer : layer + 1, mine]
                dlog_out[layer, :, :chan] = dlog[layer, :, mine]
                scan_out[layer, :low, :chan] = scan_w[:low, layer, mine]
                scan_out[layer, rank:, :chan] = scan_w[low:, layer, mine]
                step_out[layer, :low, :chan] = step_w[:, layer, mine]


def down_weights(units, w, rest):
    main = w[:, 2 * units :]
    return jnp.concatenate([main, rest[0][...]], axis=1) if rest else main


def ffn_forward_kernel(units, f0, f1, f2, f3, w, *refs):
    rest, (hidden, p0, p1, p2, p3) = refs[:-5], refs[-5:]
    both = mm(rows_of((f0, f1, f2, f3)), w[:, : 2 * units])
    hidden[...] = both
    gate = both[:, :units]
    activ = (gate * sigmoid(gate) * both[:, units:]).astype(BF16)
    to_parts((p0, p1, p2, p3), mm(activ, down_weights(units, w, rest), NT))


def ffn_backward_kernel(units, d0, d1, d2, d3, hidden, w, *refs):
    rest, (d_hidden, activ, p0, p1, p2, p3) = refs[:-6], refs[-6:]
    d_activ = mm(rows_of((d0, d1, d2, d3)), down_weights(units, w, rest))
    gate = hidden[:, :units]
    up = hidden[:, units:]
    sig = sigmoid(gate)
    swish = gate * sig
    activ[...] = (swish * up).astype(BF16)
    low = jnp.concatenate(
        [d_activ * up * (sig * (1.0 + gate * (1.0 - sig))), d_activ * swish], axis=1
    ).astype(BF16)
    d_hidden[...] = low
    to_parts((p0, p1, p2, p3), mm(low, w[:, : 2 * units], NT))


def ffn_weights_kernel(units, place, f0, f1, f2, f3, d0, d1, d2, d3, d_hidden, activ, *refs):
    outs, rest = refs[:3], refs[3:]
    to_shares(place, outs, 0, mm(rows_of((f0, f1, f2, f3)), d_hidden[...], TN))
    d_down = mm(rows_of((d0, d1, d2, d3)), activ[...], TN)
    main = outs[0].shape[2] - 2 * units
    to_shares(place, outs, 2 * units, d_down[:, :main])
    if rest:
        rest[0][...] = d_down[:, main:].astype(BF16)


def rms_scale(values, gain_vec):
    return (
        values * lax.rsqrt(jnp.mean(values * values, axis=-1, keepdims=True) + EPSILON) * gain_vec
    )


def mix_branches(resid_in, attn_out, ssm_out, gain_attn, gain_ssm, gain_ffn):
    residual = resid_in + 0.5 * (rms_scale(attn_out, gain_attn) + rms_scale(ssm_out, gain_ssm))
    return (residual, rms_scale(residual, gain_ffn))


def per_device(
    dp_size,
    tensor_size,
    hidden_in,
    out_grad,
    lengths,
    norm_gains,
    q_weight,
    kv_weight,
    o_weight,
    in_weight,
    conv_weight,
    conv_bias,
    step_bias,
    decay_log,
    skip_gain,
    scan_weight,
    step_weight,
    ssm_weight,
    gate_weight,
    down_weight,
):
    layers = q_weight.shape[0]
    batches, _, length, width = hidden_in.shape
    fast = dp_size // GROUP
    share = width // dp_size
    chan = in_weight.shape[3] // GROUP
    wide = -(-chan // LANES) * LANES
    units = gate_weight.shape[3] // GROUP
    rank_true = step_weight.shape[1]
    state = decay_log.shape[2]
    rank = -(-rank_true // 16) * 16
    proj_rows = rank + 2 * state
    cols = Mix(chan)
    over = 3 * units % LANES
    extra = over if over <= -cols.end % LANES else 0
    ffn_cols = 3 * units - extra
    mix_cols = cols.end + extra
    dp_idx = lax.axis_index("dp")
    slow_idx = dp_idx // fast
    fast_idx = dp_idx % fast
    tensor_idx = lax.axis_index("tensor")
    rows_here = batches * length // tensor_size
    seqs = GROUP * batches
    tokens = seqs * length
    half = tensor_size // 2

    def slow_perm(by):
        return [
            (s * fast + f, ((s + by) % GROUP) * fast + f) for s in range(GROUP) for f in range(fast)
        ]

    def fast_perm(by):
        return [
            (s * fast + f, s * fast + (f + by) % fast) for s in range(GROUP) for f in range(fast)
        ]

    core_perm = [(t, t ^ 1) for t in range(tensor_size)]
    chip_perm = [(t, t ^ 2) for t in range(tensor_size)]
    core_idx = tensor_idx % 2
    chip_idx = tensor_idx // 2

    def slow(values, by):
        return lax.ppermute(values, "dp", slow_perm(by)) if by % GROUP else values

    def other_fast(values, by):
        return lax.ppermute(values, "dp", fast_perm(by)) if by % fast else values

    def add_low(*terms):
        total = terms[0].astype(F32)
        for term in terms[1:]:
            total = total + term.astype(F32)
        return total.astype(BF16)

    def after(values, *earlier):
        return lax.optimization_barrier((values,) + earlier)[0] if earlier else values

    def gather_far(own):
        return jnp.concatenate([slow(own, by) for by in range(GROUP)], axis=0)

    def joined(values, done):
        values, done = tuple(values), tuple(done)
        return list(lax.optimization_barrier(values + done)[: len(values)]) if done else list(values)

    def gather_near(mine, beside=()):
        chip = after(lax.ppermute(mine, "tensor", chip_perm), *beside)
        core = lax.ppermute(mine, "tensor", core_perm)
        return [mine, chip, core, lax.ppermute(chip, "tensor", core_perm)]

    def gather_tokens(own):
        return gather_near(gather_far(own))

    def scatter_core(parts):
        return add_low(parts[1], lax.ppermute(parts[3], "tensor", core_perm))

    def scatter_near(parts, far=None):
        far = scatter_core(parts) if far is None else far
        near = add_low(parts[0], lax.ppermute(parts[2], "tensor", core_perm))
        return add_low(near, lax.ppermute(far, "tensor", chip_perm))

    def scatter_far(total):
        total = total.reshape(GROUP, rows_here, width)
        result = total[0].astype(F32)
        for by in range(1, GROUP):
            result = result + slow(total[by], GROUP - by).astype(F32)
        return result

    def sum_near(values):
        halves = values.reshape(2, values.shape[0] // 2, tokens)
        mine = lax.dynamic_index_in_dim(halves, core_idx, 0, False)
        theirs = lax.dynamic_index_in_dim(halves, 1 - core_idx, 0, False)
        mine = add_low(mine, lax.ppermute(theirs, "tensor", core_perm))
        return add_low(mine, lax.ppermute(mine, "tensor", chip_perm))

    def sum_far(mine, work=None):
        chunk = tokens // GROUP
        terms = [mine] + [slow(mine, by) for by in range(1, GROUP)]
        mine = add_low(*[jnp.roll(term, by * chunk, axis=1) for by, term in enumerate(terms)])
        mine = mine if work is None else after(mine, work)
        theirs = lax.ppermute(mine, "tensor", core_perm)
        return jnp.where(
            core_idx == 0,
            jnp.concatenate([mine, theirs], axis=0),
            jnp.concatenate([theirs, mine], axis=0),
        )

    place = jnp.stack([slow_idx, tensor_idx, chip_idx, core_idx, fast_idx]).astype(jnp.int32)

    middle = share // 16 * 8
    one, three, two = (1, 0, share), (3, 0, share), (2, 0, share)
    two_a, two_b = (2, 0, middle), (2, middle, share)

    def send(pieces, unit, *ties):
        by, low, high = unit
        return slow(after(pieces[by][low:high], *ties), by)

    class Fetched:
        def __init__(self, own):
            self.full = jnp.zeros((GROUP, fast, share, own.shape[1]), BF16)
            self.add((0, 0, share), own)

        def add(self, unit, piece):
            by, low, _ = unit
            for turn in range(fast):
                self.full = lax.dynamic_update_slice(
                    self.full,
                    other_fast(piece, turn)[None, None],
                    ((slow_idx - by) % GROUP, (fast_idx - turn) % fast, low, 0),
                )

        def whole(self):
            return self.full.reshape(width, self.full.shape[3])

    def rows_round(own, units_in, tie):
        columns = own.shape[1]
        half = jnp.zeros((GROUP, share, columns), BF16)
        for (by, low, _), piece in [((0, 0, share), own)] + list(units_in.items()):
            half = lax.dynamic_update_slice(half, piece[None], ((slow_idx - by) % GROUP, low, 0))
        moved = [half] + [other_fast(half, turn) for turn in range(1, fast)]
        moved = joined(moved, [tie])
        if fast == 2:
            first, second = moved
            full = jnp.where(
                fast_idx == 0, jnp.stack([first, second], 1), jnp.stack([second, first], 1)
            )
        else:
            full = jnp.zeros((GROUP, fast, share, columns), BF16)
            for turn, rows in enumerate(moved):
                full = lax.dynamic_update_slice(
                    full, rows[:, None], (0, (fast_idx - turn) % fast, 0, 0)
                )
        return full.reshape(width, columns)

    def shares_out(columns):
        some = out((fast - 1, 2, share, columns), BF16)
        return [out((GROUP, share, columns), BF16), some, some]

    def go_round(some, *ties):
        some = after(some, *ties)
        return [other_fast(some[turn - 1], turn) for turn in range(1, fast)]

    def add_round(keep, moved, pieces):
        return {by: add_low(keep[by], *[m[k] for m in moved]) for k, by in enumerate(pieces)}

    def all_pieces(rows, units_in, tie):
        names = (one, three) + ((two,) if two in units_in else (two_a, two_b))
        own, first, third, *second = joined([rows[0]] + [units_in[unit] for unit in names], [tie])
        second = second[0] if len(second) == 1 else jnp.concatenate(second, axis=0)
        return own, first, second, third

    def stacked(rows, units_in, tie):
        return jnp.stack(all_pieces(rows, units_in, tie))

    o_turned = o_weight.swapaxes(1, 2)
    ssm_turned = ssm_weight.swapaxes(1, 2)
    down_turned = down_weight.swapaxes(1, 2)

    def pack_mix(layer, place):
        inner = in_weight[layer]
        both = kv_weight[layer]
        packed = call(
            functools.partial(pack_mix_kernel, cols, chan, units, extra, tensor_size),
            [out((share, mix_cols), BF16)] * GROUP,
            [
                q_weight,
                both[:, 0],
                both[:, 1],
                o_turned,
                inner[:, 0],
                inner[:, 1],
                ssm_turned,
                down_turned,
            ],
            5,
            place=place,
            layers=(layer, None, None, layer, None, None, layer, layer),
        )
        return packed

    def pack_ffn(layer, place):
        gate = gate_weight[layer]
        packed = call(
            functools.partial(pack_ffn_kernel, units, extra),
            [out((share, ffn_cols), BF16)] * GROUP,
            [gate[:, 0], gate[:, 1], down_turned],
            3,
            place=place,
            layers=(None, None, layer),
        )
        return packed

    vecs, dlogs, scan_mats, step_mats = call(
        functools.partial(small_weights_kernel, chan, wide, rank),
        [
            out((layers, 8, wide), F32),
            out((layers, state, wide), F32),
            out((layers, proj_rows, wide), BF16),
            out((layers, rank, wide), BF16),
        ],
        [
            conv_weight,
            conv_bias,
            step_bias,
            decay_log.swapaxes(1, 2),
            skip_gain,
            scan_weight.transpose(2, 0, 1),
            step_weight.swapaxes(0, 1),
        ],
        2,
        place=place,
    )

    bf_rows = lambda columns: out((tokens, columns), BF16)
    f_rows = lambda columns: out((tokens, columns), F32)
    tiled = pltpu.VMEM((wide // LANES, tokens, LANES), F32)
    state_tiled = pltpu.VMEM((length, state, seqs, LANES), F32)
    scan_scratch = [
        tiled,
        tiled,
        state_tiled,
        state_tiled,
        pltpu.VMEM((state, seqs, wide), F32),
        tiled,
    ]

    def own_rows(values):
        flat = values.reshape(batches * length, width)
        return lax.dynamic_slice_in_dim(flat, tensor_idx * rows_here, rows_here, 0)

    part_outs = [out((tokens // 4, width), BF16)] * 4
    token = tensor_idx * rows_here + jnp.arange(rows_here)
    mask = (token % length < lengths[token // length, 0]).astype(F32)[:, None]
    grad_run = own_rows(out_grad).astype(F32) * mask
    part_outs = [out((tokens // 4, width), BF16)] * 4
    running = own_rows(hidden_in).astype(F32)
    kept = []
    fetched = []
    own = pack_mix(0, place)
    first = {unit: send(own, unit) for unit in (one, three)}
    first[two] = send(own, two, first[one], first[three])
    mix_packed = [own]
    ffn_packed = [pack_ffn(0, after(place, first[one]))]
    place_later = after(place, first[one], first[three])
    for layer in range(1, layers):
        mix_packed.append(pack_mix(layer, place_later))
        ffn_packed.append(pack_ffn(layer, place_later))
    for layer in range(layers):
        final = layer + 1 == layers
        gains = norm_gains[layer]
        normed, pull_input = jax.vjp(rms_scale, running, gains[0])
        normed = normed.astype(BF16)
        ffn_own, ffn_in_units = ffn_packed[layer], {}
        if layer == 0:
            mix_got = Fetched(own[0])
            for unit, piece in first.items():
                mix_got.add(unit, piece)
            n = gather_tokens(normed)
            mix_w = after(mix_got.whole(), *[p[0] for p in mix_packed[1:] + ffn_packed])
        else:
            n = gather_far(normed)
            for unit in (one, three, two_a):
                ffn_in_units[unit] = send(ffn_own, unit, n)
            n = gather_near(n, [ffn_in_units[one]])
            mix_w = mix_got.whole()
        ready = joined(n, [mix_w])
        if layer == 0:
            for unit in (one, three, two_a):
                ffn_in_units[unit] = send(ffn_own, unit, first[two])
        xi, z, conv, qkv, heads, proj_part, *attn_parts = call(
            functools.partial(mix_forward_kernel, cols, chan, wide, length),
            [
                f_rows(wide),
                f_rows(wide),
                bf_rows(wide),
                bf_rows(cols.o),
                bf_rows(2 * HEAD),
                out((proj_rows, tokens), BF16),
            ]
            + part_outs
            + ([out((width, extra), BF16)] if extra else []),
            ready + [mix_w, vecs, scan_mats],
            7,
            place=place,
            layers=(None,) * 5 + (layer, layer),
        )
        attn_parts, rest_w = attn_parts[:4], attn_parts[4:]
        proj = sum_far(sum_near(after(proj_part, *ffn_in_units.values())))
        ffn_in_units[two_b] = send(ffn_own, two_b, proj)
        attn_total = scatter_near(joined(attn_parts, [proj]))
        gated, *ssm_parts = call(
            functools.partial(
                scan_forward_kernel, cols, chan, wide, rank, state, seqs, length
            ),
            [bf_rows(wide)] + part_outs,
            [proj, conv, z, step_mats, vecs, dlogs, mix_w],
            11,
            scan_scratch,
            place=place,
            layers=(None,) * 3 + (layer,) * 3,
        )
        ssm_parts = joined(ssm_parts, [attn_total, ffn_in_units[two_b]])
        attn_out = scatter_far(after(attn_total, ssm_parts[0]))
        ssm_out = scatter_far(scatter_near(ssm_parts))
        (residual, ffn_in), pull_mix = jax.vjp(
            mix_branches, running, attn_out, ssm_out, gains[1], gains[2], gains[3]
        )
        ffn_in = ffn_in.astype(BF16)
        f = gather_far(ffn_in)
        ffn_w = rows_round(ffn_own[0], ffn_in_units, ffn_in)
        fetched.append((mix_w, ffn_w, rest_w))
        if final:
            f = gather_near(f, [ffn_w])
            d_out = gather_tokens(after(grad_run.astype(BF16), f[2]))
            ffn_w = after(ffn_w, d_out[0])
        else:
            own = mix_packed[layer + 1]
            mix_got = Fetched(own[0])
            unit_two = send(own, two, f)
            f = gather_near(f, [unit_two, ffn_w])
            mix_got.add(two, unit_two)
        ready = joined(f, [ffn_w])
        if not final:
            unit_one = send(own, one, ready[0])
        hidden, *ffn_parts = call(
            functools.partial(ffn_forward_kernel, units),
            [f_rows(2 * units)] + part_outs,
            ready + [ffn_w] + rest_w,
            7,
        )
        if not final:
            ffn_parts = joined(ffn_parts, [unit_one])
            mix_got.add(one, unit_one)
            unit_three = send(own, three, ffn_parts[0])
            total = after(scatter_near(ffn_parts), unit_three)
            mix_got.add(three, unit_three)
            running = residual + scatter_far(total)
        kept.append((n, pull_input, xi, z, conv, qkv, heads, proj, gated, pull_mix, f, hidden))

    def every_tensor(values):
        moved = lax.ppermute(values, "tensor", chip_perm)
        values = jnp.where(chip_idx == 0, jnp.stack([values, moved]), jnp.stack([moved, values]))
        moved = lax.ppermute(values, "tensor", core_perm)
        values = jnp.where(
            core_idx == 0, jnp.stack([values, moved], 1), jnp.stack([moved, values], 1)
        )
        return values.reshape((tensor_size,) + values.shape[2:])

    def tensor_blocks(mine):
        chip = lax.ppermute(mine, "tensor", chip_perm)
        core = lax.ppermute(mine, "tensor", core_perm)
        return [mine, chip, core, lax.ppermute(chip, "tensor", core_perm)]

    def every_fast(values):
        turned = jnp.stack([other_fast(values, turn) for turn in range(fast)])
        return [
            lax.dynamic_index_in_dim(turned, (fast_idx - source) % fast, 0, False)
            for source in range(fast)
        ]

    def every_slow(values):
        turned = jnp.stack([slow(values, by) for by in range(GROUP)])
        return [
            lax.dynamic_index_in_dim(turned, (slow_idx - source) % GROUP, 0, False)
            for source in range(GROUP)
        ]

    def rounded(values):
        return lax.optimization_barrier(values.astype(BF16))

    def all_rows(own, *ties):
        return every_tensor(after(rounded(own), *ties)).reshape(batches, 1, length, width)

    big = {"heads": None, "mix": None, "ffn": None}
    small_rows = []
    gain_grads = [None] * layers
    early_rows = late_rows = None

    def heads_blocks(pair, tie):
        return tensor_blocks(jnp.stack([p[:, : cols.s] for p in joined(pair, [tie])]))

    def finish_mix(layer, rows, units_in, blocks, tie, last):
        big["heads"] = call_into(
            functools.partial(unpack_heads_kernel, cols, tensor_size),
            layer,
            [
                out((layers, share, KVH * GQ * HEAD), F32),
                out((layers, share, 2, KVH * HEAD), F32),
                out((layers, share, KVH * GQ * HEAD), F32),
            ],
            big["heads"],
            blocks,
            after(place, last),
        )
        pieces = stacked(rows, units_in, tie)
        big["mix"] = call_into(
            functools.partial(unpack_channels_kernel, cols, chan),
            layer,
            [
                out((layers, share, GROUP * chan), F32),
                out((layers, share, 2, GROUP * chan), F32),
            ],
            big["mix"],
            [pieces],
            place,
        )
        return pieces

    def finish_ffn(layer, rows, units_in, mix_pieces, tie):
        big["ffn"] = call_into(
            functools.partial(unpack_ffn_kernel, units, extra),
            layer,
            [
                out((layers, share, 2, GROUP * units), F32),
                out((layers, share, GROUP * units), F32),
            ],
            big["ffn"],
            [stacked(rows, units_in, tie), mix_pieces],
            place,
        )

    def small_near(rows):
        parts = rows.reshape(fast, rows.shape[0] // fast, chan)
        terms = []
        for turn in range(fast):
            part = lax.dynamic_index_in_dim(parts, (fast_idx + turn) % fast, 0, False)
            terms.append(other_fast(part, turn).astype(F32))
        return rounded(sum(terms))

    above = None
    for layer in reversed(range(layers)):
        mix_w, ffn_w, rest_w = fetched[layer]
        n, pull_input, xi, z, conv, qkv, heads, proj, gated, pull_mix, f, hidden = kept[layer]
        if above is not None:
            mix_rows, ffn_above, ffn_above_units = above
            d_out = gather_far(grad_run.astype(BF16))
            d_out = gather_near(after(d_out, mix_rows[1], mix_rows[3]))
            running = residual + scatter_far(after(out_total, d_out[0]))
            output = (running * mask).astype(BF16)
            ffn_w = after(ffn_w, output)
        ready = joined(d_out, [ffn_w])
        if above is not None:
            mix_units = {one: send(mix_rows, one, ready[0])}
        d_hidden, activ, *parts = call(
            functools.partial(ffn_backward_kernel, units),
            [bf_rows(2 * units), bf_rows(units)] + part_outs,
            ready + [hidden, ffn_w] + rest_w,
            7,
        )
        done = []
        if above is not None:
            parts = joined(parts, [mix_units[one]])
            mix_units[three] = send(mix_rows, three, parts[0])
            done = [mix_units[three]]
        far = scatter_core(parts)
        d_ffn_w = call(
            functools.partial(ffn_weights_kernel, units),
            shares_out(ffn_cols) + ([out((width, extra), BF16)] if extra else []),
            f + joined(d_out, [far]) + [d_hidden, activ],
            6,
            place=place,
        )
        total = after(scatter_near(parts, far), d_ffn_w[0], *done)
        d_ffn_in = scatter_far(total)
        if above is None:
            out_total = scatter_near(joined(ffn_parts, [total]))
        grad_resid, d_attn, d_ssm, d_gain_attn, d_gain_ssm, d_gain_ffn = pull_mix(
            (grad_run, d_ffn_in)
        )
        moved = go_round(d_ffn_w[1])
        d_ssm = gather_far(d_ssm.astype(BF16))
        d_ssm = gather_near(d_ssm if above is not None else after(d_ssm, out_total))
        d_attn = gather_far(after(d_attn.astype(BF16), d_ssm[0]))
        done = [d_attn]
        ffn_rows = add_round(after(d_ffn_w[0], d_ssm[0]), moved, (1, 3))
        ffn_even = go_round(d_ffn_w[2], ffn_rows[1])
        ready = joined(d_ssm, done + list(ffn_rows.values()))
        d_attn = gather_near(after(d_attn, ready[0]))
        ffn_units = {one: send(ffn_rows, one, ready[0])}
        done = []
        if above is None:
            ffn_units[three] = send(ffn_rows, three, ready[0])
        else:
            mix_units[two] = send(mix_rows, two, ready[0])
            done = [mix_units[two]]
        d_proj, d_conv, d_z, small_scan, d_step_w = call(
            functools.partial(
                scan_backward_kernel, cols, chan, wide, rank, state, seqs, length
            ),
            [
                out((proj_rows, tokens), BF16),
                f_rows(wide),
                bf_rows(wide),
                out((16 + state, wide), BF16),
                out((rank, wide), BF16),
            ],
            ready + [proj, conv, z, step_mats, vecs, dlogs, mix_w],
            26,
            scan_scratch
            + [
                pltpu.VMEM((length, STATES_AT_ONCE * (wide // LANES), seqs, LANES), F32),
                tiled,
                tiled,
                tiled,
                state_tiled,
                state_tiled,
            ],
            place=place,
            layers=(None,) * 7 + (layer,) * 3,
        )
        d_proj = after(d_proj, *ffn_units.values(), *done, *ffn_even, *d_attn[1:3])
        ffn_rows.update(add_round(after(d_ffn_w[0], d_proj), ffn_even, (2, 0)))
        (d_qkv,) = call(
            functools.partial(attend_backward_kernel, cols, length),
            [bf_rows(cols.o)],
            joined(d_attn, [d_proj]) + [mix_w, qkv],
            5,
            place=place,
        )
        d_near = sum_near(d_proj)
        d_proj = sum_far(d_near, d_qkv)
        if above is not None:
            odd = heads_blocks((mix_units[one], mix_units[three]), d_near)
            d_proj = after(d_proj, *odd[1:3])
            even = heads_blocks((above[0][0], mix_units[two]), d_proj)
        beside = two_a if above is None else three
        ffn_units[beside] = send(ffn_rows, beside, d_proj)
        d_x, *parts, d_scan_w, small_conv = call(
            functools.partial(mix_backward_kernel, cols, chan, length),
            [bf_rows(wide)] + part_outs + [out((proj_rows, wide), BF16), out((16, wide), BF16)],
            [d_proj, conv, xi, d_conv, d_z, d_qkv, mix_w, vecs, scan_mats],
            6,
            place=place,
            layers=(None,) * 7 + (layer, layer),
        )
        parts = joined(parts, [ffn_units[beside]] + ([] if above is None else even[1:3]))
        beside = two_b if above is None else two_a
        ffn_units[beside] = send(ffn_rows, beside, parts[0])
        done = [ffn_units[beside]]
        far = scatter_core(parts)
        d_mix_w = call(
            functools.partial(mix_weights_kernel, cols, chan, extra),
            shares_out(mix_cols),
            n + d_attn + d_ssm + [d_qkv, heads, gated, after(d_x, far), d_z] + list(d_ffn_w[3:]),
            7,
            place=place,
        )
        done.append(d_mix_w[0])
        total = after(scatter_near(parts, far), *done)
        d_normed = scatter_far(total)
        if above is not None:
            mix_above = finish_mix(layer + 1, above[0], mix_units, even + odd, total, total)
            d_normed = after(d_normed, big["heads"][0], big["mix"][0])
        keep, odd, even = d_mix_w
        mix_rows = add_round(keep, go_round(odd), (1, 3))
        if layer == 0:
            d_normed = after(d_normed, mix_rows[1], mix_rows[3])
        moved = go_round(even, mix_rows[1])
        mix_rows.update(add_round(after(keep, d_normed), moved, (2, 0)))
        grad_lower, d_gain_input = pull_input(d_normed)
        grad_run = grad_resid + grad_lower
        gain_grads[layer] = jnp.stack([d_gain_input, d_gain_attn, d_gain_ssm, d_gain_ffn])
        small = jnp.concatenate([small_scan, small_conv, d_step_w, d_scan_w], axis=0)[:, :chan]
        small_rows.append(small)
        above = (mix_rows, ffn_rows, ffn_units)

    mix_units = {unit: send(mix_rows, unit) for unit in (one, three)}
    gains = jnp.sum(every_tensor(rounded(jnp.stack(gain_grads))).astype(F32), axis=0)
    done = [mix_rows[2], mix_rows[0]]
    if layers > 1:
        finish_ffn(1, ffn_above, ffn_above_units, mix_above, d_normed)
        done.append(big["ffn"][1])
    gains = after(gains, *mix_units.values(), *done)
    small_count = layers * small_rows[0].shape[0]
    small = jnp.concatenate(small_rows[::-1] + [rounded(gains).reshape(-1, chan)], axis=0)
    padding = -small.shape[0] % (8 * fast)
    mix_units[two] = send(mix_rows, two, gains)
    small = small_near(jnp.pad(small, ((0, padding), (0, 0))))
    small = after(small, mix_units[two])
    for unit in (one, three, two_a, two_b):
        if unit not in ffn_units:
            ffn_units[unit] = send(ffn_rows, unit, small)
    output = all_rows(output, small)
    input_grad = all_rows(grad_run, small).astype(F32)
    tie = small
    odd = heads_blocks((mix_units[one], mix_units[three]), tie)
    even = heads_blocks((mix_rows[0], mix_units[two]), tie)
    small = jnp.stack(every_slow(small))
    shared = jnp.concatenate(every_fast(small), axis=1)
    mix_pieces = finish_mix(0, mix_rows, mix_units, even + odd, tie, shared)
    finish_ffn(0, ffn_rows, ffn_units, mix_pieces, shared)
    grad_gains = jnp.sum(
        shared[:, small_count : shared.shape[1] - padding].astype(F32), axis=0
    ).reshape(norm_gains.shape)
    (
        grad_conv_weight,
        grad_conv_bias,
        grad_step_bias,
        grad_decay,
        grad_skip,
        grad_scan,
        grad_step_weight,
    ) = call(
        functools.partial(small_grads_kernel, chan, rank, state),
        [
            out(conv_weight.shape, F32),
            out(conv_bias.shape, F32),
            out(step_bias.shape, F32),
            out((layers, state, GROUP * chan), F32),
            out(skip_gain.shape, F32),
            out((rank_true + 2 * state, layers, GROUP * chan), F32),
            out((rank_true, layers, GROUP * chan), F32),
        ],
        [shared],
        4,
        place=place,
    )
    grad_decay = grad_decay.swapaxes(1, 2)
    grad_scan = grad_scan.transpose(1, 2, 0)
    grad_step_weight = grad_step_weight.swapaxes(0, 1)
    d_q, d_kv, d_o = big["heads"]
    d_ssm_w, d_in = big["mix"]
    d_gate, d_down = big["ffn"]
    return (
        output,
        input_grad,
        grad_gains,
        d_q,
        d_kv,
        d_o.swapaxes(1, 2),
        d_in,
        grad_conv_weight,
        grad_conv_bias,
        grad_step_bias,
        grad_decay,
        grad_skip,
        grad_scan,
        grad_step_weight,
        d_ssm_w.swapaxes(1, 2),
        d_gate,
        d_down.swapaxes(1, 2),
    )


def solution(mesh):
    return jax.shard_map(
        functools.partial(per_device, mesh.shape["dp"], mesh.shape["tensor"]),
        mesh=mesh,
        in_specs=(
            P(None, "dp", None, None),
            P(None, "dp", None, None),
            P(None, "dp"),
            P(),
            P(None, "dp", None),
            P(None, "dp", None, None),
            P(None, None, "dp"),
            P(None, "dp", None, "tensor"),
            P(None, None, "tensor"),
            P(None, "tensor"),
            P(None, "tensor"),
            P(None, "tensor", None),
            P(None, "tensor"),
            P(None, "tensor", None),
            P(None, None, "tensor"),
            P(None, "tensor", "dp"),
            P(None, "dp", None, "tensor"),
            P(None, "tensor", "dp"),
        ),
        out_specs=(
            P(None, "dp", None, None),
            P(None, "dp", None, None),
            P(),
            P(None, "dp", None),
            P(None, "dp", None, None),
            P(None, None, "dp"),
            P(None, "dp", None, "tensor"),
            P(None, None, "tensor"),
            P(None, "tensor"),
            P(None, "tensor"),
            P(None, "tensor", None),
            P(None, "tensor"),
            P(None, "tensor", None),
            P(None, None, "tensor"),
            P(None, "tensor", "dp"),
            P(None, "dp", None, "tensor"),
            P(None, "tensor", "dp"),
        ),
        check_vma=False,
    )
```

```python
import functools

import jax
import jax.numpy as jnp
from jax import lax
from jax.experimental import pallas as pl
from jax.experimental.pallas import tpu as pltpu
from jax.sharding import PartitionSpec as P

KVH = 5
HEAD = 64
GQ = 5
CONV = 4
WINDOW = 1024
EPSILON = 1e-06
GROUP = 4
LANES = 128
F32 = jnp.float32
BF16 = jnp.bfloat16
NN = (((1,), (0,)), ((), ()))
NT = (((1,), (1,)), ((), ()))
TN = (((0,), (0,)), ((), ()))


def mm(left, right, dims=NN):
    return lax.dot_general(left, right, dims, preferred_element_type=F32)


def sigmoid(v):
    return 1.0 / (1.0 + jnp.exp(-v))


def softplus(v):
    return jnp.maximum(v, 0.0) + jnp.log(1.0 + jnp.exp(-jnp.abs(v)))


def params(megabytes=56):
    return pltpu.CompilerParams(vmem_limit_bytes=megabytes * 2**20)


def cost(micros):
    return pl.CostEstimate(flops=int(micros * 10**9), bytes_accessed=1, transcendentals=0)


def call(kernel, outs, args, micros, scratch=(), place=None, layers=()):
    vmem = pl.BlockSpec(memory_space=pltpu.VMEM)
    specs = []
    for k, a in enumerate(args):
        layer = layers[k] if k < len(layers) else None
        if layer is None:
            specs.append(vmem)
        else:
            at = (layer,) + (0,) * (a.ndim - 1)
            specs.append(pl.BlockSpec((None,) + a.shape[1:], lambda step, at=at: at))
    if place is not None:
        specs.insert(0, pl.BlockSpec(memory_space=pltpu.SMEM))
        args = [place] + list(args)
    return pl.pallas_call(
        kernel,
        out_shape=outs,
        grid=(1,) if layers else (),
        in_specs=specs,
        out_specs=[vmem] * len(outs),
        scratch_shapes=list(scratch),
        compiler_params=params(),
        cost_estimate=cost(micros),
    )(*args)


def call_into(kernel, layer, outs, before, args, place):
    vmem = pl.BlockSpec(memory_space=pltpu.VMEM)
    specs = [pl.BlockSpec(memory_space=pltpu.SMEM)] + [vmem] * len(args)
    out_specs = []
    for o in outs:
        at = (layer,) + (0,) * (len(o.shape) - 1)
        out_specs.append(pl.BlockSpec((None,) + o.shape[1:], lambda step, at=at: at))
    operands = [place] + list(args)
    aliases = {}
    if before is not None:
        aliases = {len(operands) + k: k for k in range(len(outs))}
        specs += [pl.BlockSpec(memory_space=pl.ANY)] * len(outs)
        operands += list(before)
    skip = len(aliases)

    def body(*refs):
        count = 1 + len(args)
        kernel(*refs[:count], *refs[count + skip :])

    return pl.pallas_call(
        body,
        out_shape=outs,
        grid=(1,),
        in_specs=specs,
        out_specs=out_specs,
        input_output_aliases=aliases,
        compiler_params=params(),
        cost_estimate=cost(4),
    )(*operands)


def out(shape, dtype):
    return jax.ShapeDtypeStruct(shape, dtype)


def widen(values, width):
    rows, have = values.shape
    if have == width:
        return values
    return jnp.concatenate([values, jnp.zeros((rows, width - have), values.dtype)], axis=1)


def shift_rows(values, amount, length):
    if amount == 0:
        return values
    rows = values.shape[0]
    place = lax.broadcasted_iota(jnp.int32, values.shape, 0) % length
    moved = pltpu.roll(values, amount % rows, 0)
    inside = place >= amount if amount > 0 else place < length + amount
    return jnp.where(inside, moved, 0.0)


def conv_pre(inner_x, taps, bias, length):
    running = bias
    for k in range(CONV):
        running = running + shift_rows(inner_x, CONV - 1 - k, length) * taps[k : k + 1]
    return running


def scores_of(queries, keys, length):
    scores = lax.dot_general(
        queries, keys, (((2,), (2,)), ((0,), (0,))), preferred_element_type=F32
    ) * HEAD ** (-0.5)
    shape = scores.shape
    query_pos = lax.broadcasted_iota(jnp.int32, shape, 1)
    key_pos = lax.broadcasted_iota(jnp.int32, shape, 2)
    allowed = (key_pos <= query_pos) & (key_pos > query_pos - WINDOW)
    scores = jnp.where(allowed, scores, -1e30)
    weights = jnp.exp(scores - jnp.max(scores, axis=-1, keepdims=True))
    return weights / jnp.sum(weights, axis=-1, keepdims=True)


class Mix:
    def __init__(self, chan):
        self.q = 0
        self.kv = 2 * HEAD
        self.o = 4 * HEAD
        self.s = 6 * HEAD
        self.x = self.s + chan
        self.z = self.x + chan
        self.end = self.z + chan


def swap(flag, first, second):
    return jnp.where(flag, second, first), jnp.where(flag, first, second)


def to_sequences(place, values):
    rows, columns = values.shape
    blocks = values.reshape(4, GROUP, rows // (4 * GROUP), columns)
    chip, core = place[2] == 1, place[3] == 1
    low, high = [], []
    for own in (0, 1):
        first, second = swap(chip, blocks[2 * own], blocks[2 * own + 1])
        low.append(first)
        high.append(second)
    parts = []
    for pair in (low, high):
        parts.append(jnp.stack(swap(core, pair[0], pair[1]), axis=1))
    return jnp.stack(parts, axis=1).reshape(rows, columns)


def to_blocks(place, values):
    rows, columns = values.shape
    parts = values.reshape(GROUP, 2, 2, rows // (4 * GROUP), columns)
    chip, core = place[2] == 1, place[3] == 1
    own, other = swap(core, parts[:, :, 0], parts[:, :, 1])
    blocks = []
    for half in (own, other):
        blocks.extend(swap(chip, half[:, 0], half[:, 1]))
    return jnp.concatenate([b.reshape(rows // 4, columns) for b in blocks], axis=0)


def rows_of(blocks):
    return jnp.concatenate([b[...] for b in blocks], axis=0)


def to_parts(parts, values):
    count = values.shape[0] // 4
    for k in range(4):
        parts[k][...] = values[k * count : (k + 1) * count].astype(BF16)


def mix_forward_kernel(cols, chan, wide, length, place, n0, n1, n2, n3, w, vec, scan_w, xi, z, conv, qkv, heads, proj, p0, p1, p2, p3, *rest):
    if rest:
        rest[0][...] = w[:, cols.end :]
    normed = rows_of((n0, n1, n2, n3))
    both = to_sequences(place, mm(normed, w[:, : cols.o]).astype(BF16))
    qkv[...] = both
    inner = to_sequences(place, mm(normed, w[:, cols.x : cols.end]))
    inner_x = widen(inner[:, :chan], wide)
    xi[...] = inner_x
    z[...] = widen(inner[:, chan:], wide)
    running = conv_pre(inner_x, vec[:CONV], vec[CONV : CONV + 1], length)
    conv_low = (running * sigmoid(running)).astype(BF16)
    conv[...] = conv_low
    proj[...] = mm(scan_w[...], conv_low, NT).astype(BF16)
    seqs = normed.shape[0] // length
    keys = both[:, cols.kv : cols.kv + HEAD].reshape(seqs, length, HEAD)
    values = both[:, cols.kv + HEAD : cols.o].reshape(seqs, length, HEAD)
    outs = []
    for h in range(2):
        queries = both[:, h * HEAD : (h + 1) * HEAD].reshape(seqs, length, HEAD)
        probs = scores_of(queries, keys, length).astype(BF16)
        mixed = lax.dot_general(
            probs, values, (((2,), (1,)), ((0,), (0,))), preferred_element_type=F32
        )
        outs.append(mixed.reshape(seqs * length, HEAD))
    heads_out = to_blocks(place, jnp.concatenate(outs, axis=1).astype(BF16))
    heads[...] = heads_out
    to_parts((p0, p1, p2, p3), mm(heads_out, w[:, cols.o : cols.s], NT))


def spread(state, wide):
    row = lax.broadcasted_iota(jnp.int32, (state, wide), 0)
    col = lax.broadcasted_iota(jnp.int32, (state, wide), 1) // LANES
    return (row == col).astype(BF16)


def lane(n):
    return slice(n * LANES, (n + 1) * LANES)


def tiles_in(ref, values):
    for n in range(ref.shape[0]):
        ref[n] = values[:, lane(n)]


def tiles_out(ref):
    return jnp.concatenate([ref[n] for n in range(ref.shape[0])], axis=1)


LOG2E = 1.4426950408889634
STATES_AT_ONCE = 8


def time_major(rows, length):
    seqs = rows // length
    came = lax.broadcasted_iota(jnp.int32, (rows, rows), 0)
    goes = lax.broadcasted_iota(jnp.int32, (rows, rows), 1)
    return (came == (goes % seqs) * length + goes // seqs).astype(BF16)


def scan_setup(rank, state, seqs, length, proj, conv, step_w, step_b, dlog, dt_s, dtx_s, drive_s, read_s, rate_s):
    pre = mm(proj[:rank], step_w[...], TN) + step_b
    dt = softplus(pre)
    tiles_in(dt_s, dt)
    tiles_in(dtx_s, dt * conv)
    table = spread(state, state * LANES)
    order = time_major(seqs * length, length)
    maps = mm(proj[rank:], order).astype(BF16)
    drive = mm(maps[:state], table, TN)
    read = mm(maps[state:], table, TN)
    for n in range(state):
        drive_s[:, n] = drive[:, lane(n)].reshape(length, seqs, LANES)
        read_s[:, n] = read[:, lane(n)].reshape(length, seqs, LANES)
    rates = -LOG2E * jnp.exp(dlog[...])
    for n in range(state):
        rate_s[n] = jnp.broadcast_to(rates[n : n + 1], (seqs, rates.shape[1]))
    return pre


def scan_forward_loop(first, tiles, seqs, length, dt_s, dtx_s, drive_s, read_s, rate_s, y_s, keep_s):
    def step(t, held):
        rows = pl.ds(t, seqs, stride=length)
        dt = [dt_s[i, rows] for i in range(tiles)]
        dtx = [dtx_s[i, rows] for i in range(tiles)]
        total = [y_s[i, rows] if first else jnp.zeros_like(dt[i]) for i in range(tiles)]
        fresh = []
        for j in range(STATES_AT_ONCE):
            n = first + j
            drive = drive_s[t, n]
            read = read_s[t, n]
            for i in range(tiles):
                decay = jnp.exp2(dt[i] * rate_s[n, :, lane(i)])
                now = decay * held[j * tiles + i] + dtx[i] * drive
                total[i] = total[i] + now * read
                if keep_s is not None:
                    keep_s[t, j * tiles + i] = now
                fresh.append(now)
        for i in range(tiles):
            y_s[i, rows] = total[i]
        return tuple(fresh)

    zero = jnp.zeros((seqs, LANES), F32)
    lax.fori_loop(0, length, step, (zero,) * (STATES_AT_ONCE * tiles), unroll=4)


def scan_forward_kernel(cols, chan, wide, rank, state, seqs, length, place, proj, conv, z, step_w, vec, dlog, w, gated, p0, p1, p2, p3, dt_s, dtx_s, drive_s, read_s, rate_s, y_s):
    conv32 = conv[...].astype(F32)
    step_b, skip = vec[CONV + 1 : CONV + 2], vec[CONV + 2 : CONV + 3]
    scan_setup(rank, state, seqs, length, proj, conv32, step_w, step_b, dlog, dt_s, dtx_s, drive_s, read_s, rate_s)
    for first in range(0, state, STATES_AT_ONCE):
        scan_forward_loop(first, wide // LANES, seqs, length, dt_s, dtx_s, drive_s, read_s, rate_s, y_s, None)
    gate = z[...]
    low = ((tiles_out(y_s) + skip * conv32) * (gate * sigmoid(gate))).astype(BF16)
    low = to_blocks(place, low)
    gated[...] = low
    to_parts((p0, p1, p2, p3), mm(low[:, :chan], w[:, cols.s : cols.x], NT))


def split_sum(table, values):
    high = values.astype(BF16)
    rest = (values - high.astype(F32)).astype(BF16)
    return mm(table, high, NT) + mm(table, rest, NT)


def scan_backward_loop(first, tiles, seqs, length, dt_s, dtx_s, drive_s, read_s, rate_s, keep_s, ds_s, ddt_s, dsrc_s, pd_s, pr_s):
    count = STATES_AT_ONCE * tiles

    def step(back, carry):
        t = length - 1 - back
        rows = pl.ds(t, seqs, stride=length)
        dt = [dt_s[i, rows] for i in range(tiles)]
        dtx = [dtx_s[i, rows] for i in range(tiles)]
        ds = [ds_s[i, rows] for i in range(tiles)]
        zero = jnp.zeros_like(dt[0])
        d_src = [dsrc_s[i, rows] if first else zero for i in range(tiles)]
        d_dt = [ddt_s[i, rows] if first else zero for i in range(tiles)]
        lams = []
        sums = []
        for j in range(STATES_AT_ONCE):
            n = first + j
            drive = drive_s[t, n]
            read = read_s[t, n]
            of_read = zero
            of_drive = zero
            for i in range(tiles):
                k = j * tiles + i
                rate = rate_s[n, :, lane(i)]
                kept = keep_s[t, k]
                lam = carry[k] + read * ds[i]
                of_read = of_read + kept * ds[i]
                of_drive = of_drive + lam * dtx[i]
                d_src[i] = d_src[i] + lam * drive
                d_log = lam * (kept - dtx[i] * drive)
                d_dt[i] = d_dt[i] + d_log * rate
                sums.append(carry[count + k] + d_log * dt[i])
                lams.append(jnp.exp2(dt[i] * rate) * lam)
            pr_s[t, n] = of_read
            pd_s[t, n] = of_drive
        for i in range(tiles):
            dsrc_s[i, rows] = d_src[i]
            ddt_s[i, rows] = d_dt[i]
        return tuple(lams) + tuple(sums)

    zero = jnp.zeros((seqs, LANES), F32)
    return lax.fori_loop(0, length, step, (zero,) * (2 * count), unroll=4)[count:]


def scan_backward_kernel(cols, chan, wide, rank, state, seqs, length, place, g0, g1, g2, g3, proj, conv, z, step_w, vec, dlog, w, d_proj, d_conv, d_z, small, d_step_w, dt_s, dtx_s, drive_s, read_s, rate_s, y_s, keep_s, ds_s, ddt_s, dsrc_s, pd_s, pr_s):
    tiles = wide // LANES
    conv32 = conv[...].astype(F32)
    step_b, skip = vec[CONV + 1 : CONV + 2], vec[CONV + 2 : CONV + 3]
    pre = scan_setup(rank, state, seqs, length, proj, conv32, step_w, step_b, dlog, dt_s, dtx_s, drive_s, read_s, rate_s)
    d_gated = to_sequences(place, mm(rows_of((g0, g1, g2, g3)), w[:, cols.s : cols.x]))
    d_gated = widen(d_gated, wide)
    gate = z[...]
    sig = sigmoid(gate)
    d_scanned = d_gated * (gate * sig)
    tiles_in(ds_s, d_scanned)
    d_rates = []
    for first in range(0, state, STATES_AT_ONCE):
        scan_forward_loop(first, tiles, seqs, length, dt_s, dtx_s, drive_s, read_s, rate_s, y_s, keep_s)
        sums = scan_backward_loop(first, tiles, seqs, length, dt_s, dtx_s, drive_s, read_s, rate_s, keep_s, ds_s, ddt_s, dsrc_s, pd_s, pr_s)
        for j in range(STATES_AT_ONCE):
            d_rates.append(
                jnp.concatenate(
                    [jnp.sum(sums[j * tiles + i], axis=0, keepdims=True) for i in range(tiles)],
                    axis=1,
                )
            )
    d_src = tiles_out(dsrc_s)
    dt = tiles_out(dt_s)
    d_dt = tiles_out(ddt_s) * (1.0 / LOG2E) + d_src * conv32
    d_conv[...] = skip * d_scanned + d_src * dt
    scanned = tiles_out(y_s) + skip * conv32
    d_z[...] = (d_gated * scanned * (sig * (1.0 + gate * (1.0 - sig)))).astype(BF16)
    d_pre = d_dt * sigmoid(pre)
    rates = -jnp.exp(dlog[...])
    sums = [
        jnp.sum(d_pre, axis=0, keepdims=True),
        jnp.sum(d_scanned * conv32, axis=0, keepdims=True),
        jnp.zeros((14, wide), F32),
        jnp.concatenate(d_rates, axis=0) * rates,
    ]
    small[...] = jnp.concatenate(sums, axis=0).astype(BF16)
    low = d_pre.astype(BF16)
    d_step_w[...] = mm(proj[:rank], low).astype(BF16)
    table = spread(state, state * LANES)
    tokens = seqs * length
    by_time = [
        jnp.concatenate([ref[:, n].reshape(tokens, LANES) for n in range(state)], axis=1)
        for ref in (pd_s, pr_s)
    ]
    d_maps = jnp.concatenate([split_sum(table, values) for values in by_time], axis=0)
    order = time_major(tokens, length)
    d_proj[:rank] = mm(step_w[...], low, NT).astype(BF16)
    d_proj[rank:] = mm(d_maps.astype(BF16), order, NT).astype(BF16)


def attend_backward_kernel(cols, length, place, g0, g1, g2, g3, w, qkv, d_qkv):
    d_heads = mm(rows_of((g0, g1, g2, g3)), w[:, cols.o : cols.s]).astype(BF16)
    d_heads = to_sequences(place, d_heads)
    both = qkv[...]
    seqs = both.shape[0] // length
    keys = both[:, cols.kv : cols.kv + HEAD].reshape(seqs, length, HEAD)
    values = both[:, cols.kv + HEAD : cols.o].reshape(seqs, length, HEAD)
    parts = []
    d_keys = 0.0
    d_values = 0.0
    for h in range(2):
        queries = both[:, h * HEAD : (h + 1) * HEAD].reshape(seqs, length, HEAD)
        d_out = d_heads[:, h * HEAD : (h + 1) * HEAD].reshape(seqs, length, HEAD)
        probs = scores_of(queries, keys, length)
        d_probs = lax.dot_general(
            d_out, values, (((2,), (2,)), ((0,), (0,))), preferred_element_type=F32
        )
        d_scores = (
            probs
            * (d_probs - jnp.sum(d_probs * probs, axis=-1, keepdims=True))
            * HEAD ** (-0.5)
        ).astype(BF16)
        d_query = lax.dot_general(
            d_scores, keys, (((2,), (1,)), ((0,), (0,))), preferred_element_type=F32
        )
        parts.append(d_query.reshape(seqs * length, HEAD))
        d_keys = d_keys + lax.dot_general(
            d_scores, queries, (((1,), (1,)), ((0,), (0,))), preferred_element_type=F32
        )
        d_values = d_values + lax.dot_general(
            probs.astype(BF16), d_out, (((1,), (1,)), ((0,), (0,))), preferred_element_type=F32
        )
    parts.append(d_keys.reshape(seqs * length, HEAD))
    parts.append(d_values.reshape(seqs * length, HEAD))
    d_qkv[...] = jnp.concatenate(parts, axis=1).astype(BF16)


def mix_backward_kernel(cols, chan, length, place, proj, conv, xi, d_conv, d_z, d_qkv, w, vec, scan_w, d_x, p0, p1, p2, p3, d_scan_w, small):
    taps, bias = vec[:CONV], vec[CONV : CONV + 1]
    d_out = d_conv[...] + mm(proj[...], scan_w[...], TN)
    inner_x = xi[...]
    running = conv_pre(inner_x, taps, bias, length)
    sig = sigmoid(running)
    d_run = d_out * (sig * (1.0 + running * (1.0 - sig)))
    d_in = 0.0
    sums = []
    for k in range(CONV):
        back = CONV - 1 - k
        d_in = d_in + shift_rows(d_run, -back, length) * taps[k : k + 1]
        sums.append(jnp.sum(d_run * shift_rows(inner_x, back, length), axis=0, keepdims=True))
    sums.append(jnp.sum(d_run, axis=0, keepdims=True))
    sums.append(jnp.zeros((16 - CONV - 1, inner_x.shape[1]), F32))
    small[...] = jnp.concatenate(sums, axis=0).astype(BF16)
    low = d_in.astype(BF16)
    d_x[...] = low
    inner = to_blocks(place, jnp.concatenate([low[:, :chan], d_z[:, :chan]], axis=1))
    heads = to_blocks(place, d_qkv[...])
    to_parts((p0, p1, p2, p3), mm(inner, w[:, cols.x : cols.end], NT) + mm(heads, w[:, : cols.o], NT))
    d_scan_w[...] = mm(proj[...], conv[...]).astype(BF16)


def mix_weights_kernel(cols, chan, extra, place, n0, n1, n2, n3, a0, a1, a2, a3, s0, s1, s2, s3, d_qkv, heads, gated, d_x, d_z, *refs):
    outs = refs[-3:]
    normed = rows_of((n0, n1, n2, n3))
    inner = jnp.concatenate([d_x[:, :chan], d_z[:, :chan]], axis=1)
    to_shares(place, outs, 0, mm(normed, to_blocks(place, d_qkv[...]), TN))
    to_shares(place, outs, cols.o, mm(rows_of((a0, a1, a2, a3)), heads[...], TN))
    to_shares(place, outs, cols.s, mm(rows_of((s0, s1, s2, s3)), gated[:, :chan], TN))
    to_shares(place, outs, cols.x, mm(normed, to_blocks(place, inner), TN))
    if extra:
        to_shares(place, outs, cols.end, refs[0][...])


def picker(rows, columns, start, valid):
    row = lax.broadcasted_iota(jnp.int32, (rows, columns), 0)
    col = lax.broadcasted_iota(jnp.int32, (rows, columns), 1)
    return ((row == start + col) & (col < valid)).astype(BF16)


def pack_mix_kernel(cols, chan, units, extra, tensor_size, place, q, key, value, o, x, z, ssm, down, *packed):
    tensor_idx = place[1]
    for slow_idx in range(GROUP):

        @pl.when(place[0] == slow_idx)
        def _():
            for by in range(GROUP):
                s = (slow_idx + by) % GROUP
                unit = s * tensor_size + tensor_idx
                group = lax.div(unit, 3)
                sub = lax.rem(unit, 3)
                valid = jnp.where(group >= KVH, 0, jnp.where(sub == 2, HEAD, 2 * HEAD))
                heads = picker(q.shape[1], 2 * HEAD, group * GQ * HEAD + sub * 2 * HEAD, valid)
                both = picker(key.shape[1], HEAD, jnp.minimum(group, KVH - 1) * HEAD, HEAD)
                mine = slice(s * chan, (s + 1) * chan)
                packed[by][:, : cols.kv] = mm(q[...], heads).astype(BF16)
                packed[by][:, cols.kv : cols.o] = jnp.concatenate(
                    [mm(key[...], both), mm(value[...], both)], axis=1
                ).astype(BF16)
                packed[by][:, cols.o : cols.s] = mm(o[...], heads).astype(BF16)
                packed[by][:, cols.s : cols.x] = ssm[:, mine]
                packed[by][:, cols.x : cols.z] = x[:, mine]
                packed[by][:, cols.z : cols.end] = z[:, mine]
                if extra:
                    packed[by][:, cols.end :] = down[:, (s + 1) * units - extra : (s + 1) * units]


def pack_ffn_kernel(units, extra, place, gate, up, down, *packed):
    for slow_idx in range(GROUP):

        @pl.when(place[0] == slow_idx)
        def _():
            for by in range(GROUP):
                s = (slow_idx + by) % GROUP
                mine = slice(s * units, (s + 1) * units)
                packed[by][:, :units] = gate[:, mine]
                packed[by][:, units : 2 * units] = up[:, mine]
                packed[by][:, 2 * units :] = down[:, s * units : (s + 1) * units - extra]


def to_shares(place, outs, start, values):
    keep, odd, even = outs
    share = keep.shape[1]
    fast = odd.shape[0] + 1
    values = values.astype(BF16)
    columns = slice(start, start + values.shape[1])
    for s in range(GROUP):
        by = lax.rem(s - place[0] + GROUP, GROUP)
        for f in range(fast):
            at = (s * fast + f) * share
            rows = values[at : at + share]
            turn = lax.rem(f - place[4] + fast, fast)

            @pl.when(turn == 0)
            def _():
                keep[by, :, columns] = rows

            @pl.when((turn > 0) & (lax.rem(by, 2) == 1))
            def _():
                odd[turn - 1, lax.div(by, 2), :, columns] = rows

            @pl.when((turn > 0) & (lax.rem(by, 2) == 0))
            def _():
                even[turn - 1, 1 - lax.div(by, 2), :, columns] = rows


def unpack_heads_kernel(cols, tensor_size, place, *refs):
    blocks, (d_q, d_kv, d_o) = (refs[:4], refs[4:8]), refs[8:]
    slow_idx = place[0]
    for tensor_idx in range(tensor_size):

        @pl.when(place[1] == tensor_idx)
        def _():
            for group in range(KVH):
                total = 0.0
                for sub in range(3):
                    unit = 3 * group + sub
                    s, t = unit // tensor_size, unit % tensor_size
                    by = lax.rem(slow_idx - s + GROUP, GROUP)
                    at = lax.div(by, 2)
                    apart = t ^ tensor_idx
                    block = apart // 2 + 2 * (apart % 2)
                    piece = jnp.where(
                        lax.rem(by, 2) == 0, blocks[0][block][at], blocks[1][block][at]
                    ).astype(F32)
                    start = group * GQ * HEAD + sub * 2 * HEAD
                    width = HEAD if sub == 2 else 2 * HEAD
                    d_q[:, start : start + width] = piece[:, :width]
                    d_o[:, start : start + width] = piece[:, cols.o : cols.o + width]
                    total = total + piece[:, cols.kv : cols.o]
                d_kv[:, 0, group * HEAD : (group + 1) * HEAD] = total[:, :HEAD]
                d_kv[:, 1, group * HEAD : (group + 1) * HEAD] = total[:, HEAD:]


def by_rows(pieces, number):
    refs = [pieces[number]] if number < 2 else [pieces[2]] if number == 3 else pieces[3:]
    low = 0
    parts = []
    for ref in refs:
        parts.append((low, low + ref.shape[0], ref))
        low = low + ref.shape[0]
    return parts


def unpack_channels_kernel(cols, chan, place, *refs):
    pieces, (d_ssm, d_in) = refs[:-2], refs[-2:]
    for slow_idx in range(GROUP):

        @pl.when(place[0] == slow_idx)
        def _():
            for s in range(GROUP):
                mine = slice(s * chan, (s + 1) * chan)
                for low, high, ref in by_rows(pieces, (slow_idx - s) % GROUP):
                    d_ssm[low:high, mine] = ref[:, cols.s : cols.x].astype(F32)
                    d_in[low:high, 0, mine] = ref[:, cols.x : cols.z].astype(F32)
                    d_in[low:high, 1, mine] = ref[:, cols.z : cols.end].astype(F32)


def unpack_ffn_kernel(units, extra, count, place, *refs):
    pieces, mix_pieces, (gate_up, down) = refs[:count], refs[count:-2], refs[-2:]
    for slow_idx in range(GROUP):

        @pl.when(place[0] == slow_idx)
        def _():
            for s in range(GROUP):
                number = (slow_idx - s) % GROUP
                mine = slice(s * units, (s + 1) * units)
                last = (s + 1) * units - extra
                for low, high, ref in by_rows(pieces, number):
                    for k in range(2):
                        part = ref[:, k * units : (k + 1) * units]
                        gate_up[low:high, k, mine] = part.astype(F32)
                    down[low:high, s * units : last] = ref[:, 2 * units :].astype(F32)
                if extra:
                    for low, high, ref in by_rows(mix_pieces, number):
                        columns = ref.shape[1]
                        few = ref[:, columns - extra :].astype(F32)
                        down[low:high, last : last + extra] = few


def small_grads_kernel(chan, rank, state, place, shared, conv_w, conv_b, step_b, dlog, skip, scan_w, step_w):
    low = step_w.shape[0]
    layers = conv_w.shape[0]
    per = 2 * 16 + state + 2 * rank + 2 * state
    for layer in range(layers):
        for s in range(GROUP):
            mine = slice(s * chan, (s + 1) * chan)

            def rows(start, count):
                at = layer * per + start
                return shared[s, at : at + count].astype(F32)

            step_b[layer : layer + 1, mine] = rows(0, 1)
            skip[layer : layer + 1, mine] = rows(1, 1)
            dlog[layer, :, mine] = rows(16, state)
            base = 16 + state
            conv_w[layer, :, mine] = rows(base, CONV)
            conv_b[layer : layer + 1, mine] = rows(base + CONV, 1)
            base = base + 16
            step_w[:, layer, mine] = rows(base, low)
            base = base + rank
            scan_w[:low, layer, mine] = rows(base, low)
            scan_w[low:, layer, mine] = rows(base + rank, 2 * state)


def small_weights_kernel(chan, wide, rank, place, conv_w, conv_b, step_b, dlog, skip, scan_w, step_w, vec, dlog_out, scan_out, step_out):
    layers = vec.shape[0]
    low = scan_w.shape[0] - 2 * dlog.shape[1]
    vec[...] = jnp.zeros(vec.shape, F32)
    dlog_out[...] = jnp.zeros(dlog_out.shape, F32)
    scan_out[...] = jnp.zeros(scan_out.shape, BF16)
    step_out[...] = jnp.zeros(step_out.shape, BF16)
    for s in range(GROUP):

        @pl.when(place[0] == s)
        def _():
            mine = slice(s * chan, (s + 1) * chan)
            for layer in range(layers):
                vec[layer, :CONV, :chan] = conv_w[layer, :, mine]
                vec[layer, CONV : CONV + 1, :chan] = conv_b[layer : layer + 1, mine]
                vec[layer, CONV + 1 : CONV + 2, :chan] = step_b[layer : layer + 1, mine]
                vec[layer, CONV + 2 : CONV + 3, :chan] = skip[layer : layer + 1, mine]
                dlog_out[layer, :, :chan] = dlog[layer, :, mine]
                scan_out[layer, :low, :chan] = scan_w[:low, layer, mine]
                scan_out[layer, rank:, :chan] = scan_w[low:, layer, mine]
                step_out[layer, :low, :chan] = step_w[:, layer, mine]


def down_weights(units, w, rest):
    main = w[:, 2 * units :]
    return jnp.concatenate([main, rest[0][...]], axis=1) if rest else main


def ffn_forward_kernel(units, f0, f1, f2, f3, w, *refs):
    rest, (hidden, p0, p1, p2, p3) = refs[:-5], refs[-5:]
    both = mm(rows_of((f0, f1, f2, f3)), w[:, : 2 * units])
    hidden[...] = both
    gate = both[:, :units]
    activ = (gate * sigmoid(gate) * both[:, units:]).astype(BF16)
    to_parts((p0, p1, p2, p3), mm(activ, down_weights(units, w, rest), NT))


def ffn_backward_kernel(units, d0, d1, d2, d3, hidden, w, *refs):
    rest, (d_hidden, activ, p0, p1, p2, p3) = refs[:-6], refs[-6:]
    d_activ = mm(rows_of((d0, d1, d2, d3)), down_weights(units, w, rest))
    gate = hidden[:, :units]
    up = hidden[:, units:]
    sig = sigmoid(gate)
    swish = gate * sig
    activ[...] = (swish * up).astype(BF16)
    low = jnp.concatenate(
        [d_activ * up * (sig * (1.0 + gate * (1.0 - sig))), d_activ * swish], axis=1
    ).astype(BF16)
    d_hidden[...] = low
    to_parts((p0, p1, p2, p3), mm(low, w[:, : 2 * units], NT))


def ffn_weights_kernel(units, place, f0, f1, f2, f3, d0, d1, d2, d3, d_hidden, activ, *refs):
    outs, rest = refs[:3], refs[3:]
    to_shares(place, outs, 0, mm(rows_of((f0, f1, f2, f3)), d_hidden[...], TN))
    d_down = mm(rows_of((d0, d1, d2, d3)), activ[...], TN)
    main = outs[0].shape[2] - 2 * units
    to_shares(place, outs, 2 * units, d_down[:, :main])
    if rest:
        rest[0][...] = d_down[:, main:].astype(BF16)


def rms_scale(values, gain_vec):
    return (
        values * lax.rsqrt(jnp.mean(values * values, axis=-1, keepdims=True) + EPSILON) * gain_vec
    )


def mix_branches(resid_in, attn_out, ssm_out, gain_attn, gain_ssm, gain_ffn):
    residual = resid_in + 0.5 * (rms_scale(attn_out, gain_attn) + rms_scale(ssm_out, gain_ssm))
    return (residual, rms_scale(residual, gain_ffn))


def per_device(
    dp_size,
    tensor_size,
    hidden_in,
    out_grad,
    lengths,
    norm_gains,
    q_weight,
    kv_weight,
    o_weight,
    in_weight,
    conv_weight,
    conv_bias,
    step_bias,
    decay_log,
    skip_gain,
    scan_weight,
    step_weight,
    ssm_weight,
    gate_weight,
    down_weight,
):
    layers = q_weight.shape[0]
    batches, _, length, width = hidden_in.shape
    fast = dp_size // GROUP
    share = width // dp_size
    chan = in_weight.shape[3] // GROUP
    wide = -(-chan // LANES) * LANES
    units = gate_weight.shape[3] // GROUP
    rank_true = step_weight.shape[1]
    state = decay_log.shape[2]
    rank = -(-rank_true // 16) * 16
    proj_rows = rank + 2 * state
    cols = Mix(chan)
    over = 3 * units % LANES
    extra = over if over <= -cols.end % LANES else 0
    ffn_cols = 3 * units - extra
    mix_cols = cols.end + extra
    dp_idx = lax.axis_index("dp")
    slow_idx = dp_idx // fast
    fast_idx = dp_idx % fast
    tensor_idx = lax.axis_index("tensor")
    rows_here = batches * length // tensor_size
    seqs = GROUP * batches
    tokens = seqs * length
    half = tensor_size // 2

    def slow_perm(by):
        return [
            (s * fast + f, ((s + by) % GROUP) * fast + f) for s in range(GROUP) for f in range(fast)
        ]

    def fast_perm(by):
        return [
            (s * fast + f, s * fast + (f + by) % fast) for s in range(GROUP) for f in range(fast)
        ]

    core_perm = [(t, t ^ 1) for t in range(tensor_size)]
    chip_perm = [(t, t ^ 2) for t in range(tensor_size)]
    core_idx = tensor_idx % 2
    chip_idx = tensor_idx // 2

    def slow(values, by):
        return lax.ppermute(values, "dp", slow_perm(by)) if by % GROUP else values

    def other_fast(values, by):
        return lax.ppermute(values, "dp", fast_perm(by)) if by % fast else values

    def add_low(*terms):
        total = terms[0].astype(F32)
        for term in terms[1:]:
            total = total + term.astype(F32)
        return total.astype(BF16)

    def after(values, *earlier):
        return lax.optimization_barrier((values,) + earlier)[0] if earlier else values

    def gather_far(own):
        return jnp.concatenate([slow(own, by) for by in range(GROUP)], axis=0)

    def joined(values, done):
        values, done = tuple(values), tuple(done)
        return list(lax.optimization_barrier(values + done)[: len(values)]) if done else list(values)

    def gather_near(mine, beside=()):
        chip = after(lax.ppermute(mine, "tensor", chip_perm), *beside)
        core = lax.ppermute(mine, "tensor", core_perm)
        return [mine, chip, core, lax.ppermute(chip, "tensor", core_perm)]

    def gather_tokens(own):
        return gather_near(gather_far(own))

    def scatter_core(parts):
        return add_low(parts[1], lax.ppermute(parts[3], "tensor", core_perm))

    def scatter_near(parts, far=None):
        far = scatter_core(parts) if far is None else far
        near = add_low(parts[0], lax.ppermute(parts[2], "tensor", core_perm))
        return add_low(near, lax.ppermute(far, "tensor", chip_perm))

    def scatter_far(total):
        total = total.reshape(GROUP, rows_here, width)
        result = total[0].astype(F32)
        for by in range(1, GROUP):
            result = result + slow(total[by], GROUP - by).astype(F32)
        return result

    def sum_near(values):
        halves = values.reshape(2, values.shape[0] // 2, tokens)
        mine = lax.dynamic_index_in_dim(halves, core_idx, 0, False)
        theirs = lax.dynamic_index_in_dim(halves, 1 - core_idx, 0, False)
        mine = add_low(mine, lax.ppermute(theirs, "tensor", core_perm))
        return add_low(mine, lax.ppermute(mine, "tensor", chip_perm))

    def sum_far(mine, work=None):
        chunk = tokens // GROUP
        terms = [mine] + [slow(mine, by) for by in range(1, GROUP)]
        terms = joined(terms, [] if work is None else [work])
        mine = add_low(*[jnp.roll(term, by * chunk, axis=1) for by, term in enumerate(terms)])
        theirs = lax.ppermute(mine, "tensor", core_perm)
        return jnp.where(
            core_idx == 0,
            jnp.concatenate([mine, theirs], axis=0),
            jnp.concatenate([theirs, mine], axis=0),
        )

    place = jnp.stack([slow_idx, tensor_idx, chip_idx, core_idx, fast_idx]).astype(jnp.int32)

    middle = share // 16 * 8
    one, three, two = (1, 0, share), (3, 0, share), (2, 0, share)
    two_a, two_b = (2, 0, middle), (2, middle, share)

    def send(pieces, unit, *ties):
        by, low, high = unit
        return slow(after(pieces[by][low:high], *ties), by)

    class Fetched:
        def __init__(self, own):
            self.full = jnp.zeros((GROUP, fast, share, own.shape[1]), BF16)
            self.add((0, 0, share), own)

        def add(self, unit, piece):
            by, low, _ = unit
            for turn in range(fast):
                self.full = lax.dynamic_update_slice(
                    self.full,
                    other_fast(piece, turn)[None, None],
                    ((slow_idx - by) % GROUP, (fast_idx - turn) % fast, low, 0),
                )

        def whole(self):
            return self.full.reshape(width, self.full.shape[3])

    def rows_round(own, units_in, tie):
        columns = own.shape[1]
        half = jnp.zeros((GROUP, share, columns), BF16)
        for (by, low, _), piece in [((0, 0, share), own)] + list(units_in.items()):
            half = lax.dynamic_update_slice(half, piece[None], ((slow_idx - by) % GROUP, low, 0))
        moved = [half] + [other_fast(half, turn) for turn in range(1, fast)]
        moved = joined(moved, [tie])
        if fast == 2:
            first, second = moved
            full = jnp.where(
                fast_idx == 0, jnp.stack([first, second], 1), jnp.stack([second, first], 1)
            )
        else:
            full = jnp.zeros((GROUP, fast, share, columns), BF16)
            for turn, rows in enumerate(moved):
                full = lax.dynamic_update_slice(
                    full, rows[:, None], (0, (fast_idx - turn) % fast, 0, 0)
                )
        return full.reshape(width, columns)

    def shares_out(columns):
        some = out((fast - 1, 2, share, columns), BF16)
        return [out((GROUP, share, columns), BF16), some, some]

    def go_round(some, *ties):
        some = after(some, *ties)
        return [other_fast(some[turn - 1], turn) for turn in range(1, fast)]

    def add_round(keep, moved, pieces):
        return {by: add_low(keep[by], *[m[k] for m in moved]) for k, by in enumerate(pieces)}

    def all_pieces(rows, units_in, tie):
        names = (one, three) + ((two,) if two in units_in else (two_a, two_b))
        return joined([rows[0]] + [units_in[unit] for unit in names], [tie])

    o_turned = o_weight.swapaxes(1, 2)
    ssm_turned = ssm_weight.swapaxes(1, 2)
    down_turned = down_weight.swapaxes(1, 2)

    def pack_mix(layer, place):
        inner = in_weight[layer]
        both = kv_weight[layer]
        packed = call(
            functools.partial(pack_mix_kernel, cols, chan, units, extra, tensor_size),
            [out((share, mix_cols), BF16)] * GROUP,
            [
                q_weight,
                both[:, 0],
                both[:, 1],
                o_turned,
                inner[:, 0],
                inner[:, 1],
                ssm_turned,
                down_turned,
            ],
            5,
            place=place,
            layers=(layer, None, None, layer, None, None, layer, layer),
        )
        return packed

    def pack_ffn(layer, place):
        gate = gate_weight[layer]
        packed = call(
            functools.partial(pack_ffn_kernel, units, extra),
            [out((share, ffn_cols), BF16)] * GROUP,
            [gate[:, 0], gate[:, 1], down_turned],
            3,
            place=place,
            layers=(None, None, layer),
        )
        return packed

    vecs, dlogs, scan_mats, step_mats = call(
        functools.partial(small_weights_kernel, chan, wide, rank),
        [
            out((layers, 8, wide), F32),
            out((layers, state, wide), F32),
            out((layers, proj_rows, wide), BF16),
            out((layers, rank, wide), BF16),
        ],
        [
            conv_weight,
            conv_bias,
            step_bias,
            decay_log.swapaxes(1, 2),
            skip_gain,
            scan_weight.transpose(2, 0, 1),
            step_weight.swapaxes(0, 1),
        ],
        2,
        place=place,
    )

    bf_rows = lambda columns: out((tokens, columns), BF16)
    f_rows = lambda columns: out((tokens, columns), F32)
    tiled = pltpu.VMEM((wide // LANES, tokens, LANES), F32)
    state_tiled = pltpu.VMEM((length, state, seqs, LANES), F32)
    scan_scratch = [
        tiled,
        tiled,
        state_tiled,
        state_tiled,
        pltpu.VMEM((state, seqs, wide), F32),
        tiled,
    ]

    def own_rows(values):
        flat = values.reshape(batches * length, width)
        return lax.dynamic_slice_in_dim(flat, tensor_idx * rows_here, rows_here, 0)

    part_outs = [out((tokens // 4, width), BF16)] * 4
    token = tensor_idx * rows_here + jnp.arange(rows_here)
    mask = (token % length < lengths[token // length, 0]).astype(F32)[:, None]
    grad_run = own_rows(out_grad).astype(F32) * mask
    part_outs = [out((tokens // 4, width), BF16)] * 4
    running = own_rows(hidden_in).astype(F32)
    kept = []
    fetched = []
    own = pack_mix(0, place)
    first = {unit: send(own, unit) for unit in (one, three)}
    first[two] = send(own, two, first[one], first[three])
    mix_packed = [own]
    ffn_packed = [pack_ffn(0, after(place, first[one]))]
    place_later = after(place, first[one], first[three])
    for layer in range(1, layers):
        mix_packed.append(pack_mix(layer, place_later))
        ffn_packed.append(pack_ffn(layer, place_later))
    for layer in range(layers):
        final = layer + 1 == layers
        gains = norm_gains[layer]
        normed, pull_input = jax.vjp(rms_scale, running, gains[0])
        normed = normed.astype(BF16)
        ffn_own, ffn_in_units = ffn_packed[layer], {}
        if layer == 0:
            mix_got = Fetched(own[0])
            for unit, piece in first.items():
                mix_got.add(unit, piece)
            n = gather_tokens(normed)
            mix_w = after(mix_got.whole(), *[p[0] for p in mix_packed[1:] + ffn_packed])
        else:
            n = gather_far(normed)
            for unit in (one, three, two_a):
                ffn_in_units[unit] = send(ffn_own, unit, n)
            n = gather_near(n, [ffn_in_units[one]])
            mix_w = mix_got.whole()
        ready = joined(n, [mix_w])
        if layer == 0:
            for unit in (one, three, two_a):
                ffn_in_units[unit] = send(ffn_own, unit, first[two])
        xi, z, conv, qkv, heads, proj_part, *attn_parts = call(
            functools.partial(mix_forward_kernel, cols, chan, wide, length),
            [
                f_rows(wide),
                f_rows(wide),
                bf_rows(wide),
                bf_rows(cols.o),
                bf_rows(2 * HEAD),
                out((proj_rows, tokens), BF16),
            ]
            + part_outs
            + ([out((width, extra), BF16)] if extra else []),
            ready + [mix_w, vecs, scan_mats],
            7,
            place=place,
            layers=(None,) * 5 + (layer, layer),
        )
        attn_parts, rest_w = attn_parts[:4], attn_parts[4:]
        proj = sum_far(sum_near(after(proj_part, *ffn_in_units.values())))
        ffn_in_units[two_b] = send(ffn_own, two_b, proj)
        attn_total = scatter_near(joined(attn_parts, [proj]))
        gated, *ssm_parts = call(
            functools.partial(
                scan_forward_kernel, cols, chan, wide, rank, state, seqs, length
            ),
            [bf_rows(wide)] + part_outs,
            [proj, conv, z, step_mats, vecs, dlogs, mix_w],
            11,
            scan_scratch,
            place=place,
            layers=(None,) * 3 + (layer,) * 3,
        )
        ssm_parts = joined(ssm_parts, [attn_total, ffn_in_units[two_b]])
        attn_out = scatter_far(after(attn_total, ssm_parts[0]))
        ssm_out = scatter_far(scatter_near(ssm_parts))
        (residual, ffn_in), pull_mix = jax.vjp(
            mix_branches, running, attn_out, ssm_out, gains[1], gains[2], gains[3]
        )
        ffn_in = ffn_in.astype(BF16)
        f = gather_far(ffn_in)
        ffn_w = rows_round(ffn_own[0], ffn_in_units, ffn_in)
        fetched.append((mix_w, ffn_w, rest_w))
        if final:
            f = gather_near(f, [ffn_w])
            d_out = gather_tokens(after(grad_run.astype(BF16), f[2]))
            ffn_w = after(ffn_w, d_out[0])
        else:
            own = mix_packed[layer + 1]
            mix_got = Fetched(own[0])
            unit_one = send(own, one, f)
            f = gather_near(f, [unit_one, ffn_w])
            mix_got.add(one, unit_one)
        ready = joined(f, [ffn_w])
        if not final:
            unit_two = send(own, two_a, ready[0])
        hidden, *ffn_parts = call(
            functools.partial(ffn_forward_kernel, units),
            [f_rows(2 * units)] + part_outs,
            ready + [ffn_w] + rest_w,
            7,
        )
        if not final:
            ffn_parts = joined(ffn_parts, [unit_two])
            mix_got.add(two_a, unit_two)
            last = {unit: send(own, unit, ffn_parts[0]) for unit in (three, two_b)}
            total = after(scatter_near(ffn_parts), *last.values())
            for unit, piece in last.items():
                mix_got.add(unit, piece)
            running = residual + scatter_far(total)
        kept.append((n, pull_input, xi, z, conv, qkv, heads, proj, gated, pull_mix, f, hidden))

    def every_tensor(values):
        moved = lax.ppermute(values, "tensor", chip_perm)
        values = jnp.where(chip_idx == 0, jnp.stack([values, moved]), jnp.stack([moved, values]))
        moved = lax.ppermute(values, "tensor", core_perm)
        values = jnp.where(
            core_idx == 0, jnp.stack([values, moved], 1), jnp.stack([moved, values], 1)
        )
        return values.reshape((tensor_size,) + values.shape[2:])

    def tensor_blocks(mine):
        chip = lax.ppermute(mine, "tensor", chip_perm)
        core = lax.ppermute(mine, "tensor", core_perm)
        return [mine, chip, core, lax.ppermute(chip, "tensor", core_perm)]

    def every_fast(values):
        turned = jnp.stack([other_fast(values, turn) for turn in range(fast)])
        return [
            lax.dynamic_index_in_dim(turned, (fast_idx - source) % fast, 0, False)
            for source in range(fast)
        ]

    def every_slow(values):
        turned = jnp.stack([slow(values, by) for by in range(GROUP)])
        return [
            lax.dynamic_index_in_dim(turned, (slow_idx - source) % GROUP, 0, False)
            for source in range(GROUP)
        ]

    def rounded(values):
        return lax.optimization_barrier(values.astype(BF16))

    def all_rows(own, *ties):
        return every_tensor(after(rounded(own), *ties)).reshape(batches, 1, length, width)

    big = {"heads": None, "mix": None, "ffn": None}
    small_rows = []
    gain_grads = [None] * layers
    early_rows = late_rows = None

    def heads_blocks(pair, tie):
        return tensor_blocks(jnp.stack([p[:, : cols.s] for p in joined(pair, [tie])]))

    def finish_mix(layer, rows, units_in, blocks, tie, last):
        big["heads"] = call_into(
            functools.partial(unpack_heads_kernel, cols, tensor_size),
            layer,
            [
                out((layers, share, KVH * GQ * HEAD), F32),
                out((layers, share, 2, KVH * HEAD), F32),
                out((layers, share, KVH * GQ * HEAD), F32),
            ],
            big["heads"],
            blocks,
            after(place, last),
        )
        pieces = all_pieces(rows, units_in, tie)
        big["mix"] = call_into(
            functools.partial(unpack_channels_kernel, cols, chan),
            layer,
            [
                out((layers, share, GROUP * chan), F32),
                out((layers, share, 2, GROUP * chan), F32),
            ],
            big["mix"],
            pieces,
            place,
        )
        return pieces

    def finish_ffn(layer, rows, units_in, mix_pieces, tie):
        pieces = all_pieces(rows, units_in, tie)
        big["ffn"] = call_into(
            functools.partial(unpack_ffn_kernel, units, extra, len(pieces)),
            layer,
            [
                out((layers, share, 2, GROUP * units), F32),
                out((layers, share, GROUP * units), F32),
            ],
            big["ffn"],
            pieces + mix_pieces,
            place,
        )

    def small_near(rows):
        parts = rows.reshape(fast, rows.shape[0] // fast, chan)
        terms = []
        for turn in range(fast):
            part = lax.dynamic_index_in_dim(parts, (fast_idx + turn) % fast, 0, False)
            terms.append(other_fast(part, turn).astype(F32))
        return rounded(sum(terms))

    above = None
    for layer in reversed(range(layers)):
        mix_w, ffn_w, rest_w = fetched[layer]
        n, pull_input, xi, z, conv, qkv, heads, proj, gated, pull_mix, f, hidden = kept[layer]
        if above is not None:
            mix_rows, ffn_above, ffn_above_units = above
            d_out = gather_far(grad_run.astype(BF16))
            d_out = gather_near(after(d_out, mix_rows[1], mix_rows[3]))
            running = residual + scatter_far(after(out_total, d_out[0]))
            output = (running * mask).astype(BF16)
            ffn_w = after(ffn_w, output)
        ready = joined(d_out, [ffn_w])
        if above is not None:
            mix_units = {one: send(mix_rows, one, ready[0])}
        d_hidden, activ, *parts = call(
            functools.partial(ffn_backward_kernel, units),
            [bf_rows(2 * units), bf_rows(units)] + part_outs,
            ready + [hidden, ffn_w] + rest_w,
            7,
        )
        done = []
        if above is not None:
            parts = joined(parts, [mix_units[one]])
            mix_units[three] = send(mix_rows, three, parts[0])
            done = [mix_units[three]]
        far = scatter_core(parts)
        d_ffn_w = call(
            functools.partial(ffn_weights_kernel, units),
            shares_out(ffn_cols) + ([out((width, extra), BF16)] if extra else []),
            f + joined(d_out, [far]) + [d_hidden, activ],
            6,
            place=place,
        )
        total = after(scatter_near(parts, far), d_ffn_w[0], *done)
        d_ffn_in = scatter_far(total)
        if above is None:
            out_total = scatter_near(joined(ffn_parts, [total]))
        grad_resid, d_attn, d_ssm, d_gain_attn, d_gain_ssm, d_gain_ffn = pull_mix(
            (grad_run, d_ffn_in)
        )
        moved = go_round(d_ffn_w[1])
        d_ssm = after(gather_far(d_ssm.astype(BF16)), *moved)
        if above is None:
            d_ssm = after(d_ssm, out_total)
        else:
            odd = heads_blocks((mix_units[one], mix_units[three]), total)
            d_ssm = after(d_ssm, *odd[1:3])
        d_ssm = gather_near(d_ssm)
        d_attn = gather_far(after(d_attn.astype(BF16), d_ssm[0]))
        done = [d_attn]
        ffn_rows = add_round(after(d_ffn_w[0], d_ssm[0]), moved, (1, 3))
        ffn_even = go_round(d_ffn_w[2], ffn_rows[1])
        ready = joined(d_ssm, done + list(ffn_rows.values()))
        d_attn = gather_near(after(d_attn, ready[0]))
        ffn_units = {one: send(ffn_rows, one, ready[0])}
        done = []
        if above is None:
            ffn_units[three] = send(ffn_rows, three, ready[0])
        else:
            mix_units[two] = send(mix_rows, two, ready[0])
            done = [mix_units[two]]
        d_proj, d_conv, d_z, small_scan, d_step_w = call(
            functools.partial(
                scan_backward_kernel, cols, chan, wide, rank, state, seqs, length
            ),
            [
                out((proj_rows, tokens), BF16),
                f_rows(wide),
                bf_rows(wide),
                out((16 + state, wide), BF16),
                out((rank, wide), BF16),
            ],
            ready + [proj, conv, z, step_mats, vecs, dlogs, mix_w],
            26,
            scan_scratch
            + [
                pltpu.VMEM((length, STATES_AT_ONCE * (wide // LANES), seqs, LANES), F32),
                tiled,
                tiled,
                tiled,
                state_tiled,
                state_tiled,
            ],
            place=place,
            layers=(None,) * 7 + (layer,) * 3,
        )
        d_proj = after(d_proj, *ffn_units.values(), *done, *ffn_even, *d_attn[1:3])
        ffn_rows.update(add_round(after(d_ffn_w[0], d_proj), ffn_even, (2, 0)))
        (d_qkv,) = call(
            functools.partial(attend_backward_kernel, cols, length),
            [bf_rows(cols.o)],
            joined(d_attn, [d_proj]) + [mix_w, qkv],
            5,
            place=place,
        )
        d_near = sum_near(d_proj)
        d_proj = sum_far(d_near, d_qkv)
        if above is not None:
            even = heads_blocks((above[0][0], mix_units[two]), d_proj)
        beside = two_a if above is None else three
        ffn_units[beside] = send(ffn_rows, beside, d_proj)
        d_x, *parts, d_scan_w, small_conv = call(
            functools.partial(mix_backward_kernel, cols, chan, length),
            [bf_rows(wide)] + part_outs + [out((proj_rows, wide), BF16), out((16, wide), BF16)],
            [d_proj, conv, xi, d_conv, d_z, d_qkv, mix_w, vecs, scan_mats],
            6,
            place=place,
            layers=(None,) * 7 + (layer, layer),
        )
        parts = joined(parts, [ffn_units[beside]] + ([] if above is None else even[1:3]))
        beside = two_b if above is None else two_a
        ffn_units[beside] = send(ffn_rows, beside, parts[0])
        done = [ffn_units[beside]]
        far = scatter_core(parts)
        d_mix_w = call(
            functools.partial(mix_weights_kernel, cols, chan, extra),
            shares_out(mix_cols),
            n + d_attn + d_ssm + [d_qkv, heads, gated, after(d_x, far), d_z] + list(d_ffn_w[3:]),
            7,
            place=place,
        )
        done.append(d_mix_w[0])
        total = after(scatter_near(parts, far), *done)
        d_normed = scatter_far(total)
        if above is not None:
            mix_above = finish_mix(layer + 1, above[0], mix_units, even + odd, total, total)
            d_normed = after(d_normed, big["heads"][0], big["mix"][0])
        keep, odd, even = d_mix_w
        mix_rows = add_round(keep, go_round(odd), (1, 3))
        if layer == 0:
            d_normed = after(d_normed, mix_rows[1], mix_rows[3])
        moved = go_round(even, mix_rows[1])
        mix_rows.update(add_round(after(keep, d_normed), moved, (2, 0)))
        grad_lower, d_gain_input = pull_input(d_normed)
        grad_run = grad_resid + grad_lower
        gain_grads[layer] = jnp.stack([d_gain_input, d_gain_attn, d_gain_ssm, d_gain_ffn])
        small = jnp.concatenate([small_scan, small_conv, d_step_w, d_scan_w], axis=0)[:, :chan]
        small_rows.append(small)
        above = (mix_rows, ffn_rows, ffn_units)

    mix_units = {unit: send(mix_rows, unit) for unit in (one, three)}
    gains = jnp.sum(every_tensor(rounded(jnp.stack(gain_grads))).astype(F32), axis=0)
    done = [mix_rows[2], mix_rows[0]]
    if layers > 1:
        finish_ffn(1, ffn_above, ffn_above_units, mix_above, d_normed)
        done.append(big["ffn"][1])
    gains = after(gains, *mix_units.values(), *done)
    small_count = layers * small_rows[0].shape[0]
    small = jnp.concatenate(small_rows[::-1] + [rounded(gains).reshape(-1, chan)], axis=0)
    padding = -small.shape[0] % (8 * fast)
    mix_units[two] = send(mix_rows, two, gains)
    small = small_near(jnp.pad(small, ((0, padding), (0, 0))))
    small = after(small, mix_units[two])
    for unit in (one, three, two_a, two_b):
        if unit not in ffn_units:
            ffn_units[unit] = send(ffn_rows, unit, small)
    output = all_rows(output, small)
    input_grad = all_rows(grad_run, small).astype(F32)
    tie = small
    odd = heads_blocks((mix_units[one], mix_units[three]), tie)
    even = heads_blocks((mix_rows[0], mix_units[two]), tie)
    small = jnp.stack(every_slow(small))
    shared = jnp.concatenate(every_fast(small), axis=1)
    mix_pieces = finish_mix(0, mix_rows, mix_units, even + odd, tie, shared)
    finish_ffn(0, ffn_rows, ffn_units, mix_pieces, shared)
    grad_gains = jnp.sum(
        shared[:, small_count : shared.shape[1] - padding].astype(F32), axis=0
    ).reshape(norm_gains.shape)
    (
        grad_conv_weight,
        grad_conv_bias,
        grad_step_bias,
        grad_decay,
        grad_skip,
        grad_scan,
        grad_step_weight,
    ) = call(
        functools.partial(small_grads_kernel, chan, rank, state),
        [
            out(conv_weight.shape, F32),
            out(conv_bias.shape, F32),
            out(step_bias.shape, F32),
            out((layers, state, GROUP * chan), F32),
            out(skip_gain.shape, F32),
            out((rank_true + 2 * state, layers, GROUP * chan), F32),
            out((rank_true, layers, GROUP * chan), F32),
        ],
        [shared],
        4,
        place=place,
    )
    grad_decay = grad_decay.swapaxes(1, 2)
    grad_scan = grad_scan.transpose(1, 2, 0)
    grad_step_weight = grad_step_weight.swapaxes(0, 1)
    d_q, d_kv, d_o = big["heads"]
    d_ssm_w, d_in = big["mix"]
    d_gate, d_down = big["ffn"]
    return (
        output,
        input_grad,
        grad_gains,
        d_q,
        d_kv,
        d_o.swapaxes(1, 2),
        d_in,
        grad_conv_weight,
        grad_conv_bias,
        grad_step_bias,
        grad_decay,
        grad_skip,
        grad_scan,
        grad_step_weight,
        d_ssm_w.swapaxes(1, 2),
        d_gate,
        d_down.swapaxes(1, 2),
    )


def solution(mesh):
    return jax.shard_map(
        functools.partial(per_device, mesh.shape["dp"], mesh.shape["tensor"]),
        mesh=mesh,
        in_specs=(
            P(None, "dp", None, None),
            P(None, "dp", None, None),
            P(None, "dp"),
            P(),
            P(None, "dp", None),
            P(None, "dp", None, None),
            P(None, None, "dp"),
            P(None, "dp", None, "tensor"),
            P(None, None, "tensor"),
            P(None, "tensor"),
            P(None, "tensor"),
            P(None, "tensor", None),
            P(None, "tensor"),
            P(None, "tensor", None),
            P(None, None, "tensor"),
            P(None, "tensor", "dp"),
            P(None, "dp", None, "tensor"),
            P(None, "tensor", "dp"),
        ),
        out_specs=(
            P(None, "dp", None, None),
            P(None, "dp", None, None),
            P(),
            P(None, "dp", None),
            P(None, "dp", None, None),
            P(None, None, "dp"),
            P(None, "dp", None, "tensor"),
            P(None, None, "tensor"),
            P(None, "tensor"),
            P(None, "tensor"),
            P(None, "tensor", None),
            P(None, "tensor"),
            P(None, "tensor", None),
            P(None, None, "tensor"),
            P(None, "tensor", "dp"),
            P(None, "dp", None, "tensor"),
            P(None, "tensor", "dp"),
        ),
        check_vma=False,
    )
```
